512 devices in a mesh: seq: 32 (over y, z_hi, core), chan: 16 (over x, z_lo).
Axes of the slice: x: 4, y: 4, z: 16 (z_hi: 4, z_lo: 4; z = z_hi * 4 + z_lo), core: 2. Of those that a mesh axis runs over, the one named last changes fastest.
Arguments:
- tokens: int32 [8192], P('seq'), may hold values from 0 to 4
- complement: int32 [5], replicated, may hold values from 0 to 4, each once
- embed: bfloat16 [5, 2048], replicated, may hold values from -6 to 6
- w_x: bfloat16 [2048, 4096], P(None, 'chan'), may hold values from -0.125 to 0.125
- w_z: bfloat16 [2048, 4096], P(None, 'chan'), may hold values from -0.125 to 0.125
- w_bc: bfloat16 [2048, 256], P('chan'), may hold values from -0.125 to 0.125
- w_dt: bfloat16 [2048, 64], P(None, 'chan'), may hold values from -0.125 to 0.125
- dt_bias: float32 [64], P('chan'), may hold values from -1 to 1
- decay_rate: float32 [64], P('chan'), may hold values from 2.4414062e-06 to 0.05
- d_skip: float32 [64], P('chan'), may hold values from 0.5 to 1.5
- conv_x: bfloat16 [4, 4096], P(None, 'chan'), may hold values from -3 to 3
- conv_bc: bfloat16 [4, 256], replicated, may hold values from -3 to 3
- norm_gain: float32 [4096], P('chan'), may hold values from 0.1 to 1.9
- w_out: bfloat16 [4096, 2048], P('chan'), may hold values from -0.09375 to 0.09375
Outputs:
- mixed_out: bfloat16 [8192, 2048], P(('seq', 'chan'))
The draws below stay inside these ranges and needn't reach their ends.
Inputs may be any that keep to these rules, and one draw needn't show every extreme that they name: `complement`: a permutation of the 5 token ids.
All inputs are finite; a program needn't handle non-finite values.
Results may differ from the reference program's by a relative error of at most 0.0073.
Values may be sent and summed in bfloat16 or wider, within the bound.
No kernel may reach another device: no remote copies, remote signals or barrier semaphores. Data moves between devices by JAX's collectives and lax.ppermute only.
A program may use at most 64 MiB of HBM per device.

```python
import math
import jax
import jax.numpy as jnp
from jax import lax

D = 2048
HEADS = 64
HEAD_DIM = 64
STATE = 128
CONV = 4
VOCAB = 5
L_DEV = 256
INNER = 4096
LENGTH = 8192


def place_ends(result, key, smallest, largest):
    longest = result.shape.index(max(result.shape))
    spots = []
    for shift in (0, 1):
        where = [jax.random.randint(jax.random.fold_in(key, axis), (), 0, length) for axis, length in enumerate(result.shape)]
        where[longest] = (where[longest] + shift) % result.shape[longest]
        spots.append(tuple(where))
    return result.at[spots[0]].set(smallest).at[spots[1]].set(largest)


def block_scale(own_key, shape, cuts, low, high):
    factor_of, own = 1.0, jax.random.fold_in(own_key, 6)
    for axis_at, blocks in cuts:
        draws = jnp.exp(jax.random.uniform(jax.random.fold_in(own, axis_at), (blocks,), jnp.float32, low / len(cuts), high / len(cuts)))
        factor_of = factor_of * jnp.repeat(draws, shape[axis_at] // blocks).reshape([-1 if axis == axis_at else 1 for axis in range(len(shape))])
    return factor_of


def scatter_about(own_key, extent, width, most, cuts=(), dtype=jnp.bfloat16):
    gain = block_scale(own_key, extent, cuts, -0.22, 0.18) if cuts else 1.0
    entries = jax.random.normal(own_key, extent, jnp.float32) * width * gain
    return jnp.minimum(jnp.maximum(entries, -most), most).astype(dtype)


def setup_inputs(seed: int = 0) -> dict:
    key_of = jax.random.split(jax.random.key(seed), 15)
    tokens = place_ends(jax.random.randint(key_of[0], (LENGTH,), 0, VOCAB), jax.random.fold_in(key_of[0], 1), 0, VOCAB - 1).astype(jnp.int32)
    complement = jax.random.permutation(key_of[1], VOCAB).astype(jnp.int32)
    embed = scatter_about(key_of[2], (VOCAB, D), 1.0, 6.0)
    w_x = scatter_about(key_of[3], (D, INNER), D ** -0.5, 0.125, ((1, 16),))
    w_z = scatter_about(key_of[4], (D, INNER), D ** -0.5, 0.125, ((1, 16),))
    w_bc = scatter_about(key_of[5], (D, 2 * STATE), D ** -0.5, 0.125, ((0, 16),))
    w_dt = scatter_about(key_of[6], (D, HEADS), D ** -0.5, 0.125, ((1, 16),))
    dt_bias = jnp.clip(jax.random.uniform(key_of[7], (HEADS,), jnp.float32, -1.0, 1.0) * block_scale(key_of[7], (HEADS,), ((0, 16),), -0.4, 0.0), -1.0, 1.0)
    decay_rate = jnp.clip(jnp.exp(math.log(0.05) - 9.927204 * jax.random.uniform(key_of[8], (HEADS,), jnp.float32) ** block_scale(key_of[8], (HEADS,), ((0, 16),), -0.2, 0.2)), 2.441406195430318e-06, 0.05)
    d_skip = jnp.clip(0.5 + 1.0 * jax.random.uniform(key_of[9], (HEADS,), jnp.float32) ** block_scale(key_of[9], (HEADS,), ((0, 16),), -0.2, 0.2), 0.5, 1.5)
    conv_x = scatter_about(key_of[10], (CONV, INNER), CONV ** -0.5, 3.0, ((1, 16),))
    conv_bc = scatter_about(key_of[11], (CONV, 2 * STATE), CONV ** -0.5, 3.0)
    norm_gain = jnp.clip(1.0 + 0.18 * jax.random.normal(key_of[12], (INNER,), jnp.float32), 0.1, 1.9)
    w_out = scatter_about(key_of[13], (INNER, D), INNER ** -0.5, 0.09375, ((0, 16),))
    return {"tokens": tokens, "complement": complement, "embed": embed, "w_x": w_x, "w_z": w_z, "w_bc": w_bc, "w_dt": w_dt, "dt_bias": dt_bias, "decay_rate": decay_rate, "d_skip": d_skip, "conv_x": conv_x, "conv_bc": conv_bc, "norm_gain": norm_gain, "w_out": w_out}


EPSILON = 1e-05

def conv_silu(raw, weight):
    count = raw.shape[0]
    rawf = lax.optimization_barrier(raw).astype(jnp.float32)
    padded = jnp.concatenate([jnp.zeros((CONV - 1, raw.shape[1]), jnp.float32), rawf], 0)
    total = jnp.zeros((count, raw.shape[1]), jnp.float32)
    for offset in range(CONV):
        total = total + padded[offset:offset + count] * weight[offset].astype(jnp.float32)
    return jax.nn.silu(total)

def ssd_scan(values, b_in, c_out, step, decay_rate):
    length = values.shape[0]
    block = L_DEV
    count = length // block
    vals = values.reshape(count, block, HEADS, HEAD_DIM)
    bins = b_in.reshape(count, block, STATE)
    couts = c_out.reshape(count, block, STATE)
    steps = step.reshape(count, block, HEADS)
    causal = (lax.iota(jnp.int32, block)[:, None] >= lax.iota(jnp.int32, block)[None, :])[None, :, :]

    def advance(state, pieces):
        vblock, bblock, cblock, sblock = pieces
        cumul = jnp.cumsum(-sblock * decay_rate[None, :], axis=0)
        cumt = cumul.T
        scores = jnp.dot(cblock, bblock.T, precision=lax.Precision.HIGHEST)
        spread = jnp.where(causal, cumt[:, :, None] - cumt[:, None, :], 0.0)
        weights = jnp.where(causal, jnp.exp(spread), 0.0) * scores[None, :, :] * sblock.T[:, None, :]
        within = jnp.einsum('hts,shp->thp', weights, vblock, precision=lax.Precision.HIGHEST)
        inter = jnp.einsum('tn,hnp->thp', cblock, state, precision=lax.Precision.HIGHEST) * jnp.exp(cumul)[:, :, None]
        last = cumul[-1]
        weighted = vblock * (jnp.exp(last[None, :] - cumul) * sblock)[:, :, None]
        fresh = jnp.einsum('sn,shp->hnp', bblock, weighted, precision=lax.Precision.HIGHEST)
        return (state * jnp.exp(last)[:, None, None] + fresh, within + inter)
    start = jnp.zeros((HEADS, STATE, HEAD_DIM), jnp.float32)
    _, outputs = lax.scan(advance, start, (vals, bins, couts, steps))
    return outputs.reshape(length, HEADS, HEAD_DIM)

def strand(ids, embed, w_x, w_z, w_bc, w_dt, dt_bias, decay_rate, d_skip, conv_x, conv_bc, norm_gain):
    length = ids.shape[0]
    emb = embed[ids]
    x_raw = jnp.dot(emb, w_x, preferred_element_type=jnp.float32).astype(jnp.bfloat16)
    z_gate = jnp.dot(emb, w_z, preferred_element_type=jnp.float32).astype(jnp.bfloat16)
    bc_raw = jnp.dot(emb, w_bc, preferred_element_type=jnp.float32).astype(jnp.bfloat16)
    dt_raw = jnp.dot(emb, w_dt, preferred_element_type=jnp.float32)
    values = conv_silu(x_raw, conv_x).reshape(length, HEADS, HEAD_DIM)
    bc_conv = conv_silu(bc_raw, conv_bc)
    b_in = bc_conv[:, :STATE]
    c_out = bc_conv[:, STATE:]
    step = jax.nn.softplus(dt_raw + dt_bias[None, :])
    scanned = ssd_scan(values, b_in, c_out, step, decay_rate)
    scanned = scanned + values * d_skip[None, :, None]
    gated = scanned.reshape(length, INNER) * jax.nn.silu(lax.optimization_barrier(z_gate).astype(jnp.float32))
    scale = lax.rsqrt(lax.optimization_barrier(jnp.mean(gated * gated, axis=1, keepdims=True)) + EPSILON)
    return (gated * scale * norm_gain[None, :]).astype(jnp.bfloat16)

def reference(tokens, complement, embed, w_x, w_z, w_bc, w_dt, dt_bias, decay_rate, d_skip, conv_x, conv_bc, norm_gain, w_out):
    params = (embed, w_x, w_z, w_bc, w_dt, dt_bias, decay_rate, d_skip, conv_x, conv_bc, norm_gain)
    forward = strand(tokens, *params)
    back_ids = jnp.flip(complement[tokens], 0).astype(jnp.int32)
    backward = strand(back_ids, *params)
    combined = (forward.astype(jnp.float32) + jnp.flip(backward, 0).astype(jnp.float32)).astype(jnp.bfloat16)
    return jnp.dot(combined, w_out, preferred_element_type=jnp.float32).astype(jnp.bfloat16)
```

```python
import jax
import jax.numpy as jnp
import numpy as np
from jax import lax
from jax.experimental import pallas as pl
from jax.experimental.pallas import tpu as pltpu
from jax.sharding import PartitionSpec as P

HEADS = 64
HEAD_DIM = 64
STATE = 128
CONV = 4
VOCAB = 5
ROWS = 256
OWN_HEADS = 4
OWN = OWN_HEADS * HEAD_DIM
SEQ = 32
CHAN = 16
CHIPS = SEQ // 2
LENGTH = SEQ * ROWS
LINES = LENGTH // 128
EPSILON = 1e-05
NONE = VOCAB
VMEM = pltpu.VMEM
SMEM = pltpu.SMEM
F32 = jnp.float32
BF16 = jnp.bfloat16


def gram_table():
    table = np.zeros((64, 1024), np.float32)
    for older in range(31):
        for newer in range(30):
            pair = lambda code: (5, 5) if code == 30 else (code // 5, code % 5)
            for tap, symbol in enumerate(pair(older) + pair(newer)):
                if symbol < VOCAB:
                    table[tap * 8 + symbol, older * 32 + newer] = 1
                    table[32 + tap * 8 + symbol, older * 32 + newer] = 1
    return table


def spread_table():
    row, column = (np.arange(128)[:, None], np.arange(OWN)[None, :])
    return (row // 32 == column // HEAD_DIM).astype(np.float32)


def place():
    return lax.axis_index("seq"), lax.axis_index("chan")


def iota(shape, axis):
    return lax.broadcasted_iota(jnp.int32, shape, axis)


def fiota(shape, axis):
    return iota(shape, axis).astype(F32)


def dot(a, b, contract):
    return lax.dot_general(a, b, ((contract[:1], contract[1:]), ((), ())), preferred_element_type=F32)


def silu(x):
    return x / (1.0 + jnp.exp(-x))


def tables_kernel(tokens, sibling, embed, w_x, w_z, w_bc, w_dt, dt_bias, decay, send, table, steps):
    seq, chan = place()
    emb = embed[...]
    x_tab = dot(emb, w_x[...], (1, 0)).astype(BF16).astype(F32)
    z_tab = dot(emb, w_z[...], (1, 0)).astype(BF16).astype(F32)
    table[...] = jnp.zeros(table.shape, F32)
    table[0:VOCAB, 0:OWN] = x_tab
    table[0:VOCAB, OWN:] = silu(z_tab)
    dt_tab = dot(emb, w_dt[...], (1, 0))
    lane = iota((VOCAB, OWN_HEADS), 1)
    bias = jnp.zeros((VOCAB, OWN_HEADS), F32)
    rate = jnp.zeros((VOCAB, OWN_HEADS), F32)
    for head in range(OWN_HEADS):
        bias = jnp.where(lane == head, dt_bias[head], bias)
        rate = jnp.where(lane == head, decay[head], rate)
    raw = dt_tab + bias
    step = jnp.maximum(raw, 0.0) + jnp.log1p(jnp.exp(-jnp.abs(raw)))
    steps[...] = jnp.zeros(steps.shape, F32)
    steps[0:VOCAB, 0:OWN_HEADS] = step
    steps[8 : 8 + VOCAB, 0:OWN_HEADS] = step * rate
    part = embed[:, pl.ds(pl.multiple_of(chan * 128, 128), 128)]
    bc = dot(part, w_bc[...], (1, 0))
    mine = tokens[...].astype(F32)
    other = sibling[...].astype(F32)
    first = lax.rem(seq, 2) == 0
    send[0, 0:VOCAB, :] = bc[:, :STATE]
    send[0, 5:7, :] = jnp.where(first, mine, other)
    send[0, 7:8, :] = jnp.zeros((1, 128), F32)
    send[0, 8 : 8 + VOCAB, :] = bc[:, STATE:]
    send[0, 13:15, :] = jnp.where(first, other, mine)
    send[0, 15:16, :] = jnp.zeros((1, 128), F32)
    block = send[0]
    for peer in range(1, CHIPS):
        send[peer] = block


def before(x, steps):
    lane, line = (iota(x.shape, 1), iota(x.shape, 0))
    turned = pltpu.roll(x, steps, 1)
    over = jnp.where(line == 0, float(NONE), pltpu.roll(turned, 1, 0))
    return jnp.where(lane < steps, over, turned)


def after(x, steps):
    lane, line = (iota(x.shape, 1), iota(x.shape, 0))
    turned = pltpu.roll(x, 128 - steps, 1)
    over = jnp.where(line == LINES - 1, float(NONE), pltpu.roll(turned, LINES - 1, 0))
    return jnp.where(lane >= 128 - steps, over, turned)


def hot(symbols, count):
    return jnp.where(fiota((count, symbols.shape[1]), 0) == symbols, 1.0, 0.0)


def taps_table(taps, table):
    return jnp.concatenate([taps[k : k + 1, :] * table for k in range(CONV)], 0)


def halves(x):
    high = x.astype(BF16)
    low = (x - high.astype(F32)).astype(BF16)
    return jnp.concatenate([high.astype(F32), low.astype(F32)], 0).astype(BF16)


def scan_kernel(
    received, complement, table, steps, step_at, conv_x, conv_bc, d_skip, gain, grams, grams_t, spread,
    out, send, tok_ref, fwd_ref, back_ref,
):
    seq, _ = place()
    for chip in range(CHIPS):
        tok_ref[4 * chip : 4 * chip + 2, :] = received[chip, 5:7, :]
        tok_ref[4 * chip + 2 : 4 * chip + 4, :] = received[chip, 13:15, :]
    bc_sum = received[0]
    for chip in range(1, CHIPS):
        bc_sum = bc_sum + received[chip]
    bc_sum = jnp.where(lax.rem(iota((16, 128), 0), 8) < VOCAB, bc_sum, 0.0)
    bc_sum = bc_sum.astype(BF16).astype(F32)
    bc_tab = jnp.concatenate([bc_sum[0:8], bc_sum[8:16]], 1)
    conv_tab = jnp.concatenate(
        [
            taps_table(conv_x[...].astype(F32), table[:, :OWN]),
            taps_table(conv_bc[...].astype(F32), bc_tab),
            jnp.concatenate([jnp.zeros((24, OWN), F32), table[:, OWN:]], 0),
        ],
        1,
    )
    conv_tab = halves(conv_tab)

    tok = tok_ref[...]
    flipped = jnp.zeros(tok.shape, F32)
    for symbol in range(VOCAB):
        flipped = jnp.where(tok == float(symbol), complement[symbol].astype(F32), flipped)
    fwd = [before(tok, 3), before(tok, 2), before(tok, 1), tok]
    back = [after(flipped, 3), after(flipped, 2), after(flipped, 1), flipped]
    for k in range(CONV):
        fwd_ref[k] = fwd[k]
        back_ref[k] = back[k]

    line = iota((LINES, 128), 0)
    start, end = (2 * seq, 2 * seq + 2)
    ahead = line < start
    inside = jnp.logical_or(ahead, line >= end)
    gram = [jnp.where(ahead, f, b) for f, b in zip(fwd, back)]
    older = gram[0] * 5.0 + gram[1] + jnp.where(ahead, 0.0, 32.0)
    newer = gram[2] * 5.0 + gram[3]
    newest = [jnp.logical_and(gram[3] == float(symbol), inside) for symbol in range(VOCAB)]
    marks = jnp.concatenate([jnp.where(hit, 1.0, 0.0) for hit in newest], 0).astype(BF16)
    row, column = (iota((128, 128), 0), iota((128, 128), 1))
    within = jnp.concatenate(
        [
            jnp.where(row > column, 1.0, 0.0),
            jnp.where(row < column, 1.0, 0.0),
            jnp.ones((128, 128), F32),
        ],
        1,
    ).astype(BF16)
    counts = dot(marks, within, (1, 0))
    parts = [counts[LINES * symbol : LINES * (symbol + 1)] for symbol in range(VOCAB)]
    totals = jnp.concatenate([part[:, 256:384] for part in parts], 1).astype(BF16)
    to, of = (iota((LINES, LINES), 0), iota((LINES, LINES), 1))
    between = jnp.logical_or(
        jnp.logical_and(to < of, of < start), jnp.logical_and(of >= end, of < to)
    )
    lines_between = dot(jnp.where(between, 1.0, 0.0).astype(BF16), totals, (1, 0))
    passed = [
        jnp.where(ahead, part[:, 0:128], part[:, 128:256]) + lines_between[:, 128 * k : 128 * k + 128]
        for k, part in enumerate(parts)
    ]
    weights = []
    for head in range(OWN_HEADS):
        lost = jnp.zeros((LINES, 128), F32)
        own_step = jnp.zeros((LINES, 128), F32)
        for symbol in range(VOCAB):
            lost = lost + step_at[8 + symbol, head] * passed[symbol]
            own_step = jnp.where(newest[symbol], step_at[symbol, head], own_step)
        weights.append(own_step * jnp.exp(-lost))

    sums = jnp.zeros((64, 128), F32)
    for first in range(0, LINES, 2):
        left, right = ([], [])
        for at in (first, first + 1):
            left.append(hot(older[at : at + 1], 64))
            hits = fiota((32, 128), 0) == newer[at : at + 1]
            right.append(
                jnp.concatenate([jnp.where(hits, w[at : at + 1], 0.0) for w in weights], 0)
            )
        sums = sums + dot(
            jnp.concatenate(left, 1).astype(BF16), jnp.concatenate(right, 1).astype(BF16), (1, 1)
        )

    gram_values = silu(dot(grams_t[...], conv_tab[:, :OWN], (1, 0)))
    gram_b = silu(dot(conv_tab[:, OWN : OWN + STATE], grams[...], (0, 0))).astype(BF16)
    same = jnp.where(lax.rem(iota((32, 128), 1), 32) == iota((32, 128), 0), 1.0, 0.0)
    states = []
    for strand in range(2):
        placed = jnp.concatenate(
            [sums[32 * strand + code : 32 * strand + code + 1] * same for code in range(32)], 0
        )
        wide = dot(placed.astype(BF16), spread[...], (1, 0))
        states.append(dot(gram_b, (wide * gram_values).astype(BF16), (1, 0)))

    hots = []
    for ref in (fwd_ref, back_ref):
        for k in range(2):
            hots.append(
                jnp.concatenate([hot(ref[tap, pl.ds(start + k, 1), :], 8) for tap in range(CONV)], 0)
            )
    hots = jnp.concatenate(hots, 1)
    mixed = dot(jnp.concatenate([hots, hots], 0).astype(BF16), conv_tab, (0, 0))
    gate = mixed[:, OWN + 2 * STATE :]
    mixed = silu(mixed[:, : OWN + 2 * STATE])
    head_of = iota((1, OWN), 1) // HEAD_DIM
    skip = jnp.zeros((1, OWN), F32)
    for head in range(OWN_HEADS):
        skip = jnp.where(head_of == head, d_skip[head], skip)
    row, column = (iota((ROWS, ROWS), 0), iota((ROWS, ROWS), 1))
    squares = []
    for strand in range(2):
        rows = slice(ROWS * strand, ROWS * (strand + 1))
        values = mixed[rows, :OWN]
        b_in = mixed[rows, OWN : OWN + STATE].astype(BF16)
        c_out = mixed[rows, OWN + STATE :]
        causal = row >= column if strand == 0 else row <= column
        order = row <= column if strand == 0 else row >= column
        symbols = hots[24:32, rows]
        seen = dot(symbols.astype(BF16), jnp.where(order, 1.0, 0.0).astype(BF16), (1, 0))
        cumul, step = ([], [])
        for head in range(OWN_HEADS):
            total = jnp.zeros((1, ROWS), F32)
            own_step = jnp.zeros((1, ROWS), F32)
            for symbol in range(VOCAB):
                total = total - step_at[8 + symbol, head] * seen[symbol : symbol + 1]
                own_step = own_step + step_at[symbol, head] * symbols[symbol : symbol + 1]
            cumul.append(total)
            step.append(own_step)
        across = jnp.transpose(
            jnp.concatenate(cumul + [jnp.zeros((128 - OWN_HEADS, ROWS), F32)], 0)
        )
        scores = dot(c_out.astype(BF16), b_in, (1, 1))
        left, right, tail_left, tail_right = ([], [], [], [])
        for head in range(OWN_HEADS):
            column_of = across[:, head : head + 1]
            decayed = jnp.exp(jnp.where(causal, column_of - cumul[head], -1e30))
            left.append((decayed * (scores * step[head])).astype(BF16))
            right.append(jnp.where(head_of == head, values, 0.0).astype(BF16))
            tail_left.append((c_out * jnp.exp(column_of)).astype(BF16))
            tail_right.append(jnp.where(head_of == head, states[strand], 0.0).astype(BF16))
        ssd = dot(
            jnp.concatenate(left + tail_left, 1), jnp.concatenate(right + tail_right, 0), (1, 0)
        )
        gated = (ssd + values * skip) * gate[rows]
        out[rows, :] = gated * gain[...]
        squared = gated * gated
        squares.append(
            jnp.sum(jnp.transpose(squared[:, :128] + squared[:, 128:]), axis=0, keepdims=True)
        )
    mine = jnp.concatenate(
        [square[:, 128 * k : 128 * k + 128] for square in squares for k in range(2)], 0
    )
    for peer in range(CHAN):
        send[peer] = mine


def project_kernel(squares, gated, w_out, out):
    total = squares[0]
    for peer in range(1, CHAN):
        total = total + squares[peer]
    scale = lax.rsqrt(total / (HEADS * HEAD_DIM) + EPSILON)
    normed = []
    for part in range(4):
        down = jnp.transpose(jnp.broadcast_to(scale[part : part + 1], (128, 128)))
        block = gated[128 * part : 128 * part + 128, :]
        normed.append((block * jnp.concatenate([down, down], 1)).astype(BF16).astype(F32))
    combined = jnp.concatenate([normed[0] + normed[2], normed[1] + normed[3]], 0).astype(BF16)
    mixed = dot(combined, w_out[...], (1, 0))
    out[...] = mixed.astype(BF16).reshape(out.shape)


def call(kernel, outs, kinds, scratch=()):
    return pl.pallas_call(
        kernel,
        out_shape=outs,
        in_specs=[pl.BlockSpec(memory_space=kind) for kind in kinds],
        out_specs=jax.tree.map(lambda _: pl.BlockSpec(memory_space=VMEM), outs),
        scratch_shapes=scratch,
        compiler_params=pltpu.CompilerParams(vmem_limit_bytes=48 * 2**20),
    )


def make_tables(*args):
    return call(
        tables_kernel,
        (
            jax.ShapeDtypeStruct((CHIPS, 16, 128), F32),
            jax.ShapeDtypeStruct((8, 2 * OWN), F32),
            jax.ShapeDtypeStruct((16, 128), F32),
        ),
        [VMEM] * 7 + [SMEM] * 2,
    )(*args)


def make_scan(received, complement, table, steps, conv_x, conv_bc, d_skip, norm_gain):
    grams = gram_table()
    return call(
        scan_kernel,
        (
            jax.ShapeDtypeStruct((2 * ROWS, OWN), F32),
            jax.ShapeDtypeStruct((CHAN, 4, 128), F32),
        ),
        [VMEM, SMEM, VMEM, VMEM, SMEM, VMEM, VMEM, SMEM, VMEM, VMEM, VMEM, VMEM],
        [
            pltpu.VMEM((LINES, 128), F32),
            pltpu.VMEM((CONV, LINES, 128), F32),
            pltpu.VMEM((CONV, LINES, 128), F32),
        ],
    )(
        received, complement, table, steps, steps, conv_x, conv_bc, d_skip, norm_gain.reshape(1, OWN),
        jnp.asarray(grams, BF16), jnp.asarray(grams.T, BF16), jnp.asarray(spread_table(), BF16),
    )


def make_project(squares, gated, w_out):
    return call(
        project_kernel, jax.ShapeDtypeStruct((CHAN, ROWS // CHAN, w_out.shape[1]), BF16), [VMEM] * 3
    )(squares, gated, w_out)


def per_device(
    tokens, complement, embed, w_x, w_z, w_bc, w_dt, dt_bias, decay_rate, d_skip, conv_x, conv_bc,
    norm_gain, w_out,
):
    own = tokens.reshape(2, 128)
    sibling = lax.ppermute(own, "seq", [(source, source ^ 1) for source in range(SEQ)])
    send, table, steps = make_tables(
        own, sibling, embed, w_x, w_z, w_bc, w_dt, dt_bias, decay_rate
    )
    groups = [
        [(2 * chip + core) * CHAN + (chip + shift) % CHAN for chip in range(CHIPS)]
        for core in range(2)
        for shift in range(CHAN)
    ]
    received = lax.all_to_all(
        send, ("seq", "chan"), 0, 0, tiled=True, axis_index_groups=groups
    )
    gated, squares = make_scan(
        received, complement, table, steps, conv_x, conv_bc, d_skip, norm_gain
    )
    squares = lax.all_to_all(squares, "chan", 0, 0, tiled=True)
    partial = make_project(squares, gated, w_out)
    pieces = lax.all_to_all(partial, "chan", 0, 0, tiled=True)
    return jnp.sum(pieces.astype(F32), axis=0).astype(BF16)


def solution(mesh):
    placed = (
        P("seq"),
        P(),
        P(),
        P(None, "chan"),
        P(None, "chan"),
        P("chan", None),
        P(None, "chan"),
        P("chan"),
        P("chan"),
        P("chan"),
        P(None, "chan"),
        P(),
        P("chan"),
        P("chan", None),
    )
    return jax.shard_map(
        per_device, mesh=mesh, in_specs=placed, out_specs=P(("seq", "chan"), None), check_vma=False
    )
```

```python
import jax
import jax.numpy as jnp
import numpy as np
from jax import lax
from jax.experimental import pallas as pl
from jax.experimental.pallas import tpu as pltpu
from jax.sharding import PartitionSpec as P

HEADS = 64
HEAD_DIM = 64
STATE = 128
CONV = 4
VOCAB = 5
ROWS = 256
OWN_HEADS = 4
OWN = OWN_HEADS * HEAD_DIM
SEQ = 32
CHAN = 16
CHIPS = SEQ // 2
LENGTH = SEQ * ROWS
LINES = LENGTH // 128
SIDE = 4
PART = ROWS // SIDE
PIECE = PART // SIDE
EPSILON = 1e-05
NONE = VOCAB
VMEM = pltpu.VMEM
SMEM = pltpu.SMEM
F32 = jnp.float32
BF16 = jnp.bfloat16


def gram_table():
    table = np.zeros((64, 1024), np.float32)
    for older in range(31):
        for newer in range(30):
            pair = lambda code: (5, 5) if code == 30 else (code // 5, code % 5)
            for tap, symbol in enumerate(pair(older) + pair(newer)):
                if symbol < VOCAB:
                    table[tap * 8 + symbol, older * 32 + newer] = 1
                    table[32 + tap * 8 + symbol, older * 32 + newer] = 1
    return table


def spread_table():
    row, column = (np.arange(128)[:, None], np.arange(OWN)[None, :])
    return (row // 32 == column // HEAD_DIM).astype(np.float32)


def place():
    return lax.axis_index("seq"), lax.axis_index("chan")


def iota(shape, axis):
    return lax.broadcasted_iota(jnp.int32, shape, axis)


def fiota(shape, axis):
    return iota(shape, axis).astype(F32)


def dot(a, b, contract):
    return lax.dot_general(a, b, ((contract[:1], contract[1:]), ((), ())), preferred_element_type=F32)


def silu(x):
    return x / (1.0 + jnp.exp(-x))


def send_kernel(tokens, sibling, embed, w_bc, send):
    seq, chan = place()
    part = embed[:, pl.ds(pl.multiple_of(chan * 128, 128), 128)]
    bc = dot(part, w_bc[...], (1, 0))
    mine = tokens[...].astype(F32)
    other = sibling[...].astype(F32)
    first = lax.rem(seq, 2) == 0
    send[0, 0:VOCAB, :] = bc[:, :STATE]
    send[0, 5:7, :] = jnp.where(first, mine, other)
    send[0, 7:8, :] = jnp.zeros((1, 128), F32)
    send[0, 8 : 8 + VOCAB, :] = bc[:, STATE:]
    send[0, 13:15, :] = jnp.where(first, other, mine)
    send[0, 15:16, :] = jnp.zeros((1, 128), F32)
    block = send[0]
    for peer in range(1, CHIPS):
        send[peer] = block


def tables_kernel(embed, w_x, w_z, w_dt, dt_bias, decay, conv_x, grams_t, table, gram_values, steps):
    emb = embed[...]
    x_tab = dot(emb, w_x[...], (1, 0)).astype(BF16).astype(F32)
    z_tab = dot(emb, w_z[...], (1, 0)).astype(BF16).astype(F32)
    pad = jnp.zeros((8 - VOCAB, OWN), F32)
    x_taps = halves(taps_table(conv_x[...].astype(F32), jnp.concatenate([x_tab, pad], 0)))
    gate = jnp.concatenate([jnp.zeros((24, OWN), F32), silu(z_tab), pad], 0)
    table[:, :OWN] = x_taps
    table[:, OWN:] = halves(gate)
    gram_values[...] = silu(dot(grams_t[...], x_taps, (1, 0)))
    dt_tab = dot(emb, w_dt[...], (1, 0))
    lane = iota((VOCAB, OWN_HEADS), 1)
    bias = jnp.zeros((VOCAB, OWN_HEADS), F32)
    rate = jnp.zeros((VOCAB, OWN_HEADS), F32)
    for head in range(OWN_HEADS):
        bias = jnp.where(lane == head, dt_bias[head], bias)
        rate = jnp.where(lane == head, decay[head], rate)
    raw = dt_tab + bias
    step = jnp.maximum(raw, 0.0) + jnp.log1p(jnp.exp(-jnp.abs(raw)))
    steps[...] = jnp.zeros(steps.shape, F32)
    steps[0:VOCAB, 0:OWN_HEADS] = step
    steps[8 : 8 + VOCAB, 0:OWN_HEADS] = step * rate


def before(x, steps):
    lane, line = (iota(x.shape, 1), iota(x.shape, 0))
    turned = pltpu.roll(x, steps, 1)
    over = jnp.where(line == 0, float(NONE), pltpu.roll(turned, 1, 0))
    return jnp.where(lane < steps, over, turned)


def after(x, steps):
    lane, line = (iota(x.shape, 1), iota(x.shape, 0))
    turned = pltpu.roll(x, 128 - steps, 1)
    over = jnp.where(line == LINES - 1, float(NONE), pltpu.roll(turned, LINES - 1, 0))
    return jnp.where(lane >= 128 - steps, over, turned)


def hot(symbols, count):
    return jnp.where(fiota((count, symbols.shape[1]), 0) == symbols, 1.0, 0.0)


def taps_table(taps, table):
    return jnp.concatenate([taps[k : k + 1, :] * table for k in range(CONV)], 0)


def halves(x):
    high = x.astype(BF16)
    low = (x - high.astype(F32)).astype(BF16)
    return jnp.concatenate([high.astype(F32), low.astype(F32)], 0).astype(BF16)


def scan_kernel(
    received, complement, table, gram_values, step_at, conv_bc, d_skip, gain, grams, spread,
    out, send, tok_ref, fwd_ref, back_ref,
):
    seq, _ = place()
    for chip in range(CHIPS):
        tok_ref[4 * chip : 4 * chip + 2, :] = received[chip, 5:7, :]
        tok_ref[4 * chip + 2 : 4 * chip + 4, :] = received[chip, 13:15, :]
    bc_sum = received[0]
    for chip in range(1, CHIPS):
        bc_sum = bc_sum + received[chip]
    bc_sum = jnp.where(lax.rem(iota((16, 128), 0), 8) < VOCAB, bc_sum, 0.0)
    bc_sum = bc_sum.astype(BF16).astype(F32)
    bc_tab = jnp.concatenate([bc_sum[0:8], bc_sum[8:16]], 1)
    bc_taps = halves(taps_table(conv_bc[...].astype(F32), bc_tab))
    conv_tab = jnp.concatenate([table[:, :OWN], bc_taps, table[:, OWN:]], 1)

    tok = tok_ref[...]
    flipped = jnp.zeros(tok.shape, F32)
    for symbol in range(VOCAB):
        flipped = jnp.where(tok == float(symbol), complement[symbol].astype(F32), flipped)
    fwd = [before(tok, 3), before(tok, 2), before(tok, 1), tok]
    back = [after(flipped, 3), after(flipped, 2), after(flipped, 1), flipped]
    for k in range(CONV):
        fwd_ref[k] = fwd[k]
        back_ref[k] = back[k]

    line = iota((LINES, 128), 0)
    start, end = (2 * seq, 2 * seq + 2)
    ahead = line < start
    inside = jnp.logical_or(ahead, line >= end)
    gram = [jnp.where(ahead, f, b) for f, b in zip(fwd, back)]
    older = gram[0] * 5.0 + gram[1] + jnp.where(ahead, 0.0, 32.0)
    newer = gram[2] * 5.0 + gram[3]
    newest = [jnp.logical_and(gram[3] == float(symbol), inside) for symbol in range(VOCAB)]
    marks = jnp.concatenate([jnp.where(hit, 1.0, 0.0) for hit in newest], 0).astype(BF16)
    row, column = (iota((128, 128), 0), iota((128, 128), 1))
    within = jnp.concatenate(
        [
            jnp.where(row > column, 1.0, 0.0),
            jnp.where(row < column, 1.0, 0.0),
            jnp.ones((128, 128), F32),
        ],
        1,
    ).astype(BF16)
    counts = dot(marks, within, (1, 0))
    parts = [counts[LINES * symbol : LINES * (symbol + 1)] for symbol in range(VOCAB)]
    totals = jnp.concatenate([part[:, 256:384] for part in parts], 1).astype(BF16)
    to, of = (iota((LINES, LINES), 0), iota((LINES, LINES), 1))
    between = jnp.logical_or(
        jnp.logical_and(to < of, of < start), jnp.logical_and(of >= end, of < to)
    )
    lines_between = dot(jnp.where(between, 1.0, 0.0).astype(BF16), totals, (1, 0))
    passed = [
        jnp.where(ahead, part[:, 0:128], part[:, 128:256]) + lines_between[:, 128 * k : 128 * k + 128]
        for k, part in enumerate(parts)
    ]
    weights = []
    for head in range(OWN_HEADS):
        lost = jnp.zeros((LINES, 128), F32)
        own_step = jnp.zeros((LINES, 128), F32)
        for symbol in range(VOCAB):
            lost = lost + step_at[8 + symbol, head] * passed[symbol]
            own_step = jnp.where(newest[symbol], step_at[symbol, head], own_step)
        weights.append(own_step * jnp.exp(-lost))

    sums = jnp.zeros((64, 128), F32)
    for first in range(0, LINES, 2):
        left, right = ([], [])
        for at in (first, first + 1):
            left.append(hot(older[at : at + 1], 64))
            hits = fiota((32, 128), 0) == newer[at : at + 1]
            right.append(
                jnp.concatenate([jnp.where(hits, w[at : at + 1], 0.0) for w in weights], 0)
            )
        sums = sums + dot(
            jnp.concatenate(left, 1).astype(BF16), jnp.concatenate(right, 1).astype(BF16), (1, 1)
        )

    gram_b = silu(dot(bc_taps[:, :STATE], grams[...], (0, 0))).astype(BF16)
    same = jnp.where(lax.rem(iota((32, 128), 1), 32) == iota((32, 128), 0), 1.0, 0.0)
    states = []
    for strand in range(2):
        placed = jnp.concatenate(
            [sums[32 * strand + code : 32 * strand + code + 1] * same for code in range(32)], 0
        )
        wide = dot(placed.astype(BF16), spread[...], (1, 0))
        states.append(dot(gram_b, (wide * gram_values[...]).astype(BF16), (1, 0)))

    hots = []
    for ref in (fwd_ref, back_ref):
        for k in range(2):
            hots.append(
                jnp.concatenate([hot(ref[tap, pl.ds(start + k, 1), :], 8) for tap in range(CONV)], 0)
            )
    hots = jnp.concatenate(hots, 1)
    mixed = dot(jnp.concatenate([hots, hots], 0).astype(BF16), conv_tab, (0, 0))
    gate = mixed[:, OWN + 2 * STATE :]
    mixed = silu(mixed[:, : OWN + 2 * STATE])
    head_of = iota((1, OWN), 1) // HEAD_DIM
    skip = jnp.zeros((1, OWN), F32)
    for head in range(OWN_HEADS):
        skip = jnp.where(head_of == head, d_skip[head], skip)
    row, column = (iota((ROWS, ROWS), 0), iota((ROWS, ROWS), 1))
    squares = []
    for strand in range(2):
        rows = slice(ROWS * strand, ROWS * (strand + 1))
        values = mixed[rows, :OWN]
        b_in = mixed[rows, OWN : OWN + STATE].astype(BF16)
        c_out = mixed[rows, OWN + STATE :]
        causal = row >= column if strand == 0 else row <= column
        order = row <= column if strand == 0 else row >= column
        symbols = hots[24:32, rows]
        seen = dot(symbols.astype(BF16), jnp.where(order, 1.0, 0.0).astype(BF16), (1, 0))
        cumul, step = ([], [])
        for head in range(OWN_HEADS):
            total = jnp.zeros((1, ROWS), F32)
            own_step = jnp.zeros((1, ROWS), F32)
            for symbol in range(VOCAB):
                total = total - step_at[8 + symbol, head] * seen[symbol : symbol + 1]
                own_step = own_step + step_at[symbol, head] * symbols[symbol : symbol + 1]
            cumul.append(total)
            step.append(own_step)
        across = jnp.transpose(
            jnp.concatenate(cumul + [jnp.zeros((128 - OWN_HEADS, ROWS), F32)], 0)
        )
        scores = dot(c_out.astype(BF16), b_in, (1, 1))
        left, right, tail_left, tail_right = ([], [], [], [])
        for head in range(OWN_HEADS):
            column_of = across[:, head : head + 1]
            decayed = jnp.exp(jnp.where(causal, column_of - cumul[head], -1e30))
            left.append((decayed * (scores * step[head])).astype(BF16))
            right.append(jnp.where(head_of == head, values, 0.0).astype(BF16))
            tail_left.append((c_out * jnp.exp(column_of)).astype(BF16))
            tail_right.append(jnp.where(head_of == head, states[strand], 0.0).astype(BF16))
        ssd = dot(
            jnp.concatenate(left + tail_left, 1), jnp.concatenate(right + tail_right, 0), (1, 0)
        )
        gated = (ssd + values * skip) * gate[rows]
        out[rows, :] = gated * gain[...]
        squared = gated * gated
        squares.append(
            jnp.sum(jnp.transpose(squared[:, :128] + squared[:, 128:]), axis=0, keepdims=True)
        )
    mine = jnp.concatenate(
        [square[:, 128 * k : 128 * k + 128] for square in squares for k in range(2)], 0
    )
    for peer in range(CHAN):
        send[peer] = mine


def project_kernel(squares, gated, w_out, out):
    total = squares[0]
    for peer in range(1, CHAN):
        total = total + squares[peer]
    scale = lax.rsqrt(total / (HEADS * HEAD_DIM) + EPSILON)
    normed = []
    for part in range(4):
        down = jnp.transpose(jnp.broadcast_to(scale[part : part + 1], (128, 128)))
        block = gated[128 * part : 128 * part + 128, :]
        normed.append((block * jnp.concatenate([down, down], 1)).astype(BF16).astype(F32))
    combined = jnp.concatenate([normed[0] + normed[2], normed[1] + normed[3]], 0).astype(BF16)
    mixed = dot(combined, w_out[...], (1, 0))
    out[...] = mixed.astype(BF16).reshape(out.shape)


def sum_kernel(received, out):
    total = received[0].astype(F32)
    for peer in range(1, SIDE):
        total = total + received[peer].astype(F32)
    out[...] = total.astype(BF16).reshape(out.shape)


def call(kernel, outs, kinds, scratch=()):
    return pl.pallas_call(
        kernel,
        out_shape=outs,
        in_specs=[pl.BlockSpec(memory_space=kind) for kind in kinds],
        out_specs=jax.tree.map(lambda _: pl.BlockSpec(memory_space=VMEM), outs),
        scratch_shapes=scratch,
        compiler_params=pltpu.CompilerParams(vmem_limit_bytes=48 * 2**20),
    )


def make_send(*args):
    return call(send_kernel, jax.ShapeDtypeStruct((CHIPS, 16, 128), F32), [VMEM] * 4)(*args)


def make_tables(*args):
    return call(
        tables_kernel,
        (
            jax.ShapeDtypeStruct((64, 2 * OWN), BF16),
            jax.ShapeDtypeStruct((1024, OWN), F32),
            jax.ShapeDtypeStruct((16, 128), F32),
        ),
        [VMEM] * 4 + [SMEM] * 2 + [VMEM] * 2,
    )(*args, jnp.asarray(gram_table().T, BF16))


def make_scan(received, complement, table, gram_values, steps, conv_bc, d_skip, norm_gain):
    return call(
        scan_kernel,
        (jax.ShapeDtypeStruct((2 * ROWS, OWN), F32), jax.ShapeDtypeStruct((CHAN, 4, 128), F32)),
        [VMEM, SMEM, VMEM, VMEM, SMEM, VMEM, SMEM, VMEM, VMEM, VMEM],
        [
            pltpu.VMEM((LINES, 128), F32),
            pltpu.VMEM((CONV, LINES, 128), F32),
            pltpu.VMEM((CONV, LINES, 128), F32),
        ],
    )(
        received, complement, table, gram_values, steps, conv_bc, d_skip, norm_gain.reshape(1, OWN),
        jnp.asarray(gram_table(), BF16), jnp.asarray(spread_table(), BF16),
    )


def make_project(squares, gated, w_out):
    return call(
        project_kernel, jax.ShapeDtypeStruct((SIDE, PART, w_out.shape[1]), BF16), [VMEM] * 3
    )(squares, gated, w_out)


def make_sum(received, shape):
    return call(sum_kernel, jax.ShapeDtypeStruct(shape, BF16), [VMEM])(received)


def device(seq, chan):
    return seq * CHAN + chan


def mixed_groups():
    side = range(SIDE)
    return [
        [
            device(2 * (SIDE * y + high) + core, (y + right) % SIDE * SIDE + (high + up) % SIDE)
            for y in side
            for high in side
        ]
        for core in range(2)
        for right in side
        for up in side
    ]


def x_groups():
    return [[x * SIDE + z for x in range(SIDE)] for z in range(SIDE)]


def z_groups():
    return [[x * SIDE + z for z in range(SIDE)] for x in range(SIDE)]


def exchange(value, axes, groups=None):
    return lax.all_to_all(value, axes, 0, 0, tiled=True, axis_index_groups=groups)


def per_device(
    tokens, complement, embed, w_x, w_z, w_bc, w_dt, dt_bias, decay_rate, d_skip, conv_x, conv_bc,
    norm_gain, w_out,
):
    own = tokens.reshape(2, 128)
    sibling = lax.ppermute(own, "seq", [(source, source ^ 1) for source in range(SEQ)])
    received = exchange(make_send(own, sibling, embed, w_bc), ("seq", "chan"), mixed_groups())
    table, gram_values, steps = make_tables(embed, w_x, w_z, w_dt, dt_bias, decay_rate, conv_x)
    gated, squares = make_scan(
        received, complement, table, gram_values, steps, conv_bc, d_skip, norm_gain
    )
    partial = make_project(exchange(squares, "chan"), gated, w_out)
    partial = make_sum(exchange(partial, "chan", x_groups()), (SIDE, PIECE, w_out.shape[1]))
    return make_sum(exchange(partial, "chan", z_groups()), (PIECE, w_out.shape[1]))


def solution(mesh):
    placed = (
        P("seq"),
        P(),
        P(),
        P(None, "chan"),
        P(None, "chan"),
        P("chan", None),
        P(None, "chan"),
        P("chan"),
        P("chan"),
        P("chan"),
        P(None, "chan"),
        P(),
        P("chan"),
        P("chan", None),
    )
    return jax.shard_map(
        per_device, mesh=mesh, in_specs=placed, out_specs=P(("seq", "chan"), None), check_vma=False
    )
```

```python
import jax
import jax.numpy as jnp
import numpy as np
from jax import lax
from jax.experimental import pallas as pl
from jax.experimental.pallas import tpu as pltpu
from jax.sharding import PartitionSpec as P

HEADS = 64
HEAD_DIM = 64
STATE = 128
CONV = 4
VOCAB = 5
ROWS = 256
OWN_HEADS = 4
OWN = OWN_HEADS * HEAD_DIM
SEQ = 32
CHAN = 16
CHIPS = SEQ // 2
LENGTH = SEQ * ROWS
LINES = LENGTH // 128
SIDE = 4
PAIR_HEADS = 2 * OWN_HEADS
PAIR = 2 * OWN
GROUP = CHAN // 2
LINE = 128
PIECE = LINE // GROUP
EPSILON = 1e-05
NONE = VOCAB
VMEM = pltpu.VMEM
SMEM = pltpu.SMEM
F32 = jnp.float32
BF16 = jnp.bfloat16


def gram_table():
    table = np.zeros((64, 1024), np.float32)
    for older in range(31):
        for newer in range(30):
            pair = lambda code: (5, 5) if code == 30 else (code // 5, code % 5)
            for tap, symbol in enumerate(pair(older) + pair(newer)):
                if symbol < VOCAB:
                    table[tap * 8 + symbol, older * 32 + newer] = 1
                    table[32 + tap * 8 + symbol, older * 32 + newer] = 1
    return table


def place():
    return lax.axis_index("seq"), lax.axis_index("chan")


def iota(shape, axis):
    return lax.broadcasted_iota(jnp.int32, shape, axis)


def fiota(shape, axis):
    return iota(shape, axis).astype(F32)


def dot(a, b, contract):
    return lax.dot_general(a, b, ((contract[:1], contract[1:]), ((), ())), preferred_element_type=F32)


def silu(x):
    return x / (1.0 + jnp.exp(-x))


def send_kernel(tokens, sibling, embed, w_bc, send):
    seq, chan = place()
    part = embed[:, pl.ds(pl.multiple_of(chan * 128, 128), 128)]
    bc = dot(part, w_bc[...], (1, 0))
    mine = tokens[...].astype(F32)
    other = sibling[...].astype(F32)
    first = lax.rem(seq, 2) == 0
    send[0, 0:VOCAB, :] = bc[:, :STATE]
    send[0, 5:7, :] = jnp.where(first, mine, other)
    send[0, 7:8, :] = jnp.zeros((1, 128), F32)
    send[0, 8 : 8 + VOCAB, :] = bc[:, STATE:]
    send[0, 13:15, :] = jnp.where(first, other, mine)
    send[0, 15:16, :] = jnp.zeros((1, 128), F32)
    block = send[0]
    for peer in range(1, CHIPS):
        send[peer] = block


def tables_kernel(embed, w_x, w_z, w_dt, params, tables):
    emb = embed[...]
    x_tab = dot(emb, w_x[...], (1, 0)).astype(BF16).astype(F32)
    z_tab = dot(emb, w_z[...], (1, 0)).astype(BF16).astype(F32)
    tables[...] = jnp.zeros(tables.shape, F32)
    tables[0:VOCAB, :] = x_tab
    tables[8 : 8 + VOCAB, :] = silu(z_tab)
    tables[16:24, :] = params[...]
    raw = dot(emb, w_dt[...], (1, 1)) + params[6:7, 0:OWN_HEADS]
    step = jnp.maximum(raw, 0.0) + jnp.log1p(jnp.exp(-jnp.abs(raw)))
    tables[24 : 24 + VOCAB, 0:OWN_HEADS] = step
    tables[24 : 24 + VOCAB, LINE : LINE + OWN_HEADS] = step * params[7:8, 0:OWN_HEADS]


def prepare_kernel(mine, other, conv_bc, grams_in, complement, tables, rows, steps):
    for side, given in enumerate((mine, other)):
        at = slice(OWN * side, OWN * (side + 1))
        x_taps = halves(taps_table(given[16:20, :], given[0:8, :]))
        tables[:, at] = x_taps
        gates = jnp.concatenate([jnp.zeros((24, OWN), F32), given[8:16, :]], 0)
        tables[:, PAIR + OWN * side : PAIR + OWN * (side + 1)] = halves(gates)
        rows[0:8, at] = given[16:24, :]
    tables[:, 2 * PAIR :] = grams_in[...]
    rows[8:12, 0 : 2 * STATE] = conv_bc[...].astype(F32)
    rows[8:12, 2 * STATE :] = jnp.zeros((4, PAIR - 2 * STATE), F32)
    rows[12:16, :] = jnp.zeros((4, PAIR), F32)
    for part in range(2):
        at = slice(LINE * part, LINE * (part + 1))
        steps[8 * part : 8 * part + 8, :] = given_steps(mine, at) + pltpu.roll(given_steps(other, at), OWN_HEADS, 1)
    lane = iota((1, LINE), 1)
    flips = jnp.zeros((1, LINE), F32)
    for symbol in range(VOCAB):
        flips = jnp.where(lane == symbol, complement[symbol].astype(F32), flips)
    steps[15:16, :] = flips


def given_steps(given, at):
    return given[24:32, at]


def before(x, steps):
    lane, line = (iota(x.shape, 1), iota(x.shape, 0))
    turned = pltpu.roll(x, steps, 1)
    over = jnp.where(line == 0, float(NONE), pltpu.roll(turned, 1, 0))
    return jnp.where(lane < steps, over, turned)


def after(x, steps):
    lane, line = (iota(x.shape, 1), iota(x.shape, 0))
    turned = pltpu.roll(x, 128 - steps, 1)
    over = jnp.where(line == LINES - 1, float(NONE), pltpu.roll(turned, LINES - 1, 0))
    return jnp.where(lane >= 128 - steps, over, turned)


def hot(symbols, count):
    return jnp.where(fiota((count, symbols.shape[1]), 0) == symbols, 1.0, 0.0)


def taps_table(taps, table):
    return jnp.concatenate([taps[k : k + 1, :] * table for k in range(CONV)], 0)


def halves(x):
    high = x.astype(BF16)
    low = (x - high.astype(F32)).astype(BF16)
    return jnp.concatenate([high.astype(F32), low.astype(F32)], 0).astype(BF16)


def scan_kernel(
    received, tables, rows, step_at, out, send,
    tok_ref, fwd_ref, back_ref,
):
    seq, chan = place()
    own_line = 2 * seq + chan // GROUP
    for chip in range(CHIPS):
        tok_ref[4 * chip : 4 * chip + 2, :] = received[chip, 5:7, :]
        tok_ref[4 * chip + 2 : 4 * chip + 4, :] = received[chip, 13:15, :]
    bc_sum = received[0]
    for chip in range(1, CHIPS):
        bc_sum = bc_sum + received[chip]
    bc_sum = jnp.where(lax.rem(iota((16, 128), 0), 8) < VOCAB, bc_sum, 0.0)
    bc_sum = bc_sum.astype(BF16).astype(F32)
    bc_tab = jnp.concatenate([bc_sum[0:8], bc_sum[8:16]], 1)
    bc_taps = halves(taps_table(rows[8:12, 0 : 2 * STATE], bc_tab))
    conv_tab = jnp.concatenate([tables[:, :PAIR], bc_taps, tables[:, PAIR : 2 * PAIR]], 1)

    tok = tok_ref[...]
    flipped = jnp.zeros(tok.shape, F32)
    for symbol in range(VOCAB):
        flipped = jnp.where(tok == float(symbol), step_at[15, symbol], flipped)
    fwd = [before(tok, 3), before(tok, 2), before(tok, 1), tok]
    back = [after(flipped, 3), after(flipped, 2), after(flipped, 1), flipped]
    for k in range(CONV):
        fwd_ref[k] = fwd[k]
        back_ref[k] = back[k]

    line = iota((LINES, 128), 0)
    ahead = line < own_line
    inside = line != own_line
    gram = [jnp.where(ahead, f, b) for f, b in zip(fwd, back)]
    older = gram[0] * 5.0 + gram[1] + jnp.where(ahead, 0.0, 32.0)
    newer = gram[2] * 5.0 + gram[3]
    newest = [jnp.logical_and(gram[3] == float(symbol), inside) for symbol in range(VOCAB)]
    marks = jnp.concatenate([jnp.where(hit, 1.0, 0.0) for hit in newest], 0).astype(BF16)
    row, column = (iota((128, 128), 0), iota((128, 128), 1))
    within = jnp.concatenate(
        [
            jnp.where(row > column, 1.0, 0.0),
            jnp.where(row < column, 1.0, 0.0),
            jnp.ones((128, 128), F32),
        ],
        1,
    ).astype(BF16)
    counts = dot(marks, within, (1, 0))
    parts = [counts[LINES * symbol : LINES * (symbol + 1)] for symbol in range(VOCAB)]
    totals = jnp.concatenate([part[:, 256:384] for part in parts], 1).astype(BF16)
    to, of = (iota((LINES, LINES), 0), iota((LINES, LINES), 1))
    between = jnp.logical_or(
        jnp.logical_and(to < of, of < own_line), jnp.logical_and(of > own_line, of < to)
    )
    lines_between = dot(jnp.where(between, 1.0, 0.0).astype(BF16), totals, (1, 0))
    passed = [
        jnp.where(ahead, part[:, 0:128], part[:, 128:256]) + lines_between[:, 128 * k : 128 * k + 128]
        for k, part in enumerate(parts)
    ]
    weights = []
    for head in range(PAIR_HEADS):
        lost = jnp.zeros((LINES, 128), F32)
        own_step = jnp.zeros((LINES, 128), F32)
        for symbol in range(VOCAB):
            lost = lost + step_at[8 + symbol, head] * passed[symbol]
            own_step = jnp.where(newest[symbol], step_at[symbol, head], own_step)
        weights.append(own_step * jnp.exp(-lost))

    sums = jnp.zeros((64, 32 * PAIR_HEADS), F32)
    for first in range(0, LINES, 2):
        left, right = ([], [])
        for at in (first, first + 1):
            left.append(hot(older[at : at + 1], 64))
            hits = fiota((32, 128), 0) == newer[at : at + 1]
            right.append(
                jnp.concatenate([jnp.where(hits, w[at : at + 1], 0.0) for w in weights], 0)
            )
        sums = sums + dot(
            jnp.concatenate(left, 1).astype(BF16), jnp.concatenate(right, 1).astype(BF16), (1, 1)
        )

    gram_b = silu(dot(bc_taps[:, :STATE], tables[:, 2 * PAIR :], (0, 0))).astype(BF16)
    wide_code = (32, 32 * PAIR_HEADS)
    same = jnp.where(lax.rem(iota(wide_code, 1), 32) == iota(wide_code, 0), 1.0, 0.0)
    gram_values = silu(dot(tables[:, 2 * PAIR :], tables[:, :PAIR], (0, 0))).astype(BF16)
    shape = (32 * PAIR_HEADS, PAIR)
    spread = jnp.where(iota(shape, 0) // 32 == iota(shape, 1) // HEAD_DIM, 1.0, 0.0).astype(BF16)
    states = []
    for strand in range(2):
        placed = jnp.concatenate(
            [sums[32 * strand + code : 32 * strand + code + 1] * same for code in range(32)], 0
        )
        wide = dot(placed.astype(BF16), spread, (1, 0))
        states.append(dot(gram_b, wide.astype(BF16) * gram_values, (1, 0)))

    hots = [
        jnp.concatenate([hot(ref[tap, pl.ds(own_line, 1), :], 8) for tap in range(CONV)], 0)
        for ref in (fwd_ref, back_ref)
    ]
    hots = jnp.concatenate(hots, 1)
    mixed = dot(jnp.concatenate([hots, hots], 0).astype(BF16), conv_tab, (0, 0))
    gate = mixed[:, PAIR + 2 * STATE :]
    mixed = silu(mixed[:, : PAIR + 2 * STATE])
    head_of = iota((1, OWN), 1) // HEAD_DIM
    row, column = (iota((LINE, LINE), 0), iota((LINE, LINE), 1))
    squares = []
    for strand in range(2):
        own = slice(LINE * strand, LINE * (strand + 1))
        b_in = mixed[own, PAIR : PAIR + STATE].astype(BF16)
        c_out = mixed[own, PAIR + STATE :]
        causal = row >= column if strand == 0 else row <= column
        order = row <= column if strand == 0 else row >= column
        symbols = hots[24:32, own]
        seen = dot(symbols.astype(BF16), jnp.where(order, 1.0, 0.0).astype(BF16), (1, 0))
        cumul, step = ([], [])
        for head in range(PAIR_HEADS):
            total = jnp.zeros((1, LINE), F32)
            own_step = jnp.zeros((1, LINE), F32)
            for symbol in range(VOCAB):
                total = total - step_at[8 + symbol, head] * seen[symbol : symbol + 1]
                own_step = own_step + step_at[symbol, head] * symbols[symbol : symbol + 1]
            cumul.append(total)
            step.append(own_step)
        across = jnp.transpose(
            jnp.concatenate(cumul + [jnp.zeros((LINE - PAIR_HEADS, LINE), F32)], 0)
        )
        scores = dot(c_out.astype(BF16), b_in, (1, 1))
        squared = jnp.zeros((LINE, LINE), F32)
        for side in range(2):
            at = slice(OWN * side, OWN * (side + 1))
            values = mixed[own, at]
            left, right, tail_left, tail_right = ([], [], [], [])
            for near in range(OWN_HEADS):
                head = OWN_HEADS * side + near
                column_of = across[:, head : head + 1]
                decayed = jnp.exp(jnp.where(causal, column_of - cumul[head], -1e30))
                left.append((decayed * (scores * step[head])).astype(BF16))
                right.append(jnp.where(head_of == near, values, 0.0).astype(BF16))
                tail_left.append((c_out * jnp.exp(column_of)).astype(BF16))
                tail_right.append(jnp.where(head_of == near, states[strand][:, at], 0.0).astype(BF16))
            ssd = dot(
                jnp.concatenate(left + tail_left, 1), jnp.concatenate(right + tail_right, 0), (1, 0)
            )
            gated = (ssd + values * rows[5:6, at]) * gate[own, at]
            out[own, at] = gated * rows[4:5, at]
            squared = squared + gated[:, :LINE] * gated[:, :LINE] + gated[:, LINE:] * gated[:, LINE:]
        squares.append(jnp.sum(jnp.transpose(squared), axis=0, keepdims=True))
    mine = jnp.concatenate(squares, 0)
    for peer in range(GROUP):
        send[peer] = mine


def project_kernel(squares, gated, w_own, w_other, out):
    total = squares[0]
    for peer in range(1, GROUP):
        total = total + squares[peer]
    scale = lax.rsqrt(total / (HEADS * HEAD_DIM) + EPSILON)
    combined = jnp.zeros((LINE, PAIR), F32)
    for strand in range(2):
        down = jnp.transpose(jnp.broadcast_to(scale[strand : strand + 1], (LINE, LINE)))
        block = gated[LINE * strand : LINE * (strand + 1), :]
        normed = block * jnp.concatenate([down] * (PAIR // LINE), 1)
        combined = combined + normed.astype(BF16).astype(F32)
    combined = combined.astype(BF16)
    mixed = dot(combined[:, :OWN], w_own[...], (1, 0)) + dot(combined[:, OWN:], w_other[...], (1, 0))
    out[...] = mixed.astype(BF16).reshape(out.shape)


def sum_kernel(received, out):
    total = received[0].astype(F32)
    for peer in range(1, GROUP):
        total = total + received[peer].astype(F32)
    out[...] = total.astype(BF16)


def call(kernel, outs, kinds, work, limit, scratch=()):
    return pl.pallas_call(
        kernel,
        out_shape=outs,
        in_specs=[pl.BlockSpec(memory_space=kind) for kind in kinds],
        out_specs=jax.tree.map(lambda _: pl.BlockSpec(memory_space=VMEM), outs),
        scratch_shapes=scratch,
        compiler_params=pltpu.CompilerParams(vmem_limit_bytes=limit * 2**20),
        cost_estimate=pl.CostEstimate(flops=work * 10**9, bytes_accessed=work * 2**20, transcendentals=0),
    )


def make_send(*args):
    return call(send_kernel, jax.ShapeDtypeStruct((CHIPS, 16, 128), F32), [VMEM] * 4, 1, 16)(*args)


def make_tables(*args):
    return call(tables_kernel, jax.ShapeDtypeStruct((32, OWN), F32), [VMEM] * 5, 1, 16)(*args)


def make_prepare(mine, other, conv_bc, complement):
    grams = gram_table()
    return call(
        prepare_kernel,
        (
            jax.ShapeDtypeStruct((64, 2 * PAIR + 1024), BF16),
            jax.ShapeDtypeStruct((16, PAIR), F32),
            jax.ShapeDtypeStruct((16, LINE), F32),
        ),
        [VMEM] * 4 + [SMEM],
        1,
        16,
    )(mine, other, conv_bc, jnp.asarray(grams, BF16), complement)


def make_scan(received, prepared):
    return call(
        scan_kernel,
        (
            jax.ShapeDtypeStruct((2 * LINE, PAIR), F32),
            jax.ShapeDtypeStruct((GROUP, 2, LINE), F32),
        ),
        [VMEM] * 3 + [SMEM],
        7,
        24,
        [
            pltpu.VMEM((LINES, 128), F32),
            pltpu.VMEM((CONV, LINES, 128), F32),
            pltpu.VMEM((CONV, LINES, 128), F32),
        ],
    )(received, *prepared)


def make_project(squares, gated, w_own, w_other):
    return call(
        project_kernel, jax.ShapeDtypeStruct((GROUP, PIECE, w_own.shape[1]), BF16), [VMEM] * 4, 1, 16
    )(squares, gated, w_own, w_other)


def make_sum(received):
    return call(sum_kernel, jax.ShapeDtypeStruct(received.shape[1:], BF16), [VMEM], 1, 16)(received)


def device(seq, chan):
    return seq * CHAN + chan


def mixed_groups():
    side = range(SIDE)
    return [
        [
            device(2 * (SIDE * y + high) + core, (y + right) % SIDE * SIDE + (high + up) % SIDE)
            for y in side
            for high in side
        ]
        for core in range(2)
        for right in side
        for up in side
    ]


def row_groups():
    return [list(range(GROUP)), list(range(GROUP, CHAN))]


def with_partner(value):
    pairs = [(x * SIDE + z, (SIDE - 1 - x) * SIDE + z) for x in range(SIDE) for z in range(SIDE)]
    return lax.ppermute(value, "chan", pairs)


def exchange(value, axes, groups=None):
    return lax.all_to_all(value, axes, 0, 0, tiled=True, axis_index_groups=groups)


def per_device(
    tokens, complement, embed, w_x, w_z, w_bc, w_dt, dt_bias, decay_rate, d_skip, conv_x, conv_bc,
    norm_gain, w_out,
):
    own = tokens.reshape(2, 128)
    sibling = lax.ppermute(own, "seq", [(source, source ^ 1) for source in range(SEQ)])
    send = make_send(own, sibling, embed, w_bc)
    send, embed, conv_x, norm_gain, d_skip, dt_bias, decay_rate = lax.optimization_barrier(
        (send, embed, conv_x, norm_gain, d_skip, dt_bias, decay_rate)
    )
    received = exchange(send, ("seq", "chan"), mixed_groups())
    by_head = jnp.pad(jnp.stack([dt_bias, decay_rate]), ((0, 0), (0, OWN - OWN_HEADS)))
    by_channel = jnp.stack([norm_gain, jnp.repeat(d_skip, HEAD_DIM)])
    params = jnp.concatenate([conv_x.astype(F32), by_channel, by_head], 0)
    tables = make_tables(embed, w_x, w_z, w_dt.T, params)
    other, w_own = lax.optimization_barrier((with_partner(tables), w_out))
    w_other = with_partner(w_own)
    prepared = make_prepare(tables, other, conv_bc, complement)
    gated, squares = make_scan(received, prepared)
    partial = make_project(exchange(squares, "chan", row_groups()), gated, w_own, w_other)
    return make_sum(exchange(partial, "chan", row_groups()))


def solution(mesh):
    placed = (
        P("seq"),
        P(),
        P(),
        P(None, "chan"),
        P(None, "chan"),
        P("chan", None),
        P(None, "chan"),
        P("chan"),
        P("chan"),
        P("chan"),
        P(None, "chan"),
        P(),
        P("chan"),
        P("chan", None),
    )
    return jax.shard_map(
        per_device, mesh=mesh, in_specs=placed, out_specs=P(("seq", "chan"), None), check_vma=False
    )
```

```python
import jax
import jax.numpy as jnp
import numpy as np
from jax import lax
from jax.experimental import pallas as pl
from jax.experimental.pallas import tpu as pltpu
from jax.sharding import PartitionSpec as P

HEADS = 64
HEAD_DIM = 64
STATE = 128
CONV = 4
VOCAB = 5
ROWS = 256
OWN_HEADS = 4
OWN = OWN_HEADS * HEAD_DIM
SEQ = 32
CHAN = 16
CHIPS = SEQ // 2
LENGTH = SEQ * ROWS
LINES = LENGTH // 128
SIDE = 4
PAIR_HEADS = 2 * OWN_HEADS
PAIR = 2 * OWN
GROUP = CHAN // 2
LINE = 128
PIECE = LINE // GROUP
EPSILON = 1e-05
NONE = VOCAB
VMEM = pltpu.VMEM
SMEM = pltpu.SMEM
F32 = jnp.float32
BF16 = jnp.bfloat16


def gram_table():
    table = np.zeros((64, 1024), np.float32)
    for older in range(31):
        for newer in range(30):
            pair = lambda code: (5, 5) if code == 30 else (code // 5, code % 5)
            for tap, symbol in enumerate(pair(older) + pair(newer)):
                if symbol < VOCAB:
                    table[tap * 8 + symbol, older * 32 + newer] = 1
                    table[32 + tap * 8 + symbol, older * 32 + newer] = 1
    return table


def place():
    return lax.axis_index("seq"), lax.axis_index("chan")


def iota(shape, axis):
    return lax.broadcasted_iota(jnp.int32, shape, axis)


def fiota(shape, axis):
    return iota(shape, axis).astype(F32)


def dot(a, b, contract):
    return lax.dot_general(a, b, ((contract[:1], contract[1:]), ((), ())), preferred_element_type=F32)


def silu(x):
    return x / (1.0 + jnp.exp(-x))


def send_kernel(tokens, sibling, embed, w_bc, send):
    seq, chan = place()
    part = embed[:, pl.ds(pl.multiple_of(chan * 128, 128), 128)]
    bc = dot(part, w_bc[...], (1, 0))
    mine = tokens[...].astype(F32)
    other = sibling[...].astype(F32)
    first = lax.rem(seq, 2) == 0
    send[0, 0:VOCAB, :] = bc[:, :STATE]
    send[0, 5:7, :] = jnp.where(first, mine, other)
    send[0, 7:8, :] = jnp.zeros((1, 128), F32)
    send[0, 8 : 8 + VOCAB, :] = bc[:, STATE:]
    send[0, 13:15, :] = jnp.where(first, other, mine)
    send[0, 15:16, :] = jnp.zeros((1, 128), F32)
    block = send[0]
    for peer in range(1, CHIPS):
        send[peer] = block


def tables_kernel(embed, w_x, w_z, w_dt, params, tables):
    emb = embed[...]
    x_tab = dot(emb, w_x[...], (1, 0)).astype(BF16).astype(F32)
    z_tab = dot(emb, w_z[...], (1, 0)).astype(BF16).astype(F32)
    tables[...] = jnp.zeros(tables.shape, F32)
    tables[0:VOCAB, :] = x_tab
    tables[8 : 8 + VOCAB, :] = silu(z_tab)
    tables[16:24, :] = params[...]
    raw = dot(emb, w_dt[...], (1, 1)) + params[6:7, 0:OWN_HEADS]
    step = jnp.maximum(raw, 0.0) + jnp.log1p(jnp.exp(-jnp.abs(raw)))
    tables[24 : 24 + VOCAB, 0:OWN_HEADS] = step
    tables[24 : 24 + VOCAB, LINE : LINE + OWN_HEADS] = step * params[7:8, 0:OWN_HEADS]


def prepare_kernel(mine, other, conv_bc, grams_in, complement, tables, rows, steps):
    for side, given in enumerate((mine, other)):
        at = slice(OWN * side, OWN * (side + 1))
        x_taps = halves(taps_table(given[16:20, :], given[0:8, :]))
        tables[:, at] = x_taps
        gates = jnp.concatenate([jnp.zeros((24, OWN), F32), given[8:16, :]], 0)
        tables[:, PAIR + OWN * side : PAIR + OWN * (side + 1)] = halves(gates)
        rows[0:8, at] = given[16:24, :]
    tables[:, 2 * PAIR :] = grams_in[...]
    rows[8:12, 0 : 2 * STATE] = conv_bc[...].astype(F32)
    rows[8:12, 2 * STATE :] = jnp.zeros((4, PAIR - 2 * STATE), F32)
    rows[12:16, :] = jnp.zeros((4, PAIR), F32)
    for part in range(2):
        at = slice(LINE * part, LINE * (part + 1))
        steps[8 * part : 8 * part + 8, :] = given_steps(mine, at) + pltpu.roll(given_steps(other, at), OWN_HEADS, 1)
    lane = iota((1, LINE), 1)
    flips = jnp.zeros((1, LINE), F32)
    for symbol in range(VOCAB):
        flips = jnp.where(lane == symbol, complement[symbol].astype(F32), flips)
    steps[15:16, :] = flips


def given_steps(given, at):
    return given[24:32, at]


def before(x, steps):
    lane, line = (iota(x.shape, 1), iota(x.shape, 0))
    turned = pltpu.roll(x, steps, 1)
    over = jnp.where(line == 0, float(NONE), pltpu.roll(turned, 1, 0))
    return jnp.where(lane < steps, over, turned)


def after(x, steps):
    lane, line = (iota(x.shape, 1), iota(x.shape, 0))
    turned = pltpu.roll(x, 128 - steps, 1)
    over = jnp.where(line == LINES - 1, float(NONE), pltpu.roll(turned, LINES - 1, 0))
    return jnp.where(lane >= 128 - steps, over, turned)


def hot(symbols, count):
    return jnp.where(fiota((count, symbols.shape[1]), 0) == symbols, 1.0, 0.0)


def taps_table(taps, table):
    return jnp.concatenate([taps[k : k + 1, :] * table for k in range(CONV)], 0)


def halves(x):
    high = x.astype(BF16)
    low = (x - high.astype(F32)).astype(BF16)
    return jnp.concatenate([high.astype(F32), low.astype(F32)], 0).astype(BF16)


def scan_kernel(
    received, tables, rows, step_at, out, send,
    tok_ref, fwd_ref, back_ref,
):
    seq, chan = place()
    own_line = 2 * seq + chan // GROUP
    for chip in range(CHIPS):
        tok_ref[4 * chip : 4 * chip + 2, :] = received[chip, 5:7, :]
        tok_ref[4 * chip + 2 : 4 * chip + 4, :] = received[chip, 13:15, :]
    bc_sum = received[0]
    for chip in range(1, CHIPS):
        bc_sum = bc_sum + received[chip]
    bc_sum = jnp.where(lax.rem(iota((16, 128), 0), 8) < VOCAB, bc_sum, 0.0)
    bc_sum = bc_sum.astype(BF16).astype(F32)
    bc_tab = jnp.concatenate([bc_sum[0:8], bc_sum[8:16]], 1)
    bc_taps = halves(taps_table(rows[8:12, 0 : 2 * STATE], bc_tab))
    conv_tab = jnp.concatenate([tables[:, :PAIR], bc_taps, tables[:, PAIR : 2 * PAIR]], 1)

    tok = tok_ref[...]
    flipped = jnp.zeros(tok.shape, F32)
    for symbol in range(VOCAB):
        flipped = jnp.where(tok == float(symbol), step_at[15, symbol], flipped)
    fwd = [before(tok, 3), before(tok, 2), before(tok, 1), tok]
    back = [after(flipped, 3), after(flipped, 2), after(flipped, 1), flipped]
    for k in range(CONV):
        fwd_ref[k] = fwd[k]
        back_ref[k] = back[k]

    line = iota((LINES, 128), 0)
    ahead = line < own_line
    inside = line != own_line
    gram = [jnp.where(ahead, f, b) for f, b in zip(fwd, back)]
    older = gram[0] * 5.0 + gram[1] + jnp.where(ahead, 0.0, 32.0)
    newer = gram[2] * 5.0 + gram[3]
    newest = [jnp.logical_and(gram[3] == float(symbol), inside) for symbol in range(VOCAB)]
    marks = jnp.concatenate([jnp.where(hit, 1.0, 0.0) for hit in newest], 0).astype(BF16)
    row, column = (iota((128, 128), 0), iota((128, 128), 1))
    within = jnp.concatenate(
        [
            jnp.where(row > column, 1.0, 0.0),
            jnp.where(row < column, 1.0, 0.0),
            jnp.ones((128, 128), F32),
        ],
        1,
    ).astype(BF16)
    counts = dot(marks, within, (1, 0))
    parts = [counts[LINES * symbol : LINES * (symbol + 1)] for symbol in range(VOCAB)]
    totals = jnp.concatenate([part[:, 256:384] for part in parts], 1).astype(BF16)
    to, of = (iota((LINES, LINES), 0), iota((LINES, LINES), 1))
    between = jnp.logical_or(
        jnp.logical_and(to < of, of < own_line), jnp.logical_and(of > own_line, of < to)
    )
    lines_between = dot(jnp.where(between, 1.0, 0.0).astype(BF16), totals, (1, 0))
    passed = [
        jnp.where(ahead, part[:, 0:128], part[:, 128:256]) + lines_between[:, 128 * k : 128 * k + 128]
        for k, part in enumerate(parts)
    ]
    weights = []
    for head in range(PAIR_HEADS):
        lost = jnp.zeros((LINES, 128), F32)
        own_step = jnp.zeros((LINES, 128), F32)
        for symbol in range(VOCAB):
            lost = lost + step_at[8 + symbol, head] * passed[symbol]
            own_step = jnp.where(newest[symbol], step_at[symbol, head], own_step)
        weights.append(own_step * jnp.exp(-lost))

    older_down = jnp.transpose(jnp.concatenate([older, older], 0))
    lanes = fiota((128, 64), 1)
    sums = jnp.zeros((32 * PAIR_HEADS, 64), F32)
    for first in range(0, LINES, 2):
        left, right = ([], [])
        for at in (first, first + 1):
            left.append(jnp.where(lanes == older_down[:, at : at + 1], 1.0, 0.0))
            hits = fiota((32, 128), 0) == newer[at : at + 1]
            right.append(
                jnp.concatenate([jnp.where(hits, w[at : at + 1], 0.0) for w in weights], 0)
            )
        sums = sums + dot(
            jnp.concatenate(right, 1).astype(BF16), jnp.concatenate(left, 0).astype(BF16), (1, 0)
        )
    sums = jnp.transpose(jnp.concatenate([sums, sums], 1))[0:64]

    gram_b = silu(dot(bc_taps[:, :STATE], tables[:, 2 * PAIR :], (0, 0))).astype(BF16)
    wide_code = (32, 32 * PAIR_HEADS)
    same = jnp.where(lax.rem(iota(wide_code, 1), 32) == iota(wide_code, 0), 1.0, 0.0)
    gram_values = silu(dot(tables[:, 2 * PAIR :], tables[:, :PAIR], (0, 0))).astype(BF16)
    shape = (32 * PAIR_HEADS, PAIR)
    spread = jnp.where(iota(shape, 0) // 32 == iota(shape, 1) // HEAD_DIM, 1.0, 0.0).astype(BF16)
    states = []
    for strand in range(2):
        placed = jnp.concatenate(
            [sums[32 * strand + code : 32 * strand + code + 1] * same for code in range(32)], 0
        )
        wide = dot(placed.astype(BF16), spread, (1, 0))
        states.append(dot(gram_b, wide.astype(BF16) * gram_values, (1, 0)))

    hots = [
        jnp.concatenate([hot(ref[tap, pl.ds(own_line, 1), :], 8) for tap in range(CONV)], 0)
        for ref in (fwd_ref, back_ref)
    ]
    hots = jnp.concatenate(hots, 1)
    mixed = dot(jnp.concatenate([hots, hots], 0).astype(BF16), conv_tab, (0, 0))
    gate = mixed[:, PAIR + 2 * STATE :]
    mixed = silu(mixed[:, : PAIR + 2 * STATE])
    head_of = iota((1, OWN), 1) // HEAD_DIM
    row, column = (iota((LINE, LINE), 0), iota((LINE, LINE), 1))
    squares = []
    for strand in range(2):
        own = slice(LINE * strand, LINE * (strand + 1))
        b_in = mixed[own, PAIR : PAIR + STATE].astype(BF16)
        c_out = mixed[own, PAIR + STATE :]
        causal = row >= column if strand == 0 else row <= column
        order = row <= column if strand == 0 else row >= column
        symbols = hots[24:32, own]
        seen = dot(symbols.astype(BF16), jnp.where(order, 1.0, 0.0).astype(BF16), (1, 0))
        cumul, step = ([], [])
        for head in range(PAIR_HEADS):
            total = jnp.zeros((1, LINE), F32)
            own_step = jnp.zeros((1, LINE), F32)
            for symbol in range(VOCAB):
                total = total - step_at[8 + symbol, head] * seen[symbol : symbol + 1]
                own_step = own_step + step_at[symbol, head] * symbols[symbol : symbol + 1]
            cumul.append(total)
            step.append(own_step)
        across = jnp.transpose(
            jnp.concatenate(cumul + [jnp.zeros((LINE - PAIR_HEADS, LINE), F32)], 0)
        )
        scores = dot(c_out.astype(BF16), b_in, (1, 1))
        squared = jnp.zeros((LINE, LINE), F32)
        for side in range(2):
            at = slice(OWN * side, OWN * (side + 1))
            values = mixed[own, at]
            left, right, tail_left, tail_right = ([], [], [], [])
            for near in range(OWN_HEADS):
                head = OWN_HEADS * side + near
                column_of = across[:, head : head + 1]
                decayed = jnp.exp(jnp.where(causal, column_of - cumul[head], -1e30))
                left.append((decayed * (scores * step[head])).astype(BF16))
                right.append(jnp.where(head_of == near, values, 0.0).astype(BF16))
                tail_left.append((c_out * jnp.exp(column_of)).astype(BF16))
                tail_right.append(jnp.where(head_of == near, states[strand][:, at], 0.0).astype(BF16))
            ssd = dot(
                jnp.concatenate(left + tail_left, 1), jnp.concatenate(right + tail_right, 0), (1, 0)
            )
            gated = (ssd + values * rows[5:6, at]) * gate[own, at]
            out[own, at] = gated * rows[4:5, at]
            squared = squared + gated[:, :LINE] * gated[:, :LINE] + gated[:, LINE:] * gated[:, LINE:]
        squares.append(jnp.sum(jnp.transpose(squared), axis=0, keepdims=True))
    mine = jnp.concatenate(squares, 0)
    for peer in range(GROUP):
        send[peer] = mine


def project_kernel(squares, gated, w_own, w_near, w_far, out):
    seq, _ = place()
    first = lax.rem(seq, 2) == 0
    total = squares[0]
    for peer in range(1, GROUP):
        total = total + squares[peer]
    scale = lax.rsqrt(total / (HEADS * HEAD_DIM) + EPSILON)
    combined = jnp.zeros((LINE, PAIR), F32)
    for strand in range(2):
        down = jnp.transpose(jnp.broadcast_to(scale[strand : strand + 1], (LINE, LINE)))
        block = gated[LINE * strand : LINE * (strand + 1), :]
        normed = block * jnp.concatenate([down] * (PAIR // LINE), 1)
        combined = combined + normed.astype(BF16).astype(F32)
    top, end = (combined[:, OWN : OWN + LINE], combined[:, OWN + LINE :])
    near, far = (jnp.where(first, top, end), jnp.where(first, end, top))
    mixed = dot(combined[:, :OWN].astype(BF16), w_own[...], (1, 0))
    mixed = mixed + dot(near.astype(BF16), w_near[...], (1, 0))
    mixed = mixed + dot(far.astype(BF16), w_far[...], (1, 0))
    out[...] = mixed.astype(BF16).reshape(out.shape)


def sum_kernel(received, out):
    total = received[0].astype(F32)
    for peer in range(1, GROUP):
        total = total + received[peer].astype(F32)
    out[...] = total.astype(BF16)


def call(kernel, outs, kinds, work, limit, scratch=()):
    return pl.pallas_call(
        kernel,
        out_shape=outs,
        in_specs=[pl.BlockSpec(memory_space=kind) for kind in kinds],
        out_specs=jax.tree.map(lambda _: pl.BlockSpec(memory_space=VMEM), outs),
        scratch_shapes=scratch,
        compiler_params=pltpu.CompilerParams(vmem_limit_bytes=limit * 2**20),
        cost_estimate=pl.CostEstimate(flops=work * 10**9, bytes_accessed=work * 2**20, transcendentals=0),
    )


def make_send(*args):
    return call(send_kernel, jax.ShapeDtypeStruct((CHIPS, 16, 128), F32), [VMEM] * 4, 1, 16)(*args)


def make_tables(*args):
    return call(tables_kernel, jax.ShapeDtypeStruct((32, OWN), F32), [VMEM] * 5, 1, 16)(*args)


def make_prepare(mine, other, conv_bc, complement):
    grams = gram_table()
    return call(
        prepare_kernel,
        (
            jax.ShapeDtypeStruct((64, 2 * PAIR + 1024), BF16),
            jax.ShapeDtypeStruct((16, PAIR), F32),
            jax.ShapeDtypeStruct((16, LINE), F32),
        ),
        [VMEM] * 4 + [SMEM],
        1,
        16,
    )(mine, other, conv_bc, jnp.asarray(grams, BF16), complement)


def make_scan(received, prepared):
    return call(
        scan_kernel,
        (
            jax.ShapeDtypeStruct((2 * LINE, PAIR), F32),
            jax.ShapeDtypeStruct((GROUP, 2, LINE), F32),
        ),
        [VMEM] * 3 + [SMEM],
        7,
        24,
        [
            pltpu.VMEM((LINES, 128), F32),
            pltpu.VMEM((CONV, LINES, 128), F32),
            pltpu.VMEM((CONV, LINES, 128), F32),
        ],
    )(received, *prepared)


def make_project(squares, gated, *weights):
    shape = (GROUP, PIECE, weights[0].shape[1])
    return call(project_kernel, jax.ShapeDtypeStruct(shape, BF16), [VMEM] * 5, 1, 16)(
        squares, gated, *weights
    )


def make_sum(received):
    return call(sum_kernel, jax.ShapeDtypeStruct(received.shape[1:], BF16), [VMEM], 1, 16)(received)


def device(seq, chan):
    return seq * CHAN + chan


def mixed_groups():
    side = range(SIDE)
    return [
        [
            device(2 * (SIDE * y + high) + core, (y + right) % SIDE * SIDE + (high + up) % SIDE)
            for y in side
            for high in side
        ]
        for core in range(2)
        for right in side
        for up in side
    ]


def row_groups():
    return [list(range(GROUP)), list(range(GROUP, CHAN))]


def with_partner(value):
    pairs = [(x * SIDE + z, (SIDE - 1 - x) * SIDE + z) for x in range(SIDE) for z in range(SIDE)]
    return lax.ppermute(value, "chan", pairs)


def with_sibling(value):
    return lax.ppermute(value, "seq", [(source, source ^ 1) for source in range(SEQ)])


def exchange(value, axes, groups=None):
    return lax.all_to_all(value, axes, 0, 0, tiled=True, axis_index_groups=groups)


def per_device(
    tokens, complement, embed, w_x, w_z, w_bc, w_dt, dt_bias, decay_rate, d_skip, conv_x, conv_bc,
    norm_gain, w_out,
):
    own = tokens.reshape(2, 128)
    send = make_send(own, with_sibling(own), embed, w_bc)
    send, embed, conv_x, norm_gain, d_skip, dt_bias, decay_rate = lax.optimization_barrier(
        (send, embed, conv_x, norm_gain, d_skip, dt_bias, decay_rate)
    )
    received = exchange(send, ("seq", "chan"), mixed_groups())
    by_head = jnp.pad(jnp.stack([dt_bias, decay_rate]), ((0, 0), (0, OWN - OWN_HEADS)))
    by_channel = jnp.stack([norm_gain, jnp.repeat(d_skip, HEAD_DIM)])
    params = jnp.concatenate([conv_x.astype(F32), by_channel, by_head], 0)
    tables = make_tables(embed, w_x, w_z, w_dt.T, params)
    half = lax.dynamic_slice_in_dim(w_out, lax.axis_index("seq") % 2 * LINE, LINE, 0)
    w_near = with_partner(half)
    other, w_near = lax.optimization_barrier((with_partner(tables), w_near))
    w_far = with_sibling(w_near)
    prepared = make_prepare(tables, other, conv_bc, complement)
    gated, squares = make_scan(received, prepared)
    partial = make_project(exchange(squares, "chan", row_groups()), gated, w_out, w_near, w_far)
    return make_sum(exchange(partial, "chan", row_groups()))


def solution(mesh):
    placed = (
        P("seq"),
        P(),
        P(),
        P(None, "chan"),
        P(None, "chan"),
        P("chan", None),
        P(None, "chan"),
        P("chan"),
        P("chan"),
        P("chan"),
        P(None, "chan"),
        P(),
        P("chan"),
        P("chan", None),
    )
    return jax.shard_map(
        per_device, mesh=mesh, in_specs=placed, out_specs=P(("seq", "chan"), None), check_vma=False
    )
```

```python
import jax
import jax.numpy as jnp
import numpy as np
from jax import lax
from jax.experimental import pallas as pl
from jax.experimental.pallas import tpu as pltpu
from jax.sharding import PartitionSpec as P

HEADS = 64
HEAD_DIM = 64
STATE = 128
CONV = 4
VOCAB = 5
ROWS = 256
OWN_HEADS = 4
OWN = OWN_HEADS * HEAD_DIM
SEQ = 32
CHAN = 16
CHIPS = SEQ // 2
LENGTH = SEQ * ROWS
LINES = LENGTH // 128
SIDE = 4
PAIR_HEADS = 2 * OWN_HEADS
PAIR = 2 * OWN
GROUP = CHAN // 2
LINE = 128
PIECE = LINE // GROUP
EPSILON = 1e-05
NONE = VOCAB
VMEM = pltpu.VMEM
SMEM = pltpu.SMEM
F32 = jnp.float32
BF16 = jnp.bfloat16


def gram_table():
    table = np.zeros((64, 1024), np.float32)
    for older in range(31):
        for newer in range(30):
            pair = lambda code: (5, 5) if code == 30 else (code // 5, code % 5)
            for tap, symbol in enumerate(pair(older) + pair(newer)):
                if symbol < VOCAB:
                    table[tap * 8 + symbol, newer * 32 + older] = 1
                    table[32 + tap * 8 + symbol, newer * 32 + older] = 1
    return table


def place():
    return lax.axis_index("seq"), lax.axis_index("chan")


def iota(shape, axis):
    return lax.broadcasted_iota(jnp.int32, shape, axis)


def fiota(shape, axis):
    return iota(shape, axis).astype(F32)


def dot(a, b, contract):
    return lax.dot_general(a, b, ((contract[:1], contract[1:]), ((), ())), preferred_element_type=F32)


def silu(x):
    return x / (1.0 + jnp.exp(-x))


def send_kernel(tokens, sibling, embed, w_bc, send):
    seq, chan = place()
    part = embed[:, pl.ds(pl.multiple_of(chan * 128, 128), 128)]
    bc = dot(part, w_bc[...], (1, 0))
    mine = tokens[...].astype(F32)
    other = sibling[...].astype(F32)
    first = lax.rem(seq, 2) == 0
    send[0, 0:VOCAB, :] = bc[:, :STATE]
    send[0, 5:7, :] = jnp.where(first, mine, other)
    send[0, 7:8, :] = jnp.zeros((1, 128), F32)
    send[0, 8 : 8 + VOCAB, :] = bc[:, STATE:]
    send[0, 13:15, :] = jnp.where(first, other, mine)
    send[0, 15:16, :] = jnp.zeros((1, 128), F32)
    block = send[0]
    for peer in range(1, CHIPS):
        send[peer] = block


def tables_kernel(embed, w_x, w_z, w_dt, params, tables):
    emb = embed[...]
    x_tab = dot(emb, w_x[...], (1, 0)).astype(BF16).astype(F32)
    z_tab = dot(emb, w_z[...], (1, 0)).astype(BF16).astype(F32)
    tables[...] = jnp.zeros(tables.shape, F32)
    tables[0:VOCAB, :] = x_tab
    tables[8 : 8 + VOCAB, :] = silu(z_tab)
    tables[16:24, :] = params[...]
    raw = dot(emb, w_dt[...], (1, 1)) + params[6:7, 0:OWN_HEADS]
    step = jnp.maximum(raw, 0.0) + jnp.log1p(jnp.exp(-jnp.abs(raw)))
    tables[24 : 24 + VOCAB, 0:OWN_HEADS] = step
    tables[24 : 24 + VOCAB, LINE : LINE + OWN_HEADS] = step * params[7:8, 0:OWN_HEADS]


def prepare_kernel(mine, other, conv_bc, grams_in, complement, tables, rows, steps):
    for side, given in enumerate((mine, other)):
        at = slice(OWN * side, OWN * (side + 1))
        x_taps = halves(taps_table(given[16:20, :], given[0:8, :]))
        tables[:, at] = x_taps
        gates = jnp.concatenate([jnp.zeros((24, OWN), F32), given[8:16, :]], 0)
        tables[:, PAIR + OWN * side : PAIR + OWN * (side + 1)] = halves(gates)
        rows[0:8, at] = given[16:24, :]
    tables[:, 2 * PAIR :] = grams_in[...]
    rows[8:12, 0 : 2 * STATE] = conv_bc[...].astype(F32)
    rows[8:12, 2 * STATE :] = jnp.zeros((4, PAIR - 2 * STATE), F32)
    rows[12:16, :] = jnp.zeros((4, PAIR), F32)
    for part in range(2):
        at = slice(LINE * part, LINE * (part + 1))
        steps[8 * part : 8 * part + 8, :] = given_steps(mine, at) + pltpu.roll(given_steps(other, at), OWN_HEADS, 1)
    lane = iota((1, LINE), 1)
    flips = jnp.zeros((1, LINE), F32)
    for symbol in range(VOCAB):
        flips = jnp.where(lane == symbol, complement[symbol].astype(F32), flips)
    steps[15:16, :] = flips


def given_steps(given, at):
    return given[24:32, at]


def before(x, steps):
    lane, line = (iota(x.shape, 1), iota(x.shape, 0))
    turned = pltpu.roll(x, steps, 1)
    over = jnp.where(line == 0, float(NONE), pltpu.roll(turned, 1, 0))
    return jnp.where(lane < steps, over, turned)


def after(x, steps):
    lane, line = (iota(x.shape, 1), iota(x.shape, 0))
    turned = pltpu.roll(x, 128 - steps, 1)
    over = jnp.where(line == LINES - 1, float(NONE), pltpu.roll(turned, LINES - 1, 0))
    return jnp.where(lane >= 128 - steps, over, turned)


def hot(symbols, count):
    return jnp.where(fiota((count, symbols.shape[1]), 0) == symbols, 1.0, 0.0)


def taps_table(taps, table):
    return jnp.concatenate([taps[k : k + 1, :] * table for k in range(CONV)], 0)


def halves(x):
    high = x.astype(BF16)
    low = (x - high.astype(F32)).astype(BF16)
    return jnp.concatenate([high.astype(F32), low.astype(F32)], 0).astype(BF16)


def scan_kernel(
    received, tables, rows, step_at, out, send,
    tok_ref, fwd_ref, back_ref, sums_ref,
):
    seq, chan = place()
    own_line = 2 * seq + chan // GROUP
    for chip in range(CHIPS):
        tok_ref[4 * chip : 4 * chip + 2, :] = received[chip, 5:7, :]
        tok_ref[4 * chip + 2 : 4 * chip + 4, :] = received[chip, 13:15, :]
    bc_sum = received[0]
    for chip in range(1, CHIPS):
        bc_sum = bc_sum + received[chip]
    bc_sum = jnp.where(lax.rem(iota((16, 128), 0), 8) < VOCAB, bc_sum, 0.0)
    bc_sum = bc_sum.astype(BF16).astype(F32)
    bc_tab = jnp.concatenate([bc_sum[0:8], bc_sum[8:16]], 1)
    bc_taps = halves(taps_table(rows[8:12, 0 : 2 * STATE], bc_tab))
    conv_tab = jnp.concatenate([tables[:, :PAIR], bc_taps, tables[:, PAIR : 2 * PAIR]], 1)

    tok = tok_ref[...]
    flipped = jnp.zeros(tok.shape, F32)
    for symbol in range(VOCAB):
        flipped = jnp.where(tok == float(symbol), step_at[15, symbol], flipped)
    fwd = [before(tok, 3), before(tok, 2), before(tok, 1), tok]
    back = [after(flipped, 3), after(flipped, 2), after(flipped, 1), flipped]
    for k in range(CONV):
        fwd_ref[k] = fwd[k]
        back_ref[k] = back[k]

    line = iota((LINES, 128), 0)
    ahead = line < own_line
    inside = line != own_line
    gram = [jnp.where(ahead, f, b) for f, b in zip(fwd, back)]
    older = gram[0] * 5.0 + gram[1] + jnp.where(ahead, 0.0, 32.0)
    newer = gram[2] * 5.0 + gram[3]
    newest = [jnp.logical_and(gram[3] == float(symbol), inside) for symbol in range(VOCAB)]
    marks = jnp.concatenate([jnp.where(hit, 1.0, 0.0) for hit in newest], 0).astype(BF16)
    row, column = (iota((128, 128), 0), iota((128, 128), 1))
    within = jnp.concatenate(
        [
            jnp.where(row > column, 1.0, 0.0),
            jnp.where(row < column, 1.0, 0.0),
            jnp.ones((128, 128), F32),
        ],
        1,
    ).astype(BF16)
    counts = dot(marks, within, (1, 0))
    parts = [counts[LINES * symbol : LINES * (symbol + 1)] for symbol in range(VOCAB)]
    totals = jnp.concatenate([part[:, 256:384] for part in parts], 1).astype(BF16)
    to, of = (iota((LINES, LINES), 0), iota((LINES, LINES), 1))
    between = jnp.logical_or(
        jnp.logical_and(to < of, of < own_line), jnp.logical_and(of > own_line, of < to)
    )
    lines_between = dot(jnp.where(between, 1.0, 0.0).astype(BF16), totals, (1, 0))
    passed = [
        jnp.where(ahead, part[:, 0:128], part[:, 128:256]) + lines_between[:, 128 * k : 128 * k + 128]
        for k, part in enumerate(parts)
    ]
    weights = []
    for head in range(PAIR_HEADS):
        lost = jnp.zeros((LINES, 128), F32)
        own_step = jnp.zeros((LINES, 128), F32)
        for symbol in range(VOCAB):
            lost = lost + step_at[8 + symbol, head] * passed[symbol]
            own_step = jnp.where(newest[symbol], step_at[symbol, head], own_step)
        weights.append(own_step * jnp.exp(-lost))

    older_down = jnp.transpose(jnp.concatenate([older, older], 0))
    lanes = fiota((128, 64), 1)
    sums = jnp.zeros((32 * PAIR_HEADS, 64), F32)
    for first in range(0, LINES, 2):
        left, right = ([], [])
        for at in (first, first + 1):
            left.append(jnp.where(lanes == older_down[:, at : at + 1], 1.0, 0.0))
            hits = fiota((32, 128), 0) == newer[at : at + 1]
            right.append(
                jnp.concatenate([jnp.where(hits, w[at : at + 1], 0.0) for w in weights], 0)
            )
        sums = sums + dot(
            jnp.concatenate(right, 1).astype(BF16), jnp.concatenate(left, 0).astype(BF16), (1, 0)
        )
    sums_ref[...] = jnp.concatenate([sums, sums], 1)

    gram_values = silu(dot(tables[:, :PAIR], tables[:, 2 * PAIR :], (0, 0))).astype(BF16)
    gram_b = silu(dot(bc_taps[:, :STATE], tables[:, 2 * PAIR :], (0, 0))).astype(BF16)
    by_newer = [sums_ref[pl.ds(newer, PAIR_HEADS, stride=32), :] for newer in range(32)]
    lane = iota((PAIR_HEADS, 128), 1)
    states = []
    for strand in range(2):
        lines = []
        for first in range(0, 32, 4):
            whole = jnp.zeros((PAIR_HEADS, 128), F32)
            for k in range(4):
                turned = pltpu.roll(by_newer[first + k], (32 * (k - strand)) % 128, 1)
                whole = jnp.where(lane // 32 == k, turned, whole)
            lines.append(whole)
        weight_of = jnp.concatenate(lines, 1)
        weighted = [
            gram_values[HEAD_DIM * head : HEAD_DIM * (head + 1)]
            * jnp.broadcast_to(weight_of[head : head + 1], (HEAD_DIM, 1024)).astype(BF16)
            for head in range(PAIR_HEADS)
        ]
        states.append(jnp.transpose(dot(jnp.concatenate(weighted, 0), gram_b, (1, 1))))

    hots = [
        jnp.concatenate([hot(ref[tap, pl.ds(own_line, 1), :], 8) for tap in range(CONV)], 0)
        for ref in (fwd_ref, back_ref)
    ]
    hots = jnp.concatenate(hots, 1)
    mixed = dot(jnp.concatenate([hots, hots], 0).astype(BF16), conv_tab, (0, 0))
    gate = mixed[:, PAIR + 2 * STATE :]
    mixed = silu(mixed[:, : PAIR + 2 * STATE])
    head_of = iota((1, OWN), 1) // HEAD_DIM
    row, column = (iota((LINE, LINE), 0), iota((LINE, LINE), 1))
    squares = []
    for strand in range(2):
        own = slice(LINE * strand, LINE * (strand + 1))
        b_in = mixed[own, PAIR : PAIR + STATE].astype(BF16)
        c_out = mixed[own, PAIR + STATE :]
        causal = row >= column if strand == 0 else row <= column
        order = row <= column if strand == 0 else row >= column
        symbols = hots[24:32, own]
        seen = dot(symbols.astype(BF16), jnp.where(order, 1.0, 0.0).astype(BF16), (1, 0))
        cumul, step = ([], [])
        for head in range(PAIR_HEADS):
            total = jnp.zeros((1, LINE), F32)
            own_step = jnp.zeros((1, LINE), F32)
            for symbol in range(VOCAB):
                total = total - step_at[8 + symbol, head] * seen[symbol : symbol + 1]
                own_step = own_step + step_at[symbol, head] * symbols[symbol : symbol + 1]
            cumul.append(total)
            step.append(own_step)
        across = jnp.transpose(
            jnp.concatenate(cumul + [jnp.zeros((LINE - PAIR_HEADS, LINE), F32)], 0)
        )
        scores = dot(c_out.astype(BF16), b_in, (1, 1))
        squared = jnp.zeros((LINE, LINE), F32)
        for side in range(2):
            at = slice(OWN * side, OWN * (side + 1))
            values = mixed[own, at]
            left, right, tail_left, tail_right = ([], [], [], [])
            for near in range(OWN_HEADS):
                head = OWN_HEADS * side + near
                column_of = across[:, head : head + 1]
                decayed = jnp.exp(jnp.where(causal, column_of - cumul[head], -1e30))
                left.append((decayed * (scores * step[head])).astype(BF16))
                right.append(jnp.where(head_of == near, values, 0.0).astype(BF16))
                tail_left.append((c_out * jnp.exp(column_of)).astype(BF16))
                tail_right.append(jnp.where(head_of == near, states[strand][:, at], 0.0).astype(BF16))
            ssd = dot(
                jnp.concatenate(left + tail_left, 1), jnp.concatenate(right + tail_right, 0), (1, 0)
            )
            gated = (ssd + values * rows[5:6, at]) * gate[own, at]
            out[own, at] = gated * rows[4:5, at]
            squared = squared + gated[:, :LINE] * gated[:, :LINE] + gated[:, LINE:] * gated[:, LINE:]
        squares.append(jnp.sum(jnp.transpose(squared), axis=0, keepdims=True))
    mine = jnp.concatenate(squares, 0)
    for peer in range(GROUP):
        send[peer] = mine


def project_kernel(squares, gated, w_own, w_other, out):
    total = squares[0]
    for peer in range(1, GROUP):
        total = total + squares[peer]
    scale = lax.rsqrt(total / (HEADS * HEAD_DIM) + EPSILON)
    combined = jnp.zeros((LINE, PAIR), F32)
    for strand in range(2):
        down = jnp.transpose(jnp.broadcast_to(scale[strand : strand + 1], (LINE, LINE)))
        block = gated[LINE * strand : LINE * (strand + 1), :]
        normed = block * jnp.concatenate([down] * (PAIR // LINE), 1)
        combined = combined + normed.astype(BF16).astype(F32)
    combined = combined.astype(BF16)
    mixed = dot(combined[:, :OWN], w_own[...], (1, 0)) + dot(combined[:, OWN:], w_other[...], (1, 0))
    out[...] = mixed.astype(BF16).reshape(out.shape)


def sum_kernel(received, out):
    total = received[0].astype(F32)
    for peer in range(1, GROUP):
        total = total + received[peer].astype(F32)
    out[...] = total.astype(BF16)


def call(kernel, outs, kinds, work, limit, scratch=()):
    return pl.pallas_call(
        kernel,
        out_shape=outs,
        in_specs=[pl.BlockSpec(memory_space=kind) for kind in kinds],
        out_specs=jax.tree.map(lambda _: pl.BlockSpec(memory_space=VMEM), outs),
        scratch_shapes=scratch,
        compiler_params=pltpu.CompilerParams(vmem_limit_bytes=limit * 2**20),
        cost_estimate=pl.CostEstimate(flops=work * 10**9, bytes_accessed=work * 2**20, transcendentals=0),
    )


def make_send(*args):
    return call(send_kernel, jax.ShapeDtypeStruct((CHIPS, 16, 128), F32), [VMEM] * 4, 1, 16)(*args)


def make_tables(*args):
    return call(tables_kernel, jax.ShapeDtypeStruct((32, OWN), F32), [VMEM] * 5, 1, 16)(*args)


def make_prepare(mine, other, conv_bc, complement):
    grams = gram_table()
    return call(
        prepare_kernel,
        (
            jax.ShapeDtypeStruct((64, 2 * PAIR + 1024), BF16),
            jax.ShapeDtypeStruct((16, PAIR), F32),
            jax.ShapeDtypeStruct((16, LINE), F32),
        ),
        [VMEM] * 4 + [SMEM],
        1,
        16,
    )(mine, other, conv_bc, jnp.asarray(grams, BF16), complement)


def make_scan(received, prepared):
    return call(
        scan_kernel,
        (
            jax.ShapeDtypeStruct((2 * LINE, PAIR), F32),
            jax.ShapeDtypeStruct((GROUP, 2, LINE), F32),
        ),
        [VMEM] * 3 + [SMEM],
        7,
        24,
        [
            pltpu.VMEM((LINES, 128), F32),
            pltpu.VMEM((CONV, LINES, 128), F32),
            pltpu.VMEM((CONV, LINES, 128), F32),
            pltpu.VMEM((32 * PAIR_HEADS, 128), F32),
        ],
    )(received, *prepared)


def make_project(squares, gated, *weights):
    shape = (GROUP, PIECE, weights[0].shape[1])
    return call(project_kernel, jax.ShapeDtypeStruct(shape, BF16), [VMEM] * 4, 1, 16)(
        squares, gated, *weights
    )


def make_sum(received):
    return call(sum_kernel, jax.ShapeDtypeStruct(received.shape[1:], BF16), [VMEM], 1, 16)(received)


def device(seq, chan):
    return seq * CHAN + chan


def mixed_groups():
    side = range(SIDE)
    return [
        [
            device(2 * (SIDE * y + high) + core, (y + right) % SIDE * SIDE + (high + up) % SIDE)
            for y in side
            for high in side
        ]
        for core in range(2)
        for right in side
        for up in side
    ]


def row_groups():
    return [list(range(GROUP)), list(range(GROUP, CHAN))]


def with_partner(value):
    pairs = [(x * SIDE + z, (SIDE - 1 - x) * SIDE + z) for x in range(SIDE) for z in range(SIDE)]
    return lax.ppermute(value, "chan", pairs)


def with_sibling(value):
    return lax.ppermute(value, "seq", [(source, source ^ 1) for source in range(SEQ)])


def exchange(value, axes, groups=None):
    return lax.all_to_all(value, axes, 0, 0, tiled=True, axis_index_groups=groups)


def per_device(
    tokens, complement, embed, w_x, w_z, w_bc, w_dt, dt_bias, decay_rate, d_skip, conv_x, conv_bc,
    norm_gain, w_out,
):
    own = tokens.reshape(2, 128)
    send = make_send(own, with_sibling(own), embed, w_bc)
    send, embed, conv_x, norm_gain, d_skip, dt_bias, decay_rate = lax.optimization_barrier(
        (send, embed, conv_x, norm_gain, d_skip, dt_bias, decay_rate)
    )
    received = exchange(send, ("seq", "chan"), mixed_groups())
    by_head = jnp.pad(jnp.stack([dt_bias, decay_rate]), ((0, 0), (0, OWN - OWN_HEADS)))
    by_channel = jnp.stack([norm_gain, jnp.repeat(d_skip, HEAD_DIM)])
    params = jnp.concatenate([conv_x.astype(F32), by_channel, by_head], 0)
    tables = make_tables(embed, w_x, w_z, w_dt.T, params)
    w_other = with_partner(w_out)
    other, w_other = lax.optimization_barrier((with_partner(tables), w_other))
    prepared = make_prepare(tables, other, conv_bc, complement)
    gated, squares = make_scan(received, prepared)
    partial = make_project(exchange(squares, "chan", row_groups()), gated, w_out, w_other)
    return make_sum(exchange(partial, "chan", row_groups()))


def solution(mesh):
    placed = (
        P("seq"),
        P(),
        P(),
        P(None, "chan"),
        P(None, "chan"),
        P("chan", None),
        P(None, "chan"),
        P("chan"),
        P("chan"),
        P("chan"),
        P(None, "chan"),
        P(),
        P("chan"),
        P("chan", None),
    )
    return jax.shard_map(
        per_device, mesh=mesh, in_specs=placed, out_specs=P(("seq", "chan"), None), check_vma=False
    )
```

```python
import jax
import jax.numpy as jnp
import numpy as np
from jax import lax
from jax.experimental import pallas as pl
from jax.experimental.pallas import tpu as pltpu
from jax.sharding import PartitionSpec as P

HEADS = 64
HEAD_DIM = 64
STATE = 128
CONV = 4
VOCAB = 5
ROWS = 256
OWN_HEADS = 4
OWN = OWN_HEADS * HEAD_DIM
SEQ = 32
CHAN = 16
CHIPS = SEQ // 2
LENGTH = SEQ * ROWS
LINES = LENGTH // 128
SIDE = 4
PAIR_HEADS = 2 * OWN_HEADS
PAIR = 2 * OWN
GROUP = CHAN // 2
LINE = 128
PIECE = LINE // GROUP
EPSILON = 1e-05
NONE = VOCAB
VMEM = pltpu.VMEM
SMEM = pltpu.SMEM
F32 = jnp.float32
BF16 = jnp.bfloat16


def gram_table():
    table = np.zeros((64, 1024), np.float32)
    for older in range(31):
        for newer in range(30):
            pair = lambda code: (5, 5) if code == 30 else (code // 5, code % 5)
            for tap, symbol in enumerate(pair(older) + pair(newer)):
                if symbol < VOCAB:
                    table[tap * 8 + symbol, newer * 32 + older] = 1
                    table[32 + tap * 8 + symbol, newer * 32 + older] = 1
    return table


def place():
    return lax.axis_index("seq"), lax.axis_index("chan")


def iota(shape, axis):
    return lax.broadcasted_iota(jnp.int32, shape, axis)


def fiota(shape, axis):
    return iota(shape, axis).astype(F32)


def dot(a, b, contract):
    return lax.dot_general(a, b, ((contract[:1], contract[1:]), ((), ())), preferred_element_type=F32)


def silu(x):
    return x / (1.0 + jnp.exp(-x))


def send_kernel(tokens, sibling, state_map, send):
    seq, _ = place()
    bc = state_map[...]
    mine = tokens[...].astype(F32)
    other = sibling[...].astype(F32)
    first = lax.rem(seq, 2) == 0
    send[0, 0:VOCAB, :] = bc[:, :STATE]
    send[0, 5:7, :] = jnp.where(first, mine, other)
    send[0, 7:8, :] = jnp.zeros((1, 128), F32)
    send[0, 8 : 8 + VOCAB, :] = bc[:, STATE:]
    send[0, 13:15, :] = jnp.where(first, other, mine)
    send[0, 15:16, :] = jnp.zeros((1, 128), F32)
    block = send[0]
    for peer in range(1, CHIPS):
        send[peer] = block


def tables_kernel(embed, w_x, w_z, w_dt, params, tables):
    emb = embed[...]
    x_tab = dot(emb, w_x[...], (1, 0)).astype(BF16).astype(F32)
    z_tab = dot(emb, w_z[...], (1, 0)).astype(BF16).astype(F32)
    tables[...] = jnp.zeros(tables.shape, F32)
    tables[0:VOCAB, :] = x_tab
    tables[8 : 8 + VOCAB, :] = silu(z_tab)
    tables[16:24, :] = params[...]
    raw = dot(emb, w_dt[...], (1, 1)) + params[6:7, 0:OWN_HEADS]
    step = jnp.maximum(raw, 0.0) + jnp.log1p(jnp.exp(-jnp.abs(raw)))
    tables[24 : 24 + VOCAB, 0:OWN_HEADS] = step
    tables[24 : 24 + VOCAB, LINE : LINE + OWN_HEADS] = step * params[7:8, 0:OWN_HEADS]


def prepare_kernel(mine, other, conv_bc, grams_in, complement, tables, rows, steps):
    for side, given in enumerate((mine, other)):
        at = slice(OWN * side, OWN * (side + 1))
        x_taps = halves(taps_table(given[16:20, :], given[0:8, :]))
        tables[:, at] = x_taps
        gates = jnp.concatenate([jnp.zeros((24, OWN), F32), given[8:16, :]], 0)
        tables[:, PAIR + OWN * side : PAIR + OWN * (side + 1)] = halves(gates)
        rows[0:8, at] = given[16:24, :]
    tables[:, 2 * PAIR :] = grams_in[...]
    rows[8:12, 0 : 2 * STATE] = conv_bc[...].astype(F32)
    rows[8:12, 2 * STATE :] = jnp.zeros((4, PAIR - 2 * STATE), F32)
    rows[12:16, :] = jnp.zeros((4, PAIR), F32)
    for part in range(2):
        at = slice(LINE * part, LINE * (part + 1))
        steps[8 * part : 8 * part + 8, :] = given_steps(mine, at) + pltpu.roll(given_steps(other, at), OWN_HEADS, 1)
    lane = iota((1, LINE), 1)
    flips = jnp.zeros((1, LINE), F32)
    for symbol in range(VOCAB):
        flips = jnp.where(lane == symbol, complement[symbol].astype(F32), flips)
    steps[15:16, :] = flips


def given_steps(given, at):
    return given[24:32, at]


def before(x, steps):
    lane, line = (iota(x.shape, 1), iota(x.shape, 0))
    turned = pltpu.roll(x, steps, 1)
    over = jnp.where(line == 0, float(NONE), pltpu.roll(turned, 1, 0))
    return jnp.where(lane < steps, over, turned)


def after(x, steps):
    lane, line = (iota(x.shape, 1), iota(x.shape, 0))
    turned = pltpu.roll(x, 128 - steps, 1)
    over = jnp.where(line == LINES - 1, float(NONE), pltpu.roll(turned, LINES - 1, 0))
    return jnp.where(lane >= 128 - steps, over, turned)


def hot(symbols, count):
    return jnp.where(fiota((count, symbols.shape[1]), 0) == symbols, 1.0, 0.0)


def taps_table(taps, table):
    return jnp.concatenate([taps[k : k + 1, :] * table for k in range(CONV)], 0)


def halves(x):
    high = x.astype(BF16)
    low = (x - high.astype(F32)).astype(BF16)
    return jnp.concatenate([high.astype(F32), low.astype(F32)], 0).astype(BF16)


def scan_kernel(
    received, tables, rows, step_at, out, send,
    tok_ref, fwd_ref, back_ref, sums_ref,
):
    seq, chan = place()
    own_line = 2 * seq + chan // GROUP
    for chip in range(CHIPS):
        tok_ref[4 * chip : 4 * chip + 2, :] = received[chip, 5:7, :]
        tok_ref[4 * chip + 2 : 4 * chip + 4, :] = received[chip, 13:15, :]
    bc_sum = received[0]
    for chip in range(1, CHIPS):
        bc_sum = bc_sum + received[chip]
    bc_sum = jnp.where(lax.rem(iota((16, 128), 0), 8) < VOCAB, bc_sum, 0.0)
    bc_sum = bc_sum.astype(BF16).astype(F32)
    bc_tab = jnp.concatenate([bc_sum[0:8], bc_sum[8:16]], 1)
    bc_taps = halves(taps_table(rows[8:12, 0 : 2 * STATE], bc_tab))
    conv_tab = jnp.concatenate([tables[:, :PAIR], bc_taps, tables[:, PAIR : 2 * PAIR]], 1)

    tok = tok_ref[...]
    flipped = jnp.zeros(tok.shape, F32)
    for symbol in range(VOCAB):
        flipped = jnp.where(tok == float(symbol), step_at[15, symbol], flipped)
    fwd = [before(tok, 3), before(tok, 2), before(tok, 1), tok]
    back = [after(flipped, 3), after(flipped, 2), after(flipped, 1), flipped]
    for k in range(CONV):
        fwd_ref[k] = fwd[k]
        back_ref[k] = back[k]

    line = iota((LINES, 128), 0)
    ahead = line < own_line
    inside = line != own_line
    gram = [jnp.where(ahead, f, b) for f, b in zip(fwd, back)]
    older = gram[0] * 5.0 + gram[1] + jnp.where(ahead, 0.0, 32.0)
    newer = gram[2] * 5.0 + gram[3]
    newest = [jnp.logical_and(gram[3] == float(symbol), inside) for symbol in range(VOCAB)]
    marks = jnp.concatenate([jnp.where(hit, 1.0, 0.0) for hit in newest], 0).astype(BF16)
    row, column = (iota((128, 128), 0), iota((128, 128), 1))
    within = jnp.concatenate(
        [
            jnp.where(row > column, 1.0, 0.0),
            jnp.where(row < column, 1.0, 0.0),
            jnp.ones((128, 128), F32),
        ],
        1,
    ).astype(BF16)
    counts = dot(marks, within, (1, 0))
    parts = [counts[LINES * symbol : LINES * (symbol + 1)] for symbol in range(VOCAB)]
    totals = jnp.concatenate([part[:, 256:384] for part in parts], 1).astype(BF16)
    to, of = (iota((LINES, LINES), 0), iota((LINES, LINES), 1))
    between = jnp.logical_or(
        jnp.logical_and(to < of, of < own_line), jnp.logical_and(of > own_line, of < to)
    )
    lines_between = dot(jnp.where(between, 1.0, 0.0).astype(BF16), totals, (1, 0))
    passed = [
        jnp.where(ahead, part[:, 0:128], part[:, 128:256]) + lines_between[:, 128 * k : 128 * k + 128]
        for k, part in enumerate(parts)
    ]
    weights = []
    for head in range(PAIR_HEADS):
        lost = jnp.zeros((LINES, 128), F32)
        own_step = jnp.zeros((LINES, 128), F32)
        for symbol in range(VOCAB):
            lost = lost + step_at[8 + symbol, head] * passed[symbol]
            own_step = jnp.where(newest[symbol], step_at[symbol, head], own_step)
        weights.append(own_step * jnp.exp(-lost))

    older_down = jnp.transpose(jnp.concatenate([older, older], 0))
    lanes = fiota((128, 64), 1)
    sums = jnp.zeros((32 * PAIR_HEADS, 64), F32)
    for first in range(0, LINES, 2):
        left, right = ([], [])
        for at in (first, first + 1):
            left.append(jnp.where(lanes == older_down[:, at : at + 1], 1.0, 0.0))
            hits = fiota((32, 128), 0) == newer[at : at + 1]
            right.append(
                jnp.concatenate([jnp.where(hits, w[at : at + 1], 0.0) for w in weights], 0)
            )
        sums = sums + dot(
            jnp.concatenate(right, 1).astype(BF16), jnp.concatenate(left, 0).astype(BF16), (1, 0)
        )
    sums_ref[...] = jnp.concatenate([sums, sums], 1)

    gram_values = silu(dot(tables[:, :PAIR], tables[:, 2 * PAIR :], (0, 0))).astype(BF16)
    gram_b = silu(dot(bc_taps[:, :STATE], tables[:, 2 * PAIR :], (0, 0))).astype(BF16)
    by_newer = [sums_ref[pl.ds(newer, PAIR_HEADS, stride=32), :] for newer in range(32)]
    lane = iota((PAIR_HEADS, 128), 1)
    states = []
    for strand in range(2):
        lines = []
        for first in range(0, 32, 4):
            whole = jnp.zeros((PAIR_HEADS, 128), F32)
            for k in range(4):
                turned = pltpu.roll(by_newer[first + k], (32 * (k - strand)) % 128, 1)
                whole = jnp.where(lane // 32 == k, turned, whole)
            lines.append(whole)
        weight_of = jnp.concatenate(lines, 1)
        weighted = [
            gram_values[HEAD_DIM * head : HEAD_DIM * (head + 1)]
            * jnp.broadcast_to(weight_of[head : head + 1], (HEAD_DIM, 1024)).astype(BF16)
            for head in range(PAIR_HEADS)
        ]
        states.append(jnp.transpose(dot(jnp.concatenate(weighted, 0), gram_b, (1, 1))))

    hots = [
        jnp.concatenate([hot(ref[tap, pl.ds(own_line, 1), :], 8) for tap in range(CONV)], 0)
        for ref in (fwd_ref, back_ref)
    ]
    hots = jnp.concatenate(hots, 1)
    mixed = dot(jnp.concatenate([hots, hots], 0).astype(BF16), conv_tab, (0, 0))
    gate = mixed[:, PAIR + 2 * STATE :]
    mixed = silu(mixed[:, : PAIR + 2 * STATE])
    head_of = iota((1, OWN), 1) // HEAD_DIM
    row, column = (iota((LINE, LINE), 0), iota((LINE, LINE), 1))
    squares = []
    for strand in range(2):
        own = slice(LINE * strand, LINE * (strand + 1))
        b_in = mixed[own, PAIR : PAIR + STATE].astype(BF16)
        c_out = mixed[own, PAIR + STATE :]
        causal = row >= column if strand == 0 else row <= column
        order = row <= column if strand == 0 else row >= column
        symbols = hots[24:32, own]
        seen = dot(symbols.astype(BF16), jnp.where(order, 1.0, 0.0).astype(BF16), (1, 0))
        cumul, step = ([], [])
        for head in range(PAIR_HEADS):
            total = jnp.zeros((1, LINE), F32)
            own_step = jnp.zeros((1, LINE), F32)
            for symbol in range(VOCAB):
                total = total - step_at[8 + symbol, head] * seen[symbol : symbol + 1]
                own_step = own_step + step_at[symbol, head] * symbols[symbol : symbol + 1]
            cumul.append(total)
            step.append(own_step)
        across = jnp.transpose(
            jnp.concatenate(cumul + [jnp.zeros((LINE - PAIR_HEADS, LINE), F32)], 0)
        )
        scores = dot(c_out.astype(BF16), b_in, (1, 1))
        squared = jnp.zeros((LINE, LINE), F32)
        for side in range(2):
            at = slice(OWN * side, OWN * (side + 1))
            values = mixed[own, at]
            left, right, tail_left, tail_right = ([], [], [], [])
            for near in range(OWN_HEADS):
                head = OWN_HEADS * side + near
                column_of = across[:, head : head + 1]
                decayed = jnp.exp(jnp.where(causal, column_of - cumul[head], -1e30))
                left.append((decayed * (scores * step[head])).astype(BF16))
                right.append(jnp.where(head_of == near, values, 0.0).astype(BF16))
                tail_left.append((c_out * jnp.exp(column_of)).astype(BF16))
                tail_right.append(jnp.where(head_of == near, states[strand][:, at], 0.0).astype(BF16))
            ssd = dot(
                jnp.concatenate(left + tail_left, 1), jnp.concatenate(right + tail_right, 0), (1, 0)
            )
            gated = (ssd + values * rows[5:6, at]) * gate[own, at]
            out[own, at] = gated * rows[4:5, at]
            squared = squared + gated[:, :LINE] * gated[:, :LINE] + gated[:, LINE:] * gated[:, LINE:]
        squares.append(jnp.sum(jnp.transpose(squared), axis=0, keepdims=True))
    mine = jnp.concatenate(squares, 0)
    for peer in range(GROUP):
        send[peer] = mine


def project_kernel(squares, gated, w_own, w_other, out):
    total = squares[0]
    for peer in range(1, GROUP):
        total = total + squares[peer]
    scale = lax.rsqrt(total / (HEADS * HEAD_DIM) + EPSILON)
    combined = jnp.zeros((LINE, PAIR), F32)
    for strand in range(2):
        down = jnp.transpose(jnp.broadcast_to(scale[strand : strand + 1], (LINE, LINE)))
        block = gated[LINE * strand : LINE * (strand + 1), :]
        normed = block * jnp.concatenate([down] * (PAIR // LINE), 1)
        combined = combined + normed.astype(BF16).astype(F32)
    combined = combined.astype(BF16)
    mixed = dot(combined[:, :OWN], w_own[...], (1, 0)) + dot(combined[:, OWN:], w_other[...], (1, 0))
    out[...] = mixed.astype(BF16).reshape(out.shape)


def sum_kernel(received, out):
    total = received[0].astype(F32)
    for peer in range(1, GROUP):
        total = total + received[peer].astype(F32)
    out[...] = total.astype(BF16)


def call(kernel, outs, kinds, work, limit, scratch=()):
    return pl.pallas_call(
        kernel,
        out_shape=outs,
        in_specs=[pl.BlockSpec(memory_space=kind) for kind in kinds],
        out_specs=jax.tree.map(lambda _: pl.BlockSpec(memory_space=VMEM), outs),
        scratch_shapes=scratch,
        compiler_params=pltpu.CompilerParams(vmem_limit_bytes=limit * 2**20),
        cost_estimate=pl.CostEstimate(flops=work * 10**9, bytes_accessed=work * 2**20, transcendentals=0),
    )


def make_send(*args):
    return call(send_kernel, jax.ShapeDtypeStruct((CHIPS, 16, 128), F32), [VMEM] * 3, 1, 16)(*args)


def make_tables(*args):
    return call(tables_kernel, jax.ShapeDtypeStruct((32, OWN), F32), [VMEM] * 5, 1, 16)(*args)


def make_prepare(mine, other, conv_bc, complement):
    grams = gram_table()
    return call(
        prepare_kernel,
        (
            jax.ShapeDtypeStruct((64, 2 * PAIR + 1024), BF16),
            jax.ShapeDtypeStruct((16, PAIR), F32),
            jax.ShapeDtypeStruct((16, LINE), F32),
        ),
        [VMEM] * 4 + [SMEM],
        1,
        16,
    )(mine, other, conv_bc, jnp.asarray(grams, BF16), complement)


def make_scan(received, prepared):
    return call(
        scan_kernel,
        (
            jax.ShapeDtypeStruct((2 * LINE, PAIR), F32),
            jax.ShapeDtypeStruct((GROUP, 2, LINE), F32),
        ),
        [VMEM] * 3 + [SMEM],
        7,
        24,
        [
            pltpu.VMEM((LINES, 128), F32),
            pltpu.VMEM((CONV, LINES, 128), F32),
            pltpu.VMEM((CONV, LINES, 128), F32),
            pltpu.VMEM((32 * PAIR_HEADS, 128), F32),
        ],
    )(received, *prepared)


def make_project(squares, gated, *weights):
    shape = (GROUP, PIECE, weights[0].shape[1])
    return call(project_kernel, jax.ShapeDtypeStruct(shape, BF16), [VMEM] * 4, 1, 16)(
        squares, gated, *weights
    )


def make_sum(received):
    return call(sum_kernel, jax.ShapeDtypeStruct(received.shape[1:], BF16), [VMEM], 1, 16)(received)


def device(seq, chan):
    return seq * CHAN + chan


def mixed_groups():
    side = range(SIDE)
    return [
        [
            device(2 * (SIDE * y + high) + core, (y + right) % SIDE * SIDE + (high + up) % SIDE)
            for y in side
            for high in side
        ]
        for core in range(2)
        for right in side
        for up in side
    ]


def row_groups():
    return [list(range(GROUP)), list(range(GROUP, CHAN))]


def with_partner(value):
    pairs = [(x * SIDE + z, (SIDE - 1 - x) * SIDE + z) for x in range(SIDE) for z in range(SIDE)]
    return lax.ppermute(value, "chan", pairs)


def with_sibling(value):
    return lax.ppermute(value, "seq", [(source, source ^ 1) for source in range(SEQ)])


def exchange(value, axes, groups=None):
    return lax.all_to_all(value, axes, 0, 0, tiled=True, axis_index_groups=groups)


def per_device(
    tokens, complement, embed, w_x, w_z, w_bc, w_dt, dt_bias, decay_rate, d_skip, conv_x, conv_bc,
    norm_gain, w_out,
):
    own = tokens.reshape(2, 128)
    depth = w_bc.shape[0]
    part = lax.dynamic_slice_in_dim(embed, lax.axis_index("chan") * depth, depth, 1)
    send = make_send(own, with_sibling(own), dot(part, w_bc, (1, 0)))
    send, embed, conv_x, norm_gain, d_skip, dt_bias, decay_rate = lax.optimization_barrier(
        (send, embed, conv_x, norm_gain, d_skip, dt_bias, decay_rate)
    )
    received = exchange(send, ("seq", "chan"), mixed_groups())
    by_head = jnp.pad(jnp.stack([dt_bias, decay_rate]), ((0, 0), (0, OWN - OWN_HEADS)))
    by_channel = jnp.stack([norm_gain, jnp.repeat(d_skip, HEAD_DIM)])
    params = jnp.concatenate([conv_x.astype(F32), by_channel, by_head], 0)
    tables = make_tables(embed, w_x, w_z, w_dt.T, params)
    w_other = with_partner(w_out)
    other, w_other = lax.optimization_barrier((with_partner(tables), w_other))
    prepared = make_prepare(tables, other, conv_bc, complement)
    gated, squares = make_scan(received, prepared)
    partial = make_project(exchange(squares, "chan", row_groups()), gated, w_out, w_other)
    return make_sum(exchange(partial, "chan", row_groups()))


def solution(mesh):
    placed = (
        P("seq"),
        P(),
        P(),
        P(None, "chan"),
        P(None, "chan"),
        P("chan", None),
        P(None, "chan"),
        P("chan"),
        P("chan"),
        P("chan"),
        P(None, "chan"),
        P(),
        P("chan"),
        P("chan", None),
    )
    return jax.shard_map(
        per_device, mesh=mesh, in_specs=placed, out_specs=P(("seq", "chan"), None), check_vma=False
    )
```

```python
import jax
import jax.numpy as jnp
import numpy as np
from jax import lax
from jax.experimental import pallas as pl
from jax.experimental.pallas import tpu as pltpu
from jax.sharding import PartitionSpec as P

HEADS = 64
HEAD_DIM = 64
STATE = 128
CONV = 4
VOCAB = 5
ROWS = 256
OWN_HEADS = 4
OWN = OWN_HEADS * HEAD_DIM
SEQ = 32
CHAN = 16
CHIPS = SEQ // 2
LENGTH = SEQ * ROWS
LINES = LENGTH // 128
SIDE = 4
PAIR_HEADS = 2 * OWN_HEADS
PAIR = 2 * OWN
GROUP = CHAN // 2
LINE = 128
PIECE = LINE // GROUP
EPSILON = 1e-05
NONE = VOCAB
VMEM = pltpu.VMEM
SMEM = pltpu.SMEM
F32 = jnp.float32
BF16 = jnp.bfloat16


def gram_table():
    table = np.zeros((64, 1024), np.float32)
    for older in range(31):
        for newer in range(30):
            pair = lambda code: (5, 5) if code == 30 else (code // 5, code % 5)
            for tap, symbol in enumerate(pair(older) + pair(newer)):
                if symbol < VOCAB:
                    table[tap * 8 + symbol, newer * 32 + older] = 1
                    table[32 + tap * 8 + symbol, newer * 32 + older] = 1
    return table


def place():
    return lax.axis_index("seq"), lax.axis_index("chan")


def iota(shape, axis):
    return lax.broadcasted_iota(jnp.int32, shape, axis)


def fiota(shape, axis):
    return iota(shape, axis).astype(F32)


def dot(a, b, contract):
    return lax.dot_general(a, b, ((contract[:1], contract[1:]), ((), ())), preferred_element_type=F32)


def silu(x):
    return x / (1.0 + jnp.exp(-x))


def send_kernel(tokens, sibling, state_map, send):
    seq, _ = place()
    bc = state_map[...]
    mine = tokens[...].astype(F32)
    other = sibling[...].astype(F32)
    first = lax.rem(seq, 2) == 0
    send[0, 0:VOCAB, :] = bc[:, :STATE]
    send[0, 5:7, :] = jnp.where(first, mine, other)
    send[0, 7:8, :] = jnp.zeros((1, 128), F32)
    send[0, 8 : 8 + VOCAB, :] = bc[:, STATE:]
    send[0, 13:15, :] = jnp.where(first, other, mine)
    send[0, 15:16, :] = jnp.zeros((1, 128), F32)
    block = send[0]
    for peer in range(1, CHIPS):
        send[peer] = block


def tables_kernel(embed, w_x, w_z, w_dt, params, tables):
    emb = embed[...]
    x_tab = dot(emb, w_x[...], (1, 0)).astype(BF16).astype(F32)
    z_tab = dot(emb, w_z[...], (1, 0)).astype(BF16).astype(F32)
    tables[...] = jnp.zeros(tables.shape, F32)
    tables[0:VOCAB, :] = x_tab
    tables[8 : 8 + VOCAB, :] = silu(z_tab)
    tables[16:24, :] = params[...]
    raw = dot(emb, w_dt[...], (1, 1)) + params[6:7, 0:OWN_HEADS]
    step = jnp.maximum(raw, 0.0) + jnp.log1p(jnp.exp(-jnp.abs(raw)))
    tables[24 : 24 + VOCAB, 0:OWN_HEADS] = step
    tables[24 : 24 + VOCAB, LINE : LINE + OWN_HEADS] = step * params[7:8, 0:OWN_HEADS]


def prepare_kernel(mine, other, conv_bc, grams_in, complement, tables, rows, steps):
    for side, given in enumerate((mine, other)):
        at = slice(OWN * side, OWN * (side + 1))
        x_taps = halves(taps_table(given[16:20, :], given[0:8, :]))
        tables[:, at] = x_taps
        gates = jnp.concatenate([jnp.zeros((24, OWN), F32), given[8:16, :]], 0)
        tables[:, PAIR + OWN * side : PAIR + OWN * (side + 1)] = halves(gates)
        rows[0:8, at] = given[16:24, :]
    tables[:, 2 * PAIR :] = grams_in[...]
    rows[8:12, 0 : 2 * STATE] = conv_bc[...].astype(F32)
    rows[8:12, 2 * STATE :] = jnp.zeros((4, PAIR - 2 * STATE), F32)
    rows[12:16, :] = jnp.zeros((4, PAIR), F32)
    for part in range(2):
        at = slice(LINE * part, LINE * (part + 1))
        steps[8 * part : 8 * part + 8, :] = given_steps(mine, at) + pltpu.roll(given_steps(other, at), OWN_HEADS, 1)
    lane = iota((1, LINE), 1)
    flips = jnp.zeros((1, LINE), F32)
    for symbol in range(VOCAB):
        flips = jnp.where(lane == symbol, complement[symbol].astype(F32), flips)
    steps[15:16, :] = flips


def given_steps(given, at):
    return given[24:32, at]


def before(x, steps):
    lane, line = (iota(x.shape, 1), iota(x.shape, 0))
    turned = pltpu.roll(x, steps, 1)
    over = jnp.where(line == 0, float(NONE), pltpu.roll(turned, 1, 0))
    return jnp.where(lane < steps, over, turned)


def after(x, steps):
    lane, line = (iota(x.shape, 1), iota(x.shape, 0))
    turned = pltpu.roll(x, 128 - steps, 1)
    over = jnp.where(line == LINES - 1, float(NONE), pltpu.roll(turned, LINES - 1, 0))
    return jnp.where(lane >= 128 - steps, over, turned)


def hot(symbols, count):
    return jnp.where(fiota((count, symbols.shape[1]), 0) == symbols, 1.0, 0.0)


def taps_table(taps, table):
    return jnp.concatenate([taps[k : k + 1, :] * table for k in range(CONV)], 0)


def halves(x):
    high = x.astype(BF16)
    low = (x - high.astype(F32)).astype(BF16)
    return jnp.concatenate([high.astype(F32), low.astype(F32)], 0).astype(BF16)


def scan_kernel(
    received, tables, rows, step_at, out, send,
    tok_ref, fwd_ref, back_ref, sums_ref,
):
    seq, chan = place()
    own_line = 2 * seq + chan // GROUP
    for chip in range(CHIPS):
        tok_ref[4 * chip : 4 * chip + 2, :] = received[chip, 5:7, :]
        tok_ref[4 * chip + 2 : 4 * chip + 4, :] = received[chip, 13:15, :]
    bc_sum = received[0]
    for chip in range(1, CHIPS):
        bc_sum = bc_sum + received[chip]
    bc_sum = jnp.where(lax.rem(iota((16, 128), 0), 8) < VOCAB, bc_sum, 0.0)
    bc_sum = bc_sum.astype(BF16).astype(F32)
    bc_tab = jnp.concatenate([bc_sum[0:8], bc_sum[8:16]], 1)
    bc_taps = halves(taps_table(rows[8:12, 0 : 2 * STATE], bc_tab))
    conv_tab = jnp.concatenate([tables[:, :PAIR], bc_taps, tables[:, PAIR : 2 * PAIR]], 1)

    tok = tok_ref[...]
    flipped = jnp.zeros(tok.shape, F32)
    for symbol in range(VOCAB):
        flipped = jnp.where(tok == float(symbol), step_at[15, symbol], flipped)
    fwd = [before(tok, 3), before(tok, 2), before(tok, 1), tok]
    back = [after(flipped, 3), after(flipped, 2), after(flipped, 1), flipped]
    for k in range(CONV):
        fwd_ref[k] = fwd[k]
        back_ref[k] = back[k]

    line = iota((LINES, 128), 0)
    ahead = line < own_line
    inside = line != own_line
    gram = [jnp.where(ahead, f, b) for f, b in zip(fwd, back)]
    older = gram[0] * 5.0 + gram[1] + jnp.where(ahead, 0.0, 32.0)
    newer = gram[2] * 5.0 + gram[3]
    newest = [jnp.logical_and(gram[3] == float(symbol), inside) for symbol in range(VOCAB)]
    marks = jnp.concatenate([jnp.where(hit, 1.0, 0.0) for hit in newest], 0).astype(BF16)
    row, column = (iota((128, 128), 0), iota((128, 128), 1))
    within = jnp.concatenate(
        [
            jnp.where(row > column, 1.0, 0.0),
            jnp.where(row < column, 1.0, 0.0),
            jnp.ones((128, 128), F32),
        ],
        1,
    ).astype(BF16)
    counts = dot(marks, within, (1, 0))
    parts = [counts[LINES * symbol : LINES * (symbol + 1)] for symbol in range(VOCAB)]
    totals = jnp.concatenate([part[:, 256:384] for part in parts], 1).astype(BF16)
    to, of = (iota((LINES, LINES), 0), iota((LINES, LINES), 1))
    between = jnp.logical_or(
        jnp.logical_and(to < of, of < own_line), jnp.logical_and(of > own_line, of < to)
    )
    lines_between = dot(jnp.where(between, 1.0, 0.0).astype(BF16), totals, (1, 0))
    passed = [
        jnp.where(ahead, part[:, 0:128], part[:, 128:256]) + lines_between[:, 128 * k : 128 * k + 128]
        for k, part in enumerate(parts)
    ]
    weights = []
    for head in range(PAIR_HEADS):
        lost = jnp.zeros((LINES, 128), F32)
        own_step = jnp.zeros((LINES, 128), F32)
        for symbol in range(VOCAB):
            lost = lost + step_at[8 + symbol, head] * passed[symbol]
            own_step = jnp.where(newest[symbol], step_at[symbol, head], own_step)
        weights.append(own_step * jnp.exp(-lost))

    head_of = iota((1, OWN), 1) // HEAD_DIM
    row, column = (iota((LINE, LINE), 0), iota((LINE, LINE), 1))
    done = {}

    def own_steps():
        hots = [
            jnp.concatenate([hot(ref[tap, pl.ds(own_line, 1), :], 8) for tap in range(CONV)], 0)
            for ref in (fwd_ref, back_ref)
        ]
        hots = jnp.concatenate(hots, 1)
        mixed = dot(jnp.concatenate([hots, hots], 0).astype(BF16), conv_tab, (0, 0))
        done["gate"] = mixed[:, PAIR + 2 * STATE :]
        yield
        first = silu(mixed[:, PAIR : PAIR + 2 * STATE])
        yield
        done["values"] = silu(mixed[:, :PAIR])
        yield
        grams = tables[:, 2 * PAIR :]
        done["gram_b"] = silu(dot(bc_taps[:, :STATE], grams, (0, 0))).astype(BF16)
        yield
        for head in range(PAIR_HEADS):
            x_taps = tables[:, LINE * (head // 2) : LINE * (head // 2 + 1)]
            if head % 2 == 0:
                both = silu(dot(x_taps, grams, (0, 0))).astype(BF16)
            done[head] = both[HEAD_DIM * (head % 2) : HEAD_DIM * (head % 2 + 1)]
            yield
        for strand in range(2):
            own = slice(LINE * strand, LINE * (strand + 1))
            b_in = first[own, :STATE].astype(BF16)
            c_out = first[own, STATE:]
            causal = row >= column if strand == 0 else row <= column
            order = row <= column if strand == 0 else row >= column
            symbols = hots[24:32, own]
            seen = dot(symbols.astype(BF16), jnp.where(order, 1.0, 0.0).astype(BF16), (1, 0))
            cumul, step = ([], [])
            for head in range(PAIR_HEADS):
                total = jnp.zeros((1, LINE), F32)
                own_step = jnp.zeros((1, LINE), F32)
                for symbol in range(VOCAB):
                    total = total - step_at[8 + symbol, head] * seen[symbol : symbol + 1]
                    own_step = own_step + step_at[symbol, head] * symbols[symbol : symbol + 1]
                cumul.append(total)
                step.append(own_step)
            yield
            across = jnp.transpose(
                jnp.concatenate(cumul + [jnp.zeros((LINE - PAIR_HEADS, LINE), F32)], 0)
            )
            scores = dot(c_out.astype(BF16), b_in, (1, 1))
            yield
            for head in range(PAIR_HEADS):
                at = slice(OWN * (head // OWN_HEADS), OWN * (head // OWN_HEADS + 1))
                column_of = across[:, head : head + 1]
                decayed = jnp.exp(jnp.where(causal, column_of - cumul[head], -1e30))
                left = (decayed * (scores * step[head])).astype(BF16)
                right = jnp.where(head_of == head % OWN_HEADS, done["values"][own, at], 0.0).astype(BF16)
                done[strand, head] = (left, right, (c_out * jnp.exp(column_of)).astype(BF16))
                yield

    steps = own_steps()

    older_down = jnp.transpose(jnp.concatenate([older, older], 0))
    lanes = fiota((128, 64), 1)
    sums = jnp.zeros((32 * PAIR_HEADS, 64), F32)
    for first in range(0, LINES, 2):
        left, right = ([], [])
        for at in (first, first + 1):
            left.append(jnp.where(lanes == older_down[:, at : at + 1], 1.0, 0.0))
            hits = fiota((32, 128), 0) == newer[at : at + 1]
            right.append(
                jnp.concatenate([jnp.where(hits, w[at : at + 1], 0.0) for w in weights], 0)
            )
        sums = sums + dot(
            jnp.concatenate(right, 1).astype(BF16), jnp.concatenate(left, 0).astype(BF16), (1, 0)
        )
        next(steps, None)
    for _ in steps:
        pass
    sums_ref[...] = jnp.concatenate([sums, sums], 1)

    by_newer = [sums_ref[pl.ds(newer, PAIR_HEADS, stride=32), :] for newer in range(32)]
    lane = iota((PAIR_HEADS, 128), 1)
    states = []
    for strand in range(2):
        lines = []
        for first in range(0, 32, 4):
            whole = jnp.zeros((PAIR_HEADS, 128), F32)
            for k in range(4):
                turned = pltpu.roll(by_newer[first + k], (32 * (k - strand)) % 128, 1)
                whole = jnp.where(lane // 32 == k, turned, whole)
            lines.append(whole)
        weight_of = jnp.concatenate(lines, 1)
        weighted = [
            done[head]
            * jnp.broadcast_to(weight_of[head : head + 1], (HEAD_DIM, 1024)).astype(BF16)
            for head in range(PAIR_HEADS)
        ]
        states.append(jnp.transpose(dot(jnp.concatenate(weighted, 0), done["gram_b"], (1, 1))))

    squares = []
    for strand in range(2):
        own = slice(LINE * strand, LINE * (strand + 1))
        squared = jnp.zeros((LINE, LINE), F32)
        for side in range(2):
            at = slice(OWN * side, OWN * (side + 1))
            values = done["values"][own, at]
            heads = [done[strand, OWN_HEADS * side + near] for near in range(OWN_HEADS)]
            tail = [
                jnp.where(head_of == near, states[strand][:, at], 0.0).astype(BF16)
                for near in range(OWN_HEADS)
            ]
            ssd = dot(
                jnp.concatenate([head[0] for head in heads] + [head[2] for head in heads], 1),
                jnp.concatenate([head[1] for head in heads] + tail, 0),
                (1, 0),
            )
            gated = (ssd + values * rows[5:6, at]) * done["gate"][own, at]
            out[own, at] = gated * rows[4:5, at]
            squared = squared + gated[:, :LINE] * gated[:, :LINE] + gated[:, LINE:] * gated[:, LINE:]
        squares.append(jnp.sum(jnp.transpose(squared), axis=0, keepdims=True))
    mine = jnp.concatenate(squares, 0)
    for peer in range(GROUP):
        send[peer] = mine


def project_kernel(squares, gated, w_own, w_other, out):
    total = squares[0]
    for peer in range(1, GROUP):
        total = total + squares[peer]
    scale = lax.rsqrt(total / (HEADS * HEAD_DIM) + EPSILON)
    combined = jnp.zeros((LINE, PAIR), F32)
    for strand in range(2):
        down = jnp.transpose(jnp.broadcast_to(scale[strand : strand + 1], (LINE, LINE)))
        block = gated[LINE * strand : LINE * (strand + 1), :]
        normed = block * jnp.concatenate([down] * (PAIR // LINE), 1)
        combined = combined + normed.astype(BF16).astype(F32)
    combined = combined.astype(BF16)
    mixed = dot(combined[:, :OWN], w_own[...], (1, 0)) + dot(combined[:, OWN:], w_other[...], (1, 0))
    out[...] = mixed.astype(BF16).reshape(out.shape)


def sum_kernel(received, out):
    total = received[0].astype(F32)
    for peer in range(1, GROUP):
        total = total + received[peer].astype(F32)
    out[...] = total.astype(BF16)


def call(kernel, outs, kinds, work, limit, scratch=()):
    return pl.pallas_call(
        kernel,
        out_shape=outs,
        in_specs=[pl.BlockSpec(memory_space=kind) for kind in kinds],
        out_specs=jax.tree.map(lambda _: pl.BlockSpec(memory_space=VMEM), outs),
        scratch_shapes=scratch,
        compiler_params=pltpu.CompilerParams(vmem_limit_bytes=limit * 2**20),
        cost_estimate=pl.CostEstimate(flops=work * 10**9, bytes_accessed=work * 2**20, transcendentals=0),
    )


def make_send(*args):
    return call(send_kernel, jax.ShapeDtypeStruct((CHIPS, 16, 128), F32), [VMEM] * 3, 1, 16)(*args)


def make_tables(*args):
    return call(tables_kernel, jax.ShapeDtypeStruct((32, OWN), F32), [VMEM] * 5, 1, 16)(*args)


def make_prepare(mine, other, conv_bc, complement):
    grams = gram_table()
    return call(
        prepare_kernel,
        (
            jax.ShapeDtypeStruct((64, 2 * PAIR + 1024), BF16),
            jax.ShapeDtypeStruct((16, PAIR), F32),
            jax.ShapeDtypeStruct((16, LINE), F32),
        ),
        [VMEM] * 4 + [SMEM],
        1,
        16,
    )(mine, other, conv_bc, jnp.asarray(grams, BF16), complement)


def make_scan(received, prepared):
    return call(
        scan_kernel,
        (
            jax.ShapeDtypeStruct((2 * LINE, PAIR), F32),
            jax.ShapeDtypeStruct((GROUP, 2, LINE), F32),
        ),
        [VMEM] * 3 + [SMEM],
        7,
        24,
        [
            pltpu.VMEM((LINES, 128), F32),
            pltpu.VMEM((CONV, LINES, 128), F32),
            pltpu.VMEM((CONV, LINES, 128), F32),
            pltpu.VMEM((32 * PAIR_HEADS, 128), F32),
        ],
    )(received, *prepared)


def make_project(squares, gated, *weights):
    shape = (GROUP, PIECE, weights[0].shape[1])
    return call(project_kernel, jax.ShapeDtypeStruct(shape, BF16), [VMEM] * 4, 1, 16)(
        squares, gated, *weights
    )


def make_sum(received):
    return call(sum_kernel, jax.ShapeDtypeStruct(received.shape[1:], BF16), [VMEM], 1, 16)(received)


def device(seq, chan):
    return seq * CHAN + chan


def mixed_groups():
    side = range(SIDE)
    return [
        [
            device(2 * (SIDE * y + high) + core, (y + right) % SIDE * SIDE + (high + up) % SIDE)
            for y in side
            for high in side
        ]
        for core in range(2)
        for right in side
        for up in side
    ]


def row_groups():
    return [list(range(GROUP)), list(range(GROUP, CHAN))]


def with_partner(value):
    pairs = [(x * SIDE + z, (SIDE - 1 - x) * SIDE + z) for x in range(SIDE) for z in range(SIDE)]
    return lax.ppermute(value, "chan", pairs)


def with_sibling(value):
    return lax.ppermute(value, "seq", [(source, source ^ 1) for source in range(SEQ)])


def exchange(value, axes, groups=None):
    return lax.all_to_all(value, axes, 0, 0, tiled=True, axis_index_groups=groups)


def per_device(
    tokens, complement, embed, w_x, w_z, w_bc, w_dt, dt_bias, decay_rate, d_skip, conv_x, conv_bc,
    norm_gain, w_out,
):
    own = tokens.reshape(2, 128)
    depth = w_bc.shape[0]
    part = lax.dynamic_slice_in_dim(embed, lax.axis_index("chan") * depth, depth, 1)
    send = make_send(own, with_sibling(own), dot(part, w_bc, (1, 0)))
    send, embed, conv_x, norm_gain, d_skip, dt_bias, decay_rate = lax.optimization_barrier(
        (send, embed, conv_x, norm_gain, d_skip, dt_bias, decay_rate)
    )
    received = exchange(send, ("seq", "chan"), mixed_groups())
    by_head = jnp.pad(jnp.stack([dt_bias, decay_rate]), ((0, 0), (0, OWN - OWN_HEADS)))
    by_channel = jnp.stack([norm_gain, jnp.repeat(d_skip, HEAD_DIM)])
    params = jnp.concatenate([conv_x.astype(F32), by_channel, by_head], 0)
    tables = make_tables(embed, w_x, w_z, w_dt.T, params)
    w_other = with_partner(w_out)
    other, w_other = lax.optimization_barrier((with_partner(tables), w_other))
    prepared = make_prepare(tables, other, conv_bc, complement)
    gated, squares = make_scan(received, prepared)
    partial = make_project(exchange(squares, "chan", row_groups()), gated, w_out, w_other)
    return make_sum(exchange(partial, "chan", row_groups()))


def solution(mesh):
    placed = (
        P("seq"),
        P(),
        P(),
        P(None, "chan"),
        P(None, "chan"),
        P("chan", None),
        P(None, "chan"),
        P("chan"),
        P("chan"),
        P("chan"),
        P(None, "chan"),
        P(),
        P("chan"),
        P("chan", None),
    )
    return jax.shard_map(
        per_device, mesh=mesh, in_specs=placed, out_specs=P(("seq", "chan"), None), check_vma=False
    )
```

```python
import jax
import jax.numpy as jnp
import numpy as np
from jax import lax
from jax.experimental import pallas as pl
from jax.experimental.pallas import tpu as pltpu
from jax.sharding import PartitionSpec as P

HEADS = 64
HEAD_DIM = 64
STATE = 128
CONV = 4
VOCAB = 5
ROWS = 256
OWN_HEADS = 4
OWN = OWN_HEADS * HEAD_DIM
SEQ = 32
CHAN = 16
CHIPS = SEQ // 2
LENGTH = SEQ * ROWS
LINES = LENGTH // 128
SIDE = 4
PAIR_HEADS = 2 * OWN_HEADS
PAIR = 2 * OWN
GROUP = CHAN // 2
LINE = 128
PIECE = LINE // GROUP
EPSILON = 1e-05
NONE = VOCAB
VMEM = pltpu.VMEM
SMEM = pltpu.SMEM
F32 = jnp.float32
BF16 = jnp.bfloat16


def gram_table():
    table = np.zeros((64, 1024), np.float32)
    for older in range(31):
        for newer in range(30):
            pair = lambda code: (5, 5) if code == 30 else (code // 5, code % 5)
            for tap, symbol in enumerate(pair(older) + pair(newer)):
                if symbol < VOCAB:
                    table[tap * 8 + symbol, newer * 32 + older] = 1
                    table[32 + tap * 8 + symbol, newer * 32 + older] = 1
    return table


def place():
    return lax.axis_index("seq"), lax.axis_index("chan")


def iota(shape, axis):
    return lax.broadcasted_iota(jnp.int32, shape, axis)


def fiota(shape, axis):
    return iota(shape, axis).astype(F32)


def dot(a, b, contract):
    return lax.dot_general(a, b, ((contract[:1], contract[1:]), ((), ())), preferred_element_type=F32)


def silu(x):
    return x / (1.0 + jnp.exp(-x))


def send_kernel(tokens, sibling, state_map, send):
    seq, _ = place()
    bc = state_map[...]
    mine = tokens[...].astype(F32)
    other = sibling[...].astype(F32)
    first = lax.rem(seq, 2) == 0
    own, other = (jnp.where(first, mine, other), jnp.where(first, other, mine))
    rest = jnp.zeros((1, 128), F32)
    block = jnp.concatenate([bc[:, :STATE], own, rest, bc[:, STATE:], other, rest], 0).astype(BF16)
    for peer in range(CHIPS):
        send[peer] = block


def tables_kernel(embed, w_x, w_z, w_dt, params, tables):
    emb = embed[...]
    x_tab = dot(emb, w_x[...], (1, 0)).astype(BF16).astype(F32)
    z_tab = dot(emb, w_z[...], (1, 0)).astype(BF16).astype(F32)
    tables[...] = jnp.zeros(tables.shape, F32)
    tables[0:VOCAB, :] = x_tab
    tables[8 : 8 + VOCAB, :] = silu(z_tab)
    tables[16:24, :] = params[...]
    raw = dot(emb, w_dt[...], (1, 1)) + params[6:7, 0:OWN_HEADS]
    step = jnp.maximum(raw, 0.0) + jnp.log1p(jnp.exp(-jnp.abs(raw)))
    tables[24 : 24 + VOCAB, 0:OWN_HEADS] = step
    tables[24 : 24 + VOCAB, LINE : LINE + OWN_HEADS] = step * params[7:8, 0:OWN_HEADS]


def prepare_kernel(mine, other, conv_bc, grams_in, complement, tables, rows, steps):
    for side, given in enumerate((mine, other)):
        at = slice(OWN * side, OWN * (side + 1))
        x_taps = halves(taps_table(given[16:20, :], given[0:8, :]))
        tables[:, at] = x_taps
        gates = jnp.concatenate([jnp.zeros((24, OWN), F32), given[8:16, :]], 0)
        tables[:, PAIR + OWN * side : PAIR + OWN * (side + 1)] = halves(gates)
        rows[0:8, at] = given[16:24, :]
    tables[:, 2 * PAIR :] = grams_in[...]
    rows[8:12, 0 : 2 * STATE] = conv_bc[...].astype(F32)
    rows[8:12, 2 * STATE :] = jnp.zeros((4, PAIR - 2 * STATE), F32)
    rows[12:16, :] = jnp.zeros((4, PAIR), F32)
    for part in range(2):
        at = slice(LINE * part, LINE * (part + 1))
        steps[8 * part : 8 * part + 8, :] = given_steps(mine, at) + pltpu.roll(given_steps(other, at), OWN_HEADS, 1)
    lane = iota((1, LINE), 1)
    flips = jnp.zeros((1, LINE), F32)
    for symbol in range(VOCAB):
        flips = jnp.where(lane == symbol, complement[symbol].astype(F32), flips)
    steps[15:16, :] = flips


def given_steps(given, at):
    return given[24:32, at]


def before(x, steps):
    lane, line = (iota(x.shape, 1), iota(x.shape, 0))
    turned = pltpu.roll(x, steps, 1)
    over = jnp.where(line == 0, float(NONE), pltpu.roll(turned, 1, 0))
    return jnp.where(lane < steps, over, turned)


def after(x, steps):
    lane, line = (iota(x.shape, 1), iota(x.shape, 0))
    turned = pltpu.roll(x, 128 - steps, 1)
    over = jnp.where(line == LINES - 1, float(NONE), pltpu.roll(turned, LINES - 1, 0))
    return jnp.where(lane >= 128 - steps, over, turned)


def hot(symbols, count):
    return jnp.where(fiota((count, symbols.shape[1]), 0) == symbols, 1.0, 0.0)


def taps_table(taps, table):
    return jnp.concatenate([taps[k : k + 1, :] * table for k in range(CONV)], 0)


def halves(x):
    high = x.astype(BF16)
    low = (x - high.astype(F32)).astype(BF16)
    return jnp.concatenate([high.astype(F32), low.astype(F32)], 0).astype(BF16)


def scan_kernel(
    received, tables, rows, step_at, out, send,
    tok_ref, fwd_ref, back_ref, sums_ref,
):
    seq, chan = place()
    own_line = 2 * seq + chan // GROUP
    bc_sum = jnp.zeros((16, 128), F32)
    for chip in range(CHIPS):
        block = received[chip].astype(F32)
        tok_ref[4 * chip : 4 * chip + 2, :] = block[5:7]
        tok_ref[4 * chip + 2 : 4 * chip + 4, :] = block[13:15]
        bc_sum = bc_sum + block
    bc_sum = jnp.where(lax.rem(iota((16, 128), 0), 8) < VOCAB, bc_sum, 0.0)
    bc_sum = bc_sum.astype(BF16).astype(F32)
    bc_tab = jnp.concatenate([bc_sum[0:8], bc_sum[8:16]], 1)
    bc_taps = halves(taps_table(rows[8:12, 0 : 2 * STATE], bc_tab))
    conv_tab = jnp.concatenate([tables[:, :PAIR], bc_taps, tables[:, PAIR : 2 * PAIR]], 1)

    tok = tok_ref[...]
    flipped = jnp.zeros(tok.shape, F32)
    for symbol in range(VOCAB):
        flipped = jnp.where(tok == float(symbol), step_at[15, symbol], flipped)
    fwd = [before(tok, 3), before(tok, 2), before(tok, 1), tok]
    back = [after(flipped, 3), after(flipped, 2), after(flipped, 1), flipped]
    for k in range(CONV):
        fwd_ref[k] = fwd[k]
        back_ref[k] = back[k]

    line = iota((LINES, 128), 0)
    ahead = line < own_line
    inside = line != own_line
    gram = [jnp.where(ahead, f, b) for f, b in zip(fwd, back)]
    older = gram[0] * 5.0 + gram[1] + jnp.where(ahead, 0.0, 32.0)
    newer = gram[2] * 5.0 + gram[3]
    newest = [jnp.logical_and(gram[3] == float(symbol), inside) for symbol in range(VOCAB)]
    marks = jnp.concatenate([jnp.where(hit, 1.0, 0.0) for hit in newest], 0).astype(BF16)
    row, column = (iota((128, 128), 0), iota((128, 128), 1))
    within = jnp.concatenate(
        [
            jnp.where(row > column, 1.0, 0.0),
            jnp.where(row < column, 1.0, 0.0),
            jnp.ones((128, 128), F32),
        ],
        1,
    ).astype(BF16)
    counts = dot(marks, within, (1, 0))
    parts = [counts[LINES * symbol : LINES * (symbol + 1)] for symbol in range(VOCAB)]
    totals = jnp.concatenate([part[:, 256:384] for part in parts], 1).astype(BF16)
    to, of = (iota((LINES, LINES), 0), iota((LINES, LINES), 1))
    between = jnp.logical_or(
        jnp.logical_and(to < of, of < own_line), jnp.logical_and(of > own_line, of < to)
    )
    lines_between = dot(jnp.where(between, 1.0, 0.0).astype(BF16), totals, (1, 0))
    passed = [
        jnp.where(ahead, part[:, 0:128], part[:, 128:256]) + lines_between[:, 128 * k : 128 * k + 128]
        for k, part in enumerate(parts)
    ]
    weights = []
    for head in range(PAIR_HEADS):
        lost = jnp.zeros((LINES, 128), F32)
        own_step = jnp.zeros((LINES, 128), F32)
        for symbol in range(VOCAB):
            lost = lost + step_at[8 + symbol, head] * passed[symbol]
            own_step = jnp.where(newest[symbol], step_at[symbol, head], own_step)
        weights.append(own_step * jnp.exp(-lost))

    head_of = iota((1, OWN), 1) // HEAD_DIM
    row, column = (iota((LINE, LINE), 0), iota((LINE, LINE), 1))
    done = {}

    def own_steps():
        hots = [
            jnp.concatenate([hot(ref[tap, pl.ds(own_line, 1), :], 8) for tap in range(CONV)], 0)
            for ref in (fwd_ref, back_ref)
        ]
        hots = jnp.concatenate(hots, 1)
        mixed = dot(jnp.concatenate([hots, hots], 0).astype(BF16), conv_tab, (0, 0))
        done["gate"] = mixed[:, PAIR + 2 * STATE :]
        yield
        first = silu(mixed[:, PAIR : PAIR + 2 * STATE])
        yield
        done["values"] = silu(mixed[:, :PAIR])
        yield
        grams = tables[:, 2 * PAIR :]
        done["gram_b"] = silu(dot(bc_taps[:, :STATE], grams, (0, 0))).astype(BF16)
        yield
        for head in range(PAIR_HEADS):
            x_taps = tables[:, LINE * (head // 2) : LINE * (head // 2 + 1)]
            if head % 2 == 0:
                both = silu(dot(x_taps, grams, (0, 0))).astype(BF16)
            done[head] = both[HEAD_DIM * (head % 2) : HEAD_DIM * (head % 2 + 1)]
            yield
        for strand in range(2):
            own = slice(LINE * strand, LINE * (strand + 1))
            b_in = first[own, :STATE].astype(BF16)
            c_out = first[own, STATE:]
            causal = row >= column if strand == 0 else row <= column
            order = row <= column if strand == 0 else row >= column
            symbols = hots[24:32, own]
            seen = dot(symbols.astype(BF16), jnp.where(order, 1.0, 0.0).astype(BF16), (1, 0))
            cumul, step = ([], [])
            for head in range(PAIR_HEADS):
                total = jnp.zeros((1, LINE), F32)
                own_step = jnp.zeros((1, LINE), F32)
                for symbol in range(VOCAB):
                    total = total - step_at[8 + symbol, head] * seen[symbol : symbol + 1]
                    own_step = own_step + step_at[symbol, head] * symbols[symbol : symbol + 1]
                cumul.append(total)
                step.append(own_step)
            yield
            across = jnp.transpose(
                jnp.concatenate(cumul + [jnp.zeros((LINE - PAIR_HEADS, LINE), F32)], 0)
            )
            scores = dot(c_out.astype(BF16), b_in, (1, 1))
            yield
            for head in range(PAIR_HEADS):
                at = slice(OWN * (head // OWN_HEADS), OWN * (head // OWN_HEADS + 1))
                column_of = across[:, head : head + 1]
                decayed = jnp.exp(jnp.where(causal, column_of - cumul[head], -1e30))
                left = (decayed * (scores * step[head])).astype(BF16)
                right = jnp.where(head_of == head % OWN_HEADS, done["values"][own, at], 0.0).astype(BF16)
                done[strand, head] = (left, right, (c_out * jnp.exp(column_of)).astype(BF16))
                yield

    steps = own_steps()

    older_down = jnp.transpose(jnp.concatenate([older, older], 0))
    lanes = fiota((128, 64), 1)
    sums = jnp.zeros((32 * PAIR_HEADS, 64), F32)
    for first in range(0, LINES, 2):
        left, right = ([], [])
        for at in (first, first + 1):
            left.append(jnp.where(lanes == older_down[:, at : at + 1], 1.0, 0.0))
            hits = fiota((32, 128), 0) == newer[at : at + 1]
            right.append(
                jnp.concatenate([jnp.where(hits, w[at : at + 1], 0.0) for w in weights], 0)
            )
        sums = sums + dot(
            jnp.concatenate(right, 1).astype(BF16), jnp.concatenate(left, 0).astype(BF16), (1, 0)
        )
        next(steps, None)
    for _ in steps:
        pass
    sums_ref[...] = jnp.concatenate([sums, sums], 1)

    by_newer = [sums_ref[pl.ds(newer, PAIR_HEADS, stride=32), :] for newer in range(32)]
    lane = iota((PAIR_HEADS, 128), 1)
    states = []
    for strand in range(2):
        lines = []
        for first in range(0, 32, 4):
            whole = jnp.zeros((PAIR_HEADS, 128), F32)
            for k in range(4):
                turned = pltpu.roll(by_newer[first + k], (32 * (k - strand)) % 128, 1)
                whole = jnp.where(lane // 32 == k, turned, whole)
            lines.append(whole)
        weight_of = jnp.concatenate(lines, 1)
        weighted = [
            done[head]
            * jnp.broadcast_to(weight_of[head : head + 1], (HEAD_DIM, 1024)).astype(BF16)
            for head in range(PAIR_HEADS)
        ]
        states.append(jnp.transpose(dot(jnp.concatenate(weighted, 0), done["gram_b"], (1, 1))))

    squares = []
    for strand in range(2):
        own = slice(LINE * strand, LINE * (strand + 1))
        squared = jnp.zeros((LINE, LINE), F32)
        for side in range(2):
            at = slice(OWN * side, OWN * (side + 1))
            values = done["values"][own, at]
            heads = [done[strand, OWN_HEADS * side + near] for near in range(OWN_HEADS)]
            tail = [
                jnp.where(head_of == near, states[strand][:, at], 0.0).astype(BF16)
                for near in range(OWN_HEADS)
            ]
            ssd = dot(
                jnp.concatenate([head[0] for head in heads] + [head[2] for head in heads], 1),
                jnp.concatenate([head[1] for head in heads] + tail, 0),
                (1, 0),
            )
            gated = (ssd + values * rows[5:6, at]) * done["gate"][own, at]
            out[own, at] = gated * rows[4:5, at]
            squared = squared + gated[:, :LINE] * gated[:, :LINE] + gated[:, LINE:] * gated[:, LINE:]
        squares.append(jnp.sum(jnp.transpose(squared), axis=0, keepdims=True))
    mine = jnp.concatenate(squares, 0)
    for peer in range(GROUP):
        send[peer] = mine


def project_kernel(squares, gated, w_own, w_other, out):
    total = squares[0]
    for peer in range(1, GROUP):
        total = total + squares[peer]
    scale = lax.rsqrt(total / (HEADS * HEAD_DIM) + EPSILON)
    combined = jnp.zeros((LINE, PAIR), F32)
    for strand in range(2):
        down = jnp.transpose(jnp.broadcast_to(scale[strand : strand + 1], (LINE, LINE)))
        block = gated[LINE * strand : LINE * (strand + 1), :]
        normed = block * jnp.concatenate([down] * (PAIR // LINE), 1)
        combined = combined + normed.astype(BF16).astype(F32)
    combined = combined.astype(BF16)
    mixed = dot(combined[:, :OWN], w_own[...], (1, 0)) + dot(combined[:, OWN:], w_other[...], (1, 0))
    out[...] = mixed.astype(BF16).reshape(out.shape)


def sum_kernel(received, out):
    total = received[0].astype(F32)
    for peer in range(1, GROUP):
        total = total + received[peer].astype(F32)
    out[...] = total.astype(BF16)


def call(kernel, outs, kinds, work, limit, scratch=()):
    return pl.pallas_call(
        kernel,
        out_shape=outs,
        in_specs=[pl.BlockSpec(memory_space=kind) for kind in kinds],
        out_specs=jax.tree.map(lambda _: pl.BlockSpec(memory_space=VMEM), outs),
        scratch_shapes=scratch,
        compiler_params=pltpu.CompilerParams(vmem_limit_bytes=limit * 2**20),
        cost_estimate=pl.CostEstimate(flops=work * 10**9, bytes_accessed=work * 2**20, transcendentals=0),
    )


def make_send(*args):
    return call(send_kernel, jax.ShapeDtypeStruct((CHIPS, 16, 128), BF16), [VMEM] * 3, 1, 16)(*args)


def make_tables(*args):
    return call(tables_kernel, jax.ShapeDtypeStruct((32, OWN), F32), [VMEM] * 5, 1, 16)(*args)


def make_prepare(mine, other, conv_bc, complement):
    grams = gram_table()
    return call(
        prepare_kernel,
        (
            jax.ShapeDtypeStruct((64, 2 * PAIR + 1024), BF16),
            jax.ShapeDtypeStruct((16, PAIR), F32),
            jax.ShapeDtypeStruct((16, LINE), F32),
        ),
        [VMEM] * 4 + [SMEM],
        1,
        16,
    )(mine, other, conv_bc, jnp.asarray(grams, BF16), complement)


def make_scan(received, prepared):
    return call(
        scan_kernel,
        (
            jax.ShapeDtypeStruct((2 * LINE, PAIR), F32),
            jax.ShapeDtypeStruct((GROUP, 2, LINE), F32),
        ),
        [VMEM] * 3 + [SMEM],
        7,
        24,
        [
            pltpu.VMEM((LINES, 128), F32),
            pltpu.VMEM((CONV, LINES, 128), F32),
            pltpu.VMEM((CONV, LINES, 128), F32),
            pltpu.VMEM((32 * PAIR_HEADS, 128), F32),
        ],
    )(received, *prepared)


def make_project(squares, gated, *weights):
    shape = (GROUP, PIECE, weights[0].shape[1])
    return call(project_kernel, jax.ShapeDtypeStruct(shape, BF16), [VMEM] * 4, 1, 16)(
        squares, gated, *weights
    )


def make_sum(received):
    return call(sum_kernel, jax.ShapeDtypeStruct(received.shape[1:], BF16), [VMEM], 1, 16)(received)


def device(seq, chan):
    return seq * CHAN + chan


def mixed_groups():
    side = range(SIDE)
    return [
        [
            device(2 * (SIDE * y + high) + core, (y + right) % SIDE * SIDE + (high + up) % SIDE)
            for y in side
            for high in side
        ]
        for core in range(2)
        for right in side
        for up in side
    ]


def row_groups():
    return [list(range(GROUP)), list(range(GROUP, CHAN))]


def with_partner(value):
    pairs = [(x * SIDE + z, (SIDE - 1 - x) * SIDE + z) for x in range(SIDE) for z in range(SIDE)]
    return lax.ppermute(value, "chan", pairs)


def with_sibling(value):
    return lax.ppermute(value, "seq", [(source, source ^ 1) for source in range(SEQ)])


def exchange(value, axes, groups=None):
    return lax.all_to_all(value, axes, 0, 0, tiled=True, axis_index_groups=groups)


def per_device(
    tokens, complement, embed, w_x, w_z, w_bc, w_dt, dt_bias, decay_rate, d_skip, conv_x, conv_bc,
    norm_gain, w_out,
):
    own = tokens.reshape(2, 128)
    depth = w_bc.shape[0]
    part = lax.dynamic_slice_in_dim(embed, lax.axis_index("chan") * depth, depth, 1)
    send = make_send(own, with_sibling(own), dot(part, w_bc, (1, 0)))
    send, embed, norm_gain, d_skip, dt_bias, decay_rate = lax.optimization_barrier(
        (send, embed, norm_gain, d_skip, dt_bias, decay_rate)
    )
    received = exchange(send, ("seq", "chan"), mixed_groups())
    by_head = jnp.pad(jnp.stack([dt_bias, decay_rate]), ((0, 0), (0, OWN - OWN_HEADS)))
    by_channel = jnp.stack([norm_gain, jnp.repeat(d_skip, HEAD_DIM)])
    params = jnp.concatenate([conv_x.astype(F32), by_channel, by_head], 0)
    tables = make_tables(embed, w_x, w_z, w_dt.T, params)
    w_other = with_partner(w_out)
    other, w_other = lax.optimization_barrier((with_partner(tables), w_other))
    prepared = make_prepare(tables, other, conv_bc, complement)
    gated, squares = make_scan(received, prepared)
    partial = make_project(exchange(squares, "chan", row_groups()), gated, w_out, w_other)
    return make_sum(exchange(partial, "chan", row_groups()))


def solution(mesh):
    placed = (
        P("seq"),
        P(),
        P(),
        P(None, "chan"),
        P(None, "chan"),
        P("chan", None),
        P(None, "chan"),
        P("chan"),
        P("chan"),
        P("chan"),
        P(None, "chan"),
        P(),
        P("chan"),
        P("chan", None),
    )
    return jax.shard_map(
        per_device, mesh=mesh, in_specs=placed, out_specs=P(("seq", "chan"), None), check_vma=False
    )
```

```python
import jax
import jax.numpy as jnp
import numpy as np
from jax import lax
from jax.experimental import pallas as pl
from jax.experimental.pallas import tpu as pltpu
from jax.sharding import PartitionSpec as P

HEADS = 64
HEAD_DIM = 64
STATE = 128
CONV = 4
VOCAB = 5
ROWS = 256
OWN_HEADS = 4
OWN = OWN_HEADS * HEAD_DIM
SEQ = 32
CHAN = 16
CHIPS = SEQ // 2
LENGTH = SEQ * ROWS
LINES = LENGTH // 128
SIDE = 4
PAIR_HEADS = 2 * OWN_HEADS
PAIR = 2 * OWN
GROUP = CHAN // 2
LINE = 128
PIECE = LINE // GROUP
EPSILON = 1e-05
NONE = VOCAB
VMEM = pltpu.VMEM
SMEM = pltpu.SMEM
F32 = jnp.float32
BF16 = jnp.bfloat16


def gram_table():
    table = np.zeros((64, 1024), np.float32)
    for older in range(31):
        for newer in range(30):
            pair = lambda code: (5, 5) if code == 30 else (code // 5, code % 5)
            for tap, symbol in enumerate(pair(older) + pair(newer)):
                if symbol < VOCAB:
                    table[tap * 8 + symbol, newer * 32 + older] = 1
                    table[32 + tap * 8 + symbol, newer * 32 + older] = 1
    return table


def place():
    return lax.axis_index("seq"), lax.axis_index("chan")


def iota(shape, axis):
    return lax.broadcasted_iota(jnp.int32, shape, axis)


def fiota(shape, axis):
    return iota(shape, axis).astype(F32)


def dot(a, b, contract):
    return lax.dot_general(a, b, ((contract[:1], contract[1:]), ((), ())), preferred_element_type=F32)


def silu(x):
    return x / (1.0 + jnp.exp(-x))


def send_kernel(tokens, sibling, state_map, send):
    seq, _ = place()
    bc = state_map[...]
    mine = tokens[...].astype(F32)
    other = sibling[...].astype(F32)
    first = lax.rem(seq, 2) == 0
    own, other = (jnp.where(first, mine, other), jnp.where(first, other, mine))
    rest = jnp.zeros((1, 128), F32)
    block = jnp.concatenate([bc[:, :STATE], own, rest, bc[:, STATE:], other, rest], 0).astype(BF16)
    for peer in range(CHIPS):
        send[peer] = block


def tables_kernel(embed, w_x, w_z, w_dt, params, tables):
    emb = embed[...]
    x_tab = dot(emb, w_x[...], (1, 0)).astype(BF16).astype(F32)
    z_tab = dot(emb, w_z[...], (1, 0)).astype(BF16).astype(F32)
    tables[...] = jnp.zeros(tables.shape, F32)
    tables[0:VOCAB, :] = x_tab
    tables[8 : 8 + VOCAB, :] = silu(z_tab)
    tables[16:24, :] = params[...]
    raw = dot(emb, w_dt[...], (1, 1)) + params[6:7, 0:OWN_HEADS]
    step = jnp.maximum(raw, 0.0) + jnp.log1p(jnp.exp(-jnp.abs(raw)))
    tables[24 : 24 + VOCAB, 0:OWN_HEADS] = step
    tables[24 : 24 + VOCAB, LINE : LINE + OWN_HEADS] = step * params[7:8, 0:OWN_HEADS]


def prepare_kernel(mine, other, conv_bc, grams_in, complement, tables, rows, steps):
    for side, given in enumerate((mine, other)):
        at = slice(OWN * side, OWN * (side + 1))
        x_taps = halves(taps_table(given[16:20, :], given[0:8, :]))
        tables[:, at] = x_taps
        gates = jnp.concatenate([jnp.zeros((24, OWN), F32), given[8:16, :]], 0)
        tables[:, PAIR + OWN * side : PAIR + OWN * (side + 1)] = halves(gates)
        rows[0:8, at] = given[16:24, :]
    tables[:, 2 * PAIR :] = grams_in[...]
    rows[8:12, 0 : 2 * STATE] = conv_bc[...].astype(F32)
    rows[8:12, 2 * STATE :] = jnp.zeros((4, PAIR - 2 * STATE), F32)
    rows[12:16, :] = jnp.zeros((4, PAIR), F32)
    for part in range(2):
        at = slice(LINE * part, LINE * (part + 1))
        steps[8 * part : 8 * part + 8, :] = given_steps(mine, at) + pltpu.roll(given_steps(other, at), OWN_HEADS, 1)
    lane = iota((1, LINE), 1)
    flips = jnp.zeros((1, LINE), F32)
    for symbol in range(VOCAB):
        flips = jnp.where(lane == symbol, complement[symbol].astype(F32), flips)
    steps[15:16, :] = flips


def given_steps(given, at):
    return given[24:32, at]


def before(x, steps):
    lane, line = (iota(x.shape, 1), iota(x.shape, 0))
    turned = pltpu.roll(x, steps, 1)
    over = jnp.where(line == 0, float(NONE), pltpu.roll(turned, 1, 0))
    return jnp.where(lane < steps, over, turned)


def after(x, steps):
    lane, line = (iota(x.shape, 1), iota(x.shape, 0))
    turned = pltpu.roll(x, 128 - steps, 1)
    over = jnp.where(line == LINES - 1, float(NONE), pltpu.roll(turned, LINES - 1, 0))
    return jnp.where(lane >= 128 - steps, over, turned)


def hot(symbols, count):
    return jnp.where(fiota((count, symbols.shape[1]), 0) == symbols, 1.0, 0.0)


def taps_table(taps, table):
    return jnp.concatenate([taps[k : k + 1, :] * table for k in range(CONV)], 0)


def halves(x):
    high = x.astype(BF16)
    low = (x - high.astype(F32)).astype(BF16)
    return jnp.concatenate([high.astype(F32), low.astype(F32)], 0).astype(BF16)


def scan_kernel(
    received, tables, rows, step_at, out, send,
    tok_ref, fwd_ref, back_ref, sums_ref,
):
    seq, chan = place()
    own_line = 2 * seq + chan // GROUP
    bc_sum = jnp.zeros((16, 128), F32)
    for chip in range(CHIPS):
        block = received[chip].astype(F32)
        tok_ref[4 * chip : 4 * chip + 2, :] = block[5:7]
        tok_ref[4 * chip + 2 : 4 * chip + 4, :] = block[13:15]
        bc_sum = bc_sum + block
    bc_sum = jnp.where(lax.rem(iota((16, 128), 0), 8) < VOCAB, bc_sum, 0.0)
    bc_sum = bc_sum.astype(BF16).astype(F32)
    bc_tab = jnp.concatenate([bc_sum[0:8], bc_sum[8:16]], 1)
    bc_taps = halves(taps_table(rows[8:12, 0 : 2 * STATE], bc_tab))
    conv_tab = jnp.concatenate([tables[:, :PAIR], bc_taps, tables[:, PAIR : 2 * PAIR]], 1)

    tok = tok_ref[...]
    flipped = jnp.zeros(tok.shape, F32)
    for symbol in range(VOCAB):
        flipped = jnp.where(tok == float(symbol), step_at[15, symbol], flipped)
    fwd = [before(tok, 3), before(tok, 2), before(tok, 1), tok]
    back = [after(flipped, 3), after(flipped, 2), after(flipped, 1), flipped]
    for k in range(CONV):
        fwd_ref[k] = fwd[k]
        back_ref[k] = back[k]

    line = iota((LINES, 128), 0)
    ahead = line < own_line
    inside = line != own_line
    gram = [jnp.where(ahead, f, b) for f, b in zip(fwd, back)]
    older = gram[0] * 5.0 + gram[1] + jnp.where(ahead, 0.0, 32.0)
    newer = gram[2] * 5.0 + gram[3]
    newest = [jnp.logical_and(gram[3] == float(symbol), inside) for symbol in range(VOCAB)]
    marks = jnp.concatenate([jnp.where(hit, 1.0, 0.0) for hit in newest], 0).astype(BF16)
    row, column = (iota((128, 128), 0), iota((128, 128), 1))
    within = jnp.concatenate(
        [
            jnp.where(row > column, 1.0, 0.0),
            jnp.where(row < column, 1.0, 0.0),
            jnp.ones((128, 128), F32),
        ],
        1,
    ).astype(BF16)
    counts = dot(marks, within, (1, 0))
    parts = [counts[LINES * symbol : LINES * (symbol + 1)] for symbol in range(VOCAB)]
    totals = jnp.concatenate([part[:, 256:384] for part in parts], 1).astype(BF16)
    to, of = (iota((LINES, LINES), 0), iota((LINES, LINES), 1))
    between = jnp.logical_or(
        jnp.logical_and(to < of, of < own_line), jnp.logical_and(of > own_line, of < to)
    )
    lines_between = dot(jnp.where(between, 1.0, 0.0).astype(BF16), totals, (1, 0))
    passed = [
        jnp.where(ahead, part[:, 0:128], part[:, 128:256]) + lines_between[:, 128 * k : 128 * k + 128]
        for k, part in enumerate(parts)
    ]
    weights = []
    for head in range(PAIR_HEADS):
        lost = jnp.zeros((LINES, 128), F32)
        own_step = jnp.zeros((LINES, 128), F32)
        for symbol in range(VOCAB):
            lost = lost + step_at[8 + symbol, head] * passed[symbol]
            own_step = jnp.where(newest[symbol], step_at[symbol, head], own_step)
        weights.append(own_step * jnp.exp(-lost))

    head_of = iota((1, OWN), 1) // HEAD_DIM
    row, column = (iota((LINE, LINE), 0), iota((LINE, LINE), 1))
    done = {}

    def own_steps():
        hots = [
            jnp.concatenate([hot(ref[tap, pl.ds(own_line, 1), :], 8) for tap in range(CONV)], 0)
            for ref in (fwd_ref, back_ref)
        ]
        hots = jnp.concatenate(hots, 1)
        mixed = dot(jnp.concatenate([hots, hots], 0).astype(BF16), conv_tab, (0, 0))
        done["gate"] = mixed[:, PAIR + 2 * STATE :]
        yield
        first = silu(mixed[:, PAIR : PAIR + 2 * STATE])
        yield
        done["values"] = silu(mixed[:, :PAIR])
        yield
        grams = tables[:, 2 * PAIR :]
        done["gram_b"] = silu(dot(bc_taps[:, :STATE], grams, (0, 0))).astype(BF16)
        yield
        for head in range(PAIR_HEADS):
            x_taps = tables[:, LINE * (head // 2) : LINE * (head // 2 + 1)]
            if head % 2 == 0:
                both = silu(dot(x_taps, grams, (0, 0))).astype(BF16)
            done[head] = both[HEAD_DIM * (head % 2) : HEAD_DIM * (head % 2 + 1)]
            yield
        for strand in range(2):
            own = slice(LINE * strand, LINE * (strand + 1))
            b_in = first[own, :STATE].astype(BF16)
            c_out = first[own, STATE:]
            causal = row >= column if strand == 0 else row <= column
            order = row <= column if strand == 0 else row >= column
            symbols = hots[24:32, own]
            seen = dot(symbols.astype(BF16), jnp.where(order, 1.0, 0.0).astype(BF16), (1, 0))
            cumul, step = ([], [])
            for head in range(PAIR_HEADS):
                total = jnp.zeros((1, LINE), F32)
                own_step = jnp.zeros((1, LINE), F32)
                for symbol in range(VOCAB):
                    total = total - step_at[8 + symbol, head] * seen[symbol : symbol + 1]
                    own_step = own_step + step_at[symbol, head] * symbols[symbol : symbol + 1]
                cumul.append(total)
                step.append(own_step)
            yield
            across = jnp.transpose(
                jnp.concatenate(cumul + [jnp.zeros((LINE - PAIR_HEADS, LINE), F32)], 0)
            )
            scores = dot(c_out.astype(BF16), b_in, (1, 1))
            done["c_out", strand] = c_out.astype(BF16)
            yield
            for head in range(PAIR_HEADS):
                at = slice(OWN * (head // OWN_HEADS), OWN * (head // OWN_HEADS + 1))
                column_of = across[:, head : head + 1]
                decayed = jnp.exp(jnp.where(causal, column_of - cumul[head], -1e30))
                left = (decayed * (scores * step[head])).astype(BF16)
                right = jnp.where(head_of == head % OWN_HEADS, done["values"][own, at], 0.0).astype(BF16)
                done[strand, head] = (left, right, jnp.exp(column_of))
                yield

    steps = own_steps()

    older_down = jnp.transpose(jnp.concatenate([older, older], 0))
    lanes = fiota((128, 64), 1)
    sums = jnp.zeros((32 * PAIR_HEADS, 64), F32)
    for first in range(0, LINES, 2):
        left, right = ([], [])
        for at in (first, first + 1):
            left.append(jnp.where(lanes == older_down[:, at : at + 1], 1.0, 0.0))
            hits = fiota((32, 128), 0) == newer[at : at + 1]
            right.append(
                jnp.concatenate([jnp.where(hits, w[at : at + 1], 0.0) for w in weights], 0)
            )
        sums = sums + dot(
            jnp.concatenate(right, 1).astype(BF16), jnp.concatenate(left, 0).astype(BF16), (1, 0)
        )
        next(steps, None)
    for _ in steps:
        pass
    sums_ref[...] = jnp.concatenate([sums, sums], 1)

    by_newer = [sums_ref[pl.ds(newer, PAIR_HEADS, stride=32), :] for newer in range(32)]
    lane = iota((PAIR_HEADS, 128), 1)
    states = []
    for strand in range(2):
        lines = []
        for first in range(0, 32, 4):
            whole = jnp.zeros((PAIR_HEADS, 128), F32)
            for k in range(4):
                turned = pltpu.roll(by_newer[first + k], (32 * (k - strand)) % 128, 1)
                whole = jnp.where(lane // 32 == k, turned, whole)
            lines.append(whole)
        weight_of = jnp.concatenate(lines, 1)
        weighted = [
            done[head]
            * jnp.broadcast_to(weight_of[head : head + 1], (HEAD_DIM, 1024)).astype(BF16)
            for head in range(PAIR_HEADS)
        ]
        states.append(dot(jnp.concatenate(weighted, 0), done["gram_b"], (1, 1)).astype(BF16))

    squares = []
    for strand in range(2):
        own = slice(LINE * strand, LINE * (strand + 1))
        squared = jnp.zeros((LINE, LINE), F32)
        carried = dot(done["c_out", strand], states[strand], (1, 1))
        for side in range(2):
            at = slice(OWN * side, OWN * (side + 1))
            values = done["values"][own, at]
            heads = [done[strand, OWN_HEADS * side + near] for near in range(OWN_HEADS)]
            growth = jnp.zeros((LINE, OWN), F32)
            for near in range(OWN_HEADS):
                growth = jnp.where(head_of == near, heads[near][2], growth)
            ssd = dot(
                jnp.concatenate([head[0] for head in heads], 1),
                jnp.concatenate([head[1] for head in heads], 0),
                (1, 0),
            )
            ssd = ssd + growth * carried[:, at]
            gated = (ssd + values * rows[5:6, at]) * done["gate"][own, at]
            out[own, at] = gated * rows[4:5, at]
            squared = squared + gated[:, :LINE] * gated[:, :LINE] + gated[:, LINE:] * gated[:, LINE:]
        squares.append(jnp.sum(jnp.transpose(squared), axis=0, keepdims=True))
    mine = jnp.concatenate(squares, 0)
    for peer in range(GROUP):
        send[peer] = mine


def project_kernel(squares, gated, w_own, w_other, out):
    total = squares[0]
    for peer in range(1, GROUP):
        total = total + squares[peer]
    scale = lax.rsqrt(total / (HEADS * HEAD_DIM) + EPSILON)
    combined = jnp.zeros((LINE, PAIR), F32)
    for strand in range(2):
        down = jnp.transpose(jnp.broadcast_to(scale[strand : strand + 1], (LINE, LINE)))
        block = gated[LINE * strand : LINE * (strand + 1), :]
        normed = block * jnp.concatenate([down] * (PAIR // LINE), 1)
        combined = combined + normed.astype(BF16).astype(F32)
    combined = combined.astype(BF16)
    mixed = dot(combined[:, :OWN], w_own[...], (1, 0)) + dot(combined[:, OWN:], w_other[...], (1, 0))
    out[...] = mixed.astype(BF16).reshape(out.shape)


def sum_kernel(received, out):
    total = received[0].astype(F32)
    for peer in range(1, GROUP):
        total = total + received[peer].astype(F32)
    out[...] = total.astype(BF16)


def call(kernel, outs, kinds, work, limit, scratch=()):
    return pl.pallas_call(
        kernel,
        out_shape=outs,
        in_specs=[pl.BlockSpec(memory_space=kind) for kind in kinds],
        out_specs=jax.tree.map(lambda _: pl.BlockSpec(memory_space=VMEM), outs),
        scratch_shapes=scratch,
        compiler_params=pltpu.CompilerParams(vmem_limit_bytes=limit * 2**20),
        cost_estimate=pl.CostEstimate(flops=work * 10**9, bytes_accessed=work * 2**20, transcendentals=0),
    )


def make_send(*args):
    return call(send_kernel, jax.ShapeDtypeStruct((CHIPS, 16, 128), BF16), [VMEM] * 3, 1, 16)(*args)


def make_tables(*args):
    return call(tables_kernel, jax.ShapeDtypeStruct((32, OWN), F32), [VMEM] * 5, 1, 16)(*args)


def make_prepare(mine, other, conv_bc, complement):
    grams = gram_table()
    return call(
        prepare_kernel,
        (
            jax.ShapeDtypeStruct((64, 2 * PAIR + 1024), BF16),
            jax.ShapeDtypeStruct((16, PAIR), F32),
            jax.ShapeDtypeStruct((16, LINE), F32),
        ),
        [VMEM] * 4 + [SMEM],
        1,
        16,
    )(mine, other, conv_bc, jnp.asarray(grams, BF16), complement)


def make_scan(received, prepared):
    return call(
        scan_kernel,
        (
            jax.ShapeDtypeStruct((2 * LINE, PAIR), F32),
            jax.ShapeDtypeStruct((GROUP, 2, LINE), F32),
        ),
        [VMEM] * 3 + [SMEM],
        7,
        24,
        [
            pltpu.VMEM((LINES, 128), F32),
            pltpu.VMEM((CONV, LINES, 128), F32),
            pltpu.VMEM((CONV, LINES, 128), F32),
            pltpu.VMEM((32 * PAIR_HEADS, 128), F32),
        ],
    )(received, *prepared)


def make_project(squares, gated, *weights):
    shape = (GROUP, PIECE, weights[0].shape[1])
    return call(project_kernel, jax.ShapeDtypeStruct(shape, BF16), [VMEM] * 4, 1, 16)(
        squares, gated, *weights
    )


def make_sum(received):
    return call(sum_kernel, jax.ShapeDtypeStruct(received.shape[1:], BF16), [VMEM], 1, 16)(received)


def device(seq, chan):
    return seq * CHAN + chan


def mixed_groups():
    side = range(SIDE)
    return [
        [
            device(2 * (SIDE * y + high) + core, (y + right) % SIDE * SIDE + (high + up) % SIDE)
            for y in side
            for high in side
        ]
        for core in range(2)
        for right in side
        for up in side
    ]


def row_groups():
    return [list(range(GROUP)), list(range(GROUP, CHAN))]


def with_partner(value):
    pairs = [(x * SIDE + z, (SIDE - 1 - x) * SIDE + z) for x in range(SIDE) for z in range(SIDE)]
    return lax.ppermute(value, "chan", pairs)


def with_sibling(value):
    return lax.ppermute(value, "seq", [(source, source ^ 1) for source in range(SEQ)])


def exchange(value, axes, groups=None):
    return lax.all_to_all(value, axes, 0, 0, tiled=True, axis_index_groups=groups)


def per_device(
    tokens, complement, embed, w_x, w_z, w_bc, w_dt, dt_bias, decay_rate, d_skip, conv_x, conv_bc,
    norm_gain, w_out,
):
    own = tokens.reshape(2, 128)
    depth = w_bc.shape[0]
    part = lax.dynamic_slice_in_dim(embed, lax.axis_index("chan") * depth, depth, 1)
    send = make_send(own, with_sibling(own), dot(part, w_bc, (1, 0)))
    send, embed, norm_gain, d_skip, dt_bias, decay_rate = lax.optimization_barrier(
        (send, embed, norm_gain, d_skip, dt_bias, decay_rate)
    )
    received = exchange(send, ("seq", "chan"), mixed_groups())
    by_head = jnp.pad(jnp.stack([dt_bias, decay_rate]), ((0, 0), (0, OWN - OWN_HEADS)))
    by_channel = jnp.stack([norm_gain, jnp.repeat(d_skip, HEAD_DIM)])
    params = jnp.concatenate([conv_x.astype(F32), by_channel, by_head], 0)
    tables = make_tables(embed, w_x, w_z, w_dt.T, params)
    w_other = with_partner(w_out)
    other, w_other = lax.optimization_barrier((with_partner(tables), w_other))
    prepared = make_prepare(tables, other, conv_bc, complement)
    gated, squares = make_scan(received, prepared)
    partial = make_project(exchange(squares, "chan", row_groups()), gated, w_out, w_other)
    return make_sum(exchange(partial, "chan", row_groups()))


def solution(mesh):
    placed = (
        P("seq"),
        P(),
        P(),
        P(None, "chan"),
        P(None, "chan"),
        P("chan", None),
        P(None, "chan"),
        P("chan"),
        P("chan"),
        P("chan"),
        P(None, "chan"),
        P(),
        P("chan"),
        P("chan", None),
    )
    return jax.shard_map(
        per_device, mesh=mesh, in_specs=placed, out_specs=P(("seq", "chan"), None), check_vma=False
    )
```

```python
import jax
import jax.numpy as jnp
import numpy as np
from jax import lax
from jax.experimental import pallas as pl
from jax.experimental.pallas import tpu as pltpu
from jax.sharding import PartitionSpec as P

HEADS = 64
HEAD_DIM = 64
STATE = 128
CONV = 4
VOCAB = 5
ROWS = 256
OWN_HEADS = 4
OWN = OWN_HEADS * HEAD_DIM
SEQ = 32
CHAN = 16
CHIPS = SEQ // 2
LENGTH = SEQ * ROWS
LINES = LENGTH // 128
SIDE = 4
PAIR_HEADS = 2 * OWN_HEADS
PAIR = 2 * OWN
GROUP = CHAN // 2
LINE = 128
PIECE = LINE // GROUP
EPSILON = 1e-05
NONE = VOCAB
VMEM = pltpu.VMEM
SMEM = pltpu.SMEM
F32 = jnp.float32
BF16 = jnp.bfloat16


def gram_table():
    table = np.zeros((64, 1024), np.float32)
    for older in range(31):
        for newer in range(30):
            pair = lambda code: (5, 5) if code == 30 else (code // 5, code % 5)
            for tap, symbol in enumerate(pair(older) + pair(newer)):
                if symbol < VOCAB:
                    table[tap * 8 + symbol, newer * 32 + older] = 1
                    table[32 + tap * 8 + symbol, newer * 32 + older] = 1
    return table


def place():
    return lax.axis_index("seq"), lax.axis_index("chan")


def iota(shape, axis):
    return lax.broadcasted_iota(jnp.int32, shape, axis)


def fiota(shape, axis):
    return iota(shape, axis).astype(F32)


def dot(a, b, contract):
    return lax.dot_general(a, b, ((contract[:1], contract[1:]), ((), ())), preferred_element_type=F32)


def silu(x):
    return x / (1.0 + jnp.exp(-x))


def send_kernel(tokens, sibling, state_map, send):
    seq, _ = place()
    bc = state_map[...]
    mine = tokens[...].astype(F32)
    other = sibling[...].astype(F32)
    first = lax.rem(seq, 2) == 0
    own, other = (jnp.where(first, mine, other), jnp.where(first, other, mine))
    rest = jnp.zeros((1, 128), F32)
    block = jnp.concatenate([bc[:, :STATE], own, rest, bc[:, STATE:], other, rest], 0).astype(BF16)
    for peer in range(CHIPS):
        send[peer] = block


def tables_kernel(embed, w_x, w_z, w_dt, params, tables):
    emb = embed[...]
    x_tab = dot(emb, w_x[...], (1, 0)).astype(BF16).astype(F32)
    z_tab = dot(emb, w_z[...], (1, 0)).astype(BF16).astype(F32)
    tables[...] = jnp.zeros(tables.shape, F32)
    tables[0:VOCAB, :] = x_tab
    tables[8 : 8 + VOCAB, :] = silu(z_tab)
    tables[16:24, :] = params[...]
    raw = dot(emb, w_dt[...], (1, 1)) + params[6:7, 0:OWN_HEADS]
    step = jnp.maximum(raw, 0.0) + jnp.log1p(jnp.exp(-jnp.abs(raw)))
    tables[24 : 24 + VOCAB, 0:OWN_HEADS] = step
    tables[24 : 24 + VOCAB, LINE : LINE + OWN_HEADS] = step * params[7:8, 0:OWN_HEADS]


def prepare_kernel(mine, other, conv_bc, grams_in, complement, tables, rows, steps):
    for side, given in enumerate((mine, other)):
        at = slice(OWN * side, OWN * (side + 1))
        x_taps = halves(taps_table(given[16:20, :], given[0:8, :]))
        tables[:, at] = x_taps
        gates = jnp.concatenate([jnp.zeros((24, OWN), F32), given[8:16, :]], 0)
        tables[:, PAIR + OWN * side : PAIR + OWN * (side + 1)] = halves(gates)
        rows[0:8, at] = given[16:24, :]
    tables[:, 2 * PAIR :] = grams_in[...]
    rows[8:12, 0 : 2 * STATE] = conv_bc[...].astype(F32)
    rows[8:12, 2 * STATE :] = jnp.zeros((4, PAIR - 2 * STATE), F32)
    rows[12:16, :] = jnp.zeros((4, PAIR), F32)
    for part in range(2):
        at = slice(LINE * part, LINE * (part + 1))
        steps[8 * part : 8 * part + 8, :] = given_steps(mine, at) + pltpu.roll(given_steps(other, at), OWN_HEADS, 1)
    lane = iota((1, LINE), 1)
    flips = jnp.zeros((1, LINE), F32)
    for symbol in range(VOCAB):
        flips = jnp.where(lane == symbol, complement[symbol].astype(F32), flips)
    steps[15:16, :] = flips


def given_steps(given, at):
    return given[24:32, at]


def before(x, steps):
    lane, line = (iota(x.shape, 1), iota(x.shape, 0))
    turned = pltpu.roll(x, steps, 1)
    over = jnp.where(line == 0, float(NONE), pltpu.roll(turned, 1, 0))
    return jnp.where(lane < steps, over, turned)


def after(x, steps):
    lane, line = (iota(x.shape, 1), iota(x.shape, 0))
    turned = pltpu.roll(x, 128 - steps, 1)
    over = jnp.where(line == LINES - 1, float(NONE), pltpu.roll(turned, LINES - 1, 0))
    return jnp.where(lane >= 128 - steps, over, turned)


def hot(symbols, count):
    return jnp.where(fiota((count, symbols.shape[1]), 0) == symbols, 1.0, 0.0)


def taps_table(taps, table):
    return jnp.concatenate([taps[k : k + 1, :] * table for k in range(CONV)], 0)


def halves(x):
    high = x.astype(BF16)
    low = (x - high.astype(F32)).astype(BF16)
    return jnp.concatenate([high.astype(F32), low.astype(F32)], 0).astype(BF16)


def scan_kernel(
    received, tables, rows, step_at, out, send,
    tok_ref, fwd_ref, back_ref, sums_ref,
):
    seq, chan = place()
    own_line = 2 * seq + chan // GROUP
    bc_sum = jnp.zeros((16, 128), F32)
    for chip in range(CHIPS):
        block = received[chip].astype(F32)
        tok_ref[4 * chip : 4 * chip + 2, :] = block[5:7]
        tok_ref[4 * chip + 2 : 4 * chip + 4, :] = block[13:15]
        bc_sum = bc_sum + block
    bc_sum = jnp.where(lax.rem(iota((16, 128), 0), 8) < VOCAB, bc_sum, 0.0)
    bc_sum = bc_sum.astype(BF16).astype(F32)
    bc_tab = jnp.concatenate([bc_sum[0:8], bc_sum[8:16]], 1)
    bc_taps = halves(taps_table(rows[8:12, 0 : 2 * STATE], bc_tab))
    conv_tab = jnp.concatenate([tables[:, :PAIR], bc_taps, tables[:, PAIR : 2 * PAIR]], 1)

    tok = tok_ref[...]
    flipped = jnp.zeros(tok.shape, F32)
    for symbol in range(VOCAB):
        flipped = jnp.where(tok == float(symbol), step_at[15, symbol], flipped)
    fwd = [before(tok, 3), before(tok, 2), before(tok, 1), tok]
    back = [after(flipped, 3), after(flipped, 2), after(flipped, 1), flipped]
    for k in range(CONV):
        fwd_ref[k] = fwd[k]
        back_ref[k] = back[k]

    line = iota((LINES, 128), 0)
    ahead = line < own_line
    inside = line != own_line
    gram = [jnp.where(ahead, f, b) for f, b in zip(fwd, back)]
    older = gram[0] * 5.0 + gram[1] + jnp.where(ahead, 0.0, 32.0)
    newer = gram[2] * 5.0 + gram[3]
    newest = [jnp.logical_and(gram[3] == float(symbol), inside) for symbol in range(VOCAB)]
    marks = jnp.concatenate([jnp.where(hit, 1.0, 0.0) for hit in newest], 0).astype(BF16)
    row, column = (iota((128, 128), 0), iota((128, 128), 1))
    within = jnp.concatenate(
        [
            jnp.where(row > column, 1.0, 0.0),
            jnp.where(row < column, 1.0, 0.0),
            jnp.ones((128, 128), F32),
        ],
        1,
    ).astype(BF16)
    counts = dot(marks, within, (1, 0))
    parts = [counts[LINES * symbol : LINES * (symbol + 1)] for symbol in range(VOCAB)]
    totals = jnp.concatenate([part[:, 256:384] for part in parts], 1).astype(BF16)
    to, of = (iota((LINES, LINES), 0), iota((LINES, LINES), 1))
    between = jnp.logical_or(
        jnp.logical_and(to < of, of < own_line), jnp.logical_and(of > own_line, of < to)
    )
    lines_between = dot(jnp.where(between, 1.0, 0.0).astype(BF16), totals, (1, 0))
    passed = [
        jnp.where(ahead, part[:, 0:128], part[:, 128:256]) + lines_between[:, 128 * k : 128 * k + 128]
        for k, part in enumerate(parts)
    ]
    weights = []
    for head in range(PAIR_HEADS):
        lost = jnp.zeros((LINES, 128), F32)
        own_step = jnp.zeros((LINES, 128), F32)
        for symbol in range(VOCAB):
            lost = lost + step_at[8 + symbol, head] * passed[symbol]
            own_step = jnp.where(newest[symbol], step_at[symbol, head], own_step)
        weights.append(own_step * jnp.exp(-lost))

    head_of = iota((1, OWN), 1) // HEAD_DIM
    row, column = (iota((LINE, LINE), 0), iota((LINE, LINE), 1))
    done = {}

    def own_steps():
        hots = [
            jnp.concatenate([hot(ref[tap, pl.ds(own_line, 1), :], 8) for tap in range(CONV)], 0)
            for ref in (fwd_ref, back_ref)
        ]
        hots = jnp.concatenate(hots, 1)
        mixed = dot(jnp.concatenate([hots, hots], 0).astype(BF16), conv_tab, (0, 0))
        done["gate"] = mixed[:, PAIR + 2 * STATE :]
        yield
        first = silu(mixed[:, PAIR : PAIR + 2 * STATE])
        yield
        done["values"] = silu(mixed[:, :PAIR])
        yield
        grams = tables[:, 2 * PAIR :]
        done["gram_b"] = silu(dot(bc_taps[:, :STATE], grams, (0, 0))).astype(BF16)
        yield
        for head in range(PAIR_HEADS):
            x_taps = tables[:, LINE * (head // 2) : LINE * (head // 2 + 1)]
            if head % 2 == 0:
                both = silu(dot(x_taps, grams, (0, 0))).astype(BF16)
            done[head] = both[HEAD_DIM * (head % 2) : HEAD_DIM * (head % 2 + 1)]
            yield
        for strand in range(2):
            own = slice(LINE * strand, LINE * (strand + 1))
            b_in = first[own, :STATE].astype(BF16)
            c_out = first[own, STATE:]
            causal = row >= column if strand == 0 else row <= column
            order = row <= column if strand == 0 else row >= column
            symbols = hots[24:32, own]
            seen = dot(symbols.astype(BF16), jnp.where(order, 1.0, 0.0).astype(BF16), (1, 0))
            cumul, step = ([], [])
            for head in range(PAIR_HEADS):
                total = jnp.zeros((1, LINE), F32)
                own_step = jnp.zeros((1, LINE), F32)
                for symbol in range(VOCAB):
                    total = total - step_at[8 + symbol, head] * seen[symbol : symbol + 1]
                    own_step = own_step + step_at[symbol, head] * symbols[symbol : symbol + 1]
                cumul.append(total)
                step.append(own_step)
            yield
            across = jnp.transpose(
                jnp.concatenate(cumul + [jnp.zeros((LINE - PAIR_HEADS, LINE), F32)], 0)
            )
            scores = dot(c_out.astype(BF16), b_in, (1, 1))
            done["c_out", strand] = c_out.astype(BF16)
            yield
            for head in range(PAIR_HEADS):
                at = slice(OWN * (head // OWN_HEADS), OWN * (head // OWN_HEADS + 1))
                column_of = across[:, head : head + 1]
                decayed = jnp.exp(jnp.where(causal, column_of - cumul[head], -1e30))
                left = (decayed * (scores * step[head])).astype(BF16)
                right = jnp.where(head_of == head % OWN_HEADS, done["values"][own, at], 0.0).astype(BF16)
                done[strand, head] = (left, right, jnp.exp(column_of))
                yield

    steps = own_steps()

    older_down = jnp.transpose(jnp.concatenate([older, older], 0))
    lanes = fiota((128, 64), 1)
    sums = jnp.zeros((32 * PAIR_HEADS, 64), F32)
    for first in range(0, LINES, 2):
        left, right = ([], [])
        for at in (first, first + 1):
            left.append(jnp.where(lanes == older_down[:, at : at + 1], 1.0, 0.0))
            hits = fiota((32, 128), 0) == newer[at : at + 1]
            right.append(
                jnp.concatenate([jnp.where(hits, w[at : at + 1], 0.0) for w in weights], 0)
            )
        sums = sums + dot(
            jnp.concatenate(right, 1).astype(BF16), jnp.concatenate(left, 0).astype(BF16), (1, 0)
        )
        next(steps, None)
    for _ in steps:
        pass
    sums_ref[...] = jnp.concatenate([sums, sums], 1)

    by_newer = [sums_ref[pl.ds(newer, PAIR_HEADS, stride=32), :] for newer in range(32)]
    lane = iota((PAIR_HEADS, 128), 1)
    states = []
    for strand in range(2):
        lines = []
        for first in range(0, 32, 4):
            whole = jnp.zeros((PAIR_HEADS, 128), F32)
            for k in range(4):
                turned = pltpu.roll(by_newer[first + k], (32 * (k - strand)) % 128, 1)
                whole = jnp.where(lane // 32 == k, turned, whole)
            lines.append(whole)
        weight_of = jnp.concatenate(lines, 1)
        weighted = [
            done[head]
            * jnp.broadcast_to(weight_of[head : head + 1], (HEAD_DIM, 1024)).astype(BF16)
            for head in range(PAIR_HEADS)
        ]
        states.append(dot(jnp.concatenate(weighted, 0), done["gram_b"], (1, 1)).astype(BF16))

    squares = []
    for strand in range(2):
        own = slice(LINE * strand, LINE * (strand + 1))
        squared = jnp.zeros((LINE, LINE), F32)
        carried = dot(done["c_out", strand], states[strand], (1, 1))
        for side in range(2):
            at = slice(OWN * side, OWN * (side + 1))
            values = done["values"][own, at]
            heads = [done[strand, OWN_HEADS * side + near] for near in range(OWN_HEADS)]
            growth = jnp.zeros((LINE, OWN), F32)
            for near in range(OWN_HEADS):
                growth = jnp.where(head_of == near, heads[near][2], growth)
            ssd = dot(
                jnp.concatenate([head[0] for head in heads], 1),
                jnp.concatenate([head[1] for head in heads], 0),
                (1, 0),
            )
            ssd = ssd + growth * carried[:, at]
            gated = (ssd + values * rows[5:6, at]) * done["gate"][own, at]
            out[own, at] = gated * rows[4:5, at]
            squared = squared + gated[:, :LINE] * gated[:, :LINE] + gated[:, LINE:] * gated[:, LINE:]
        squares.append(jnp.sum(jnp.transpose(squared), axis=0, keepdims=True))
    mine = jnp.concatenate(squares, 0)
    for peer in range(GROUP):
        send[peer] = mine


def project_kernel(squares, gated, w_own, w_other, out):
    total = squares[0]
    for peer in range(1, GROUP):
        total = total + squares[peer]
    scale = lax.rsqrt(total / (HEADS * HEAD_DIM) + EPSILON)
    combined = jnp.zeros((LINE, PAIR), F32)
    for strand in range(2):
        down = jnp.transpose(jnp.broadcast_to(scale[strand : strand + 1], (LINE, LINE)))
        block = gated[LINE * strand : LINE * (strand + 1), :]
        normed = block * jnp.concatenate([down] * (PAIR // LINE), 1)
        combined = combined + normed.astype(BF16).astype(F32)
    combined = combined.astype(BF16)
    mixed = dot(combined[:, :OWN], w_own[...], (1, 0)) + dot(combined[:, OWN:], w_other[...], (1, 0))
    out[...] = mixed.astype(BF16).reshape(out.shape)


def sum_kernel(received, out):
    total = received[0].astype(F32)
    for peer in range(1, GROUP):
        total = total + received[peer].astype(F32)
    out[...] = total.astype(BF16)


def call(kernel, outs, kinds, work, limit, scratch=()):
    return pl.pallas_call(
        kernel,
        out_shape=outs,
        in_specs=[pl.BlockSpec(memory_space=kind) for kind in kinds],
        out_specs=jax.tree.map(lambda _: pl.BlockSpec(memory_space=VMEM), outs),
        scratch_shapes=scratch,
        compiler_params=pltpu.CompilerParams(vmem_limit_bytes=limit * 2**20),
        cost_estimate=pl.CostEstimate(flops=work * 10**9, bytes_accessed=work * 2**20, transcendentals=0),
    )


def make_send(*args):
    return call(send_kernel, jax.ShapeDtypeStruct((CHIPS, 16, 128), BF16), [VMEM] * 3, 1, 16)(*args)


def make_tables(*args):
    return call(tables_kernel, jax.ShapeDtypeStruct((32, OWN), F32), [VMEM] * 5, 1, 16)(*args)


def make_prepare(mine, other, conv_bc, complement):
    grams = gram_table()
    return call(
        prepare_kernel,
        (
            jax.ShapeDtypeStruct((64, 2 * PAIR + 1024), BF16),
            jax.ShapeDtypeStruct((16, PAIR), F32),
            jax.ShapeDtypeStruct((16, LINE), F32),
        ),
        [VMEM] * 4 + [SMEM],
        1,
        16,
    )(mine, other, conv_bc, jnp.asarray(grams, BF16), complement)


def make_scan(received, prepared):
    return call(
        scan_kernel,
        (
            jax.ShapeDtypeStruct((2 * LINE, PAIR), F32),
            jax.ShapeDtypeStruct((GROUP, 2, LINE), F32),
        ),
        [VMEM] * 3 + [SMEM],
        7,
        24,
        [
            pltpu.VMEM((LINES, 128), F32),
            pltpu.VMEM((CONV, LINES, 128), F32),
            pltpu.VMEM((CONV, LINES, 128), F32),
            pltpu.VMEM((32 * PAIR_HEADS, 128), F32),
        ],
    )(received, *prepared)


def make_project(squares, gated, *weights):
    shape = (GROUP, PIECE, weights[0].shape[1])
    return call(project_kernel, jax.ShapeDtypeStruct(shape, BF16), [VMEM] * 4, 1, 16)(
        squares, gated, *weights
    )


def make_sum(received):
    return call(sum_kernel, jax.ShapeDtypeStruct(received.shape[1:], BF16), [VMEM], 1, 16)(received)


def device(seq, chan):
    return seq * CHAN + chan


def mixed_groups():
    side = range(SIDE)
    return [
        [
            device(2 * (SIDE * y + high) + core, (y ^ right) * SIDE + (high ^ up))
            for y in side
            for high in side
        ]
        for core in range(2)
        for right in side
        for up in side
    ]


def row_groups():
    return [list(range(GROUP)), list(range(GROUP, CHAN))]


def with_partner(value):
    pairs = [(x * SIDE + z, (SIDE - 1 - x) * SIDE + z) for x in range(SIDE) for z in range(SIDE)]
    return lax.ppermute(value, "chan", pairs)


def with_sibling(value):
    return lax.ppermute(value, "seq", [(source, source ^ 1) for source in range(SEQ)])


def exchange(value, axes, groups=None):
    return lax.all_to_all(value, axes, 0, 0, tiled=True, axis_index_groups=groups)


def per_device(
    tokens, complement, embed, w_x, w_z, w_bc, w_dt, dt_bias, decay_rate, d_skip, conv_x, conv_bc,
    norm_gain, w_out,
):
    own = tokens.reshape(2, 128)
    depth = w_bc.shape[0]
    part = lax.dynamic_slice_in_dim(embed, lax.axis_index("chan") * depth, depth, 1)
    send = make_send(own, with_sibling(own), dot(part, w_bc, (1, 0)))
    send, embed, norm_gain, d_skip, dt_bias, decay_rate = lax.optimization_barrier(
        (send, embed, norm_gain, d_skip, dt_bias, decay_rate)
    )
    received = exchange(send, ("seq", "chan"), mixed_groups())
    by_head = jnp.pad(jnp.stack([dt_bias, decay_rate]), ((0, 0), (0, OWN - OWN_HEADS)))
    by_channel = jnp.stack([norm_gain, jnp.repeat(d_skip, HEAD_DIM)])
    params = jnp.concatenate([conv_x.astype(F32), by_channel, by_head], 0)
    tables = make_tables(embed, w_x, w_z, w_dt.T, params)
    w_other = with_partner(w_out)
    other, w_other = lax.optimization_barrier((with_partner(tables), w_other))
    prepared = make_prepare(tables, other, conv_bc, complement)
    gated, squares = make_scan(received, prepared)
    partial = make_project(exchange(squares, "chan", row_groups()), gated, w_out, w_other)
    return make_sum(exchange(partial, "chan", row_groups()))


def solution(mesh):
    placed = (
        P("seq"),
        P(),
        P(),
        P(None, "chan"),
        P(None, "chan"),
        P("chan", None),
        P(None, "chan"),
        P("chan"),
        P("chan"),
        P("chan"),
        P(None, "chan"),
        P(),
        P("chan"),
        P("chan", None),
    )
    return jax.shard_map(
        per_device, mesh=mesh, in_specs=placed, out_specs=P(("seq", "chan"), None), check_vma=False
    )
```
